512 devices in a mesh: row: 16 (over y, x_lo), col: 16 (over x_hi, z), half: 2 (over core).
Axes of the slice: x: 4 (x_hi: 2, x_lo: 2; x = x_hi * 2 + x_lo), y: 8, z: 8, core: 2. Of those that a mesh axis runs over, the one named last changes fastest.
Arguments:
- frames: float32 [512, 16384], P('half', ('row', 'col')), as said below
Outputs:
- covariance: float32 [16384, 16384], P('row', ('col', 'half'))
Inputs may be any that keep to these rules, and one draw needn't show every extreme that they name: `frames`: positive intensities: a pixel background times a frame brightness times a rough factor.
All inputs are finite; a program needn't handle non-finite values.
Results may differ from the reference program's by a relative error of at most 0.00008.
Values sent between devices are 32-bit elements; how exact they have to be, the bound alone decides.
A program may use at most 64 MiB of HBM per device.

```python
import jax
import jax.numpy as jnp
from jax import lax

FRAMES = 512
PIXELS = 16384


def draw_frames(key, part):
    key = jax.random.fold_in(key, 5)
    first, second, third = jax.random.split(key, 3)
    background = jnp.exp(jax.random.uniform(first, (1, PIXELS), jnp.float32, jnp.log(0.5), jnp.log(4.0)))
    bright = jax.random.uniform(second, (FRAMES, 1), jnp.float32, 0.8, 1.25)
    rough = 1.0 + 0.25 * jnp.clip(jax.random.normal(third, (FRAMES, PIXELS), jnp.float32), -3.0, 3.0)
    return (background * bright * rough).astype(jnp.float32)


def setup_inputs(seed: int = 0) -> dict:
    key_of = jax.random.split(jax.random.key(seed), 2)
    frames = draw_frames(jax.random.fold_in(key_of[1], 71), 0)
    return dict(frames=frames)


def reference(frames):
    pixel_mean = jnp.sum(frames, axis=0) / FRAMES
    centered = frames - pixel_mean[None, :]
    product = lax.dot_general(centered, centered, (((0,), (0,)), ((), ())), precision=lax.Precision.HIGHEST, preferred_element_type=jnp.float32)
    return product / (FRAMES - 1)
```

```python
import jax
import jax.numpy as jnp
from jax import lax
from jax.experimental import pallas as pl
from jax.experimental.pallas import tpu as pltpu
from jax.sharding import PartitionSpec as P

MESH = pl.DeviceIdType.MESH
FRAMES = 512
RING = 8
TILE = 128


def mod8(value):
    return lax.rem(value + 16, RING)


def kernel(stage, out_ref, raw, traw, rows, cols, rhs,
           swap_s, swap_r, t_s, t_r, rx_s, rx_r, cx_s, cx_r,
           rr_s, rr_r, cr_s, cr_r, sib_s, sib_r):
    row = lax.axis_index("row")
    col = lax.axis_index("col")
    half = lax.axis_index("half")
    y, xl = row // 2, lax.rem(row, 2)
    xh, z = col // RING, lax.rem(col, RING)
    other = 1 - half

    sibling = (row, col, other)
    rx_peer = (row, (1 - xh) * RING + z, half)
    cx_peer = (y * 2 + 1 - xl, col, half)
    z_peer = {1: (row, xh * RING + mod8(z + 1), half), -1: (row, xh * RING + mod8(z - 1), half)}
    y_peer = {1: (mod8(y + 1) * 2 + xl, col, half), -1: (mod8(y - 1) * 2 + xl, col, half)}

    t_dest, t_self = [], []
    for s in range(2):
        sign = 1 - 2 * lax.rem(s + xh + 1, 2)
        yy = mod8(y + sign * (z - lax.rem(row, RING)))
        t_dest.append((yy * 2 + s, row, xh))
        t_self.append((yy * 2 + s == row) & (row == col) & (xh == half))

    def part(yy, s):
        sign = 1 - 2 * lax.rem(s + half + 1, 2)
        return mod8(z + sign * (yy - col // 2))

    t_col = RING * half + part(y, xl)
    from_self = (row == col) & (col == t_col)

    barrier = pltpu.get_barrier_semaphore()
    for peer in (sibling, rx_peer, cx_peer, z_peer[1], z_peer[-1], y_peer[1], y_peer[-1], (col, t_col, other)):
        pl.semaphore_signal(barrier, inc=1, device_id=peer, device_id_type=MESH)

    @pl.when(jnp.logical_not(from_self))
    def _():
        pl.semaphore_signal(barrier, inc=1, device_id=(col, t_col, half), device_id_type=MESH)

    raw[half] = stage[pl.ds(pl.multiple_of(half * 32, 32), 32), :]
    pl.semaphore_wait(barrier, jnp.where(from_self, 8, 9))

    def remote(src, dst, send, recv, peer):
        return pltpu.make_async_remote_copy(
            src_ref=src, dst_ref=dst, send_sem=send, recv_sem=recv, device_id=peer, device_id_type=MESH)

    pending = []

    def start(copy):
        copy.start()
        pending.append(copy)

    t_copies = []
    for s in range(2):
        src = stage.at[pl.ds(s * 32, 32)]
        far = remote(src, traw.at[half], t_s.at[s], t_r.at[half], t_dest[s])
        near = pltpu.make_async_copy(src, traw.at[half], t_r.at[half])

        @pl.when(t_self[s])
        def _():
            near.start()

        @pl.when(jnp.logical_not(t_self[s]))
        def _():
            far.start()

        t_copies.append(far)
    swap = remote(stage.at[pl.ds(pl.multiple_of(other * 32, 32), 32)], raw.at[half], swap_s, swap_r, sibling)
    swap.start()

    def center(src, dst):
        total = jnp.sum(src[0], axis=1, keepdims=True) + jnp.sum(src[1], axis=1, keepdims=True)
        mean = total / FRAMES
        dst[:, :256] = src[0] - mean
        dst[:, 256:] = src[1] - mean

    def row_ref(u, d):
        k = (xh if u == 0 else 1 - xh) * RING + mod8(z + d)
        return rows.at[k, half]

    def col_ref(u, d):
        s = xl if u == 0 else 1 - xl
        return cols.at[part(mod8(y + d), s), s]

    def to_sibling(ref, slot):
        start(remote(ref, ref, sib_s.at[slot], sib_r.at[slot], sibling))

    def hop(which, direction, step, u):
        d = -direction * (step - 1)
        i = 0 if direction == 1 else 1
        if which == "row":
            ref, send, recv, peer = row_ref(u, d), rr_s, rr_r, z_peer[direction]
        else:
            ref, send, recv, peer = col_ref(u, d), cr_s, cr_r, y_peer[direction]
        return remote(ref, ref, send.at[i, step - 1, u], recv.at[i, step - 1, u], peer)

    def sends(direction, step, u):
        return step < 4 or (step == 4 and (direction == 1) == (u == 0))

    def slot_of(direction, step, u):
        if step == 4:
            return 14 + u
        return 2 + (step - 1) * 4 + (0 if direction == 1 else 2) + u

    def first(which, u):
        for direction in (1, -1):
            start(hop(which, direction, 1, u))
        if which == "row":
            to_sibling(row_ref(u, 0), u)

    def forward(which, step):
        for u in range(2):
            for direction in (1, -1):
                if not sends(direction, step, u):
                    continue
                d = -direction * step
                ref = row_ref(u, d) if which == "row" else col_ref(u, d)
                recv = rr_r if which == "row" else cr_r
                i = 0 if direction == 1 else 1
                pltpu.make_async_copy(ref, ref, recv.at[i, step - 1, u]).wait()
                if sends(direction, step + 1, u):
                    start(hop(which, direction, step + 1, u))
                if which == "row":
                    to_sibling(ref, slot_of(direction, step, u))

    pltpu.make_async_copy(raw.at[other], raw.at[other], swap_r).wait()
    center(raw, row_ref(0, 0))
    start(remote(row_ref(0, 0), row_ref(0, 0), rx_s, rx_r, rx_peer))
    first("row", 0)

    for g in range(2):
        pltpu.make_async_copy(traw.at[g], traw.at[g], t_r.at[g]).wait()
    center(traw, col_ref(0, 0))
    start(remote(col_ref(0, 0), col_ref(0, 0), cx_s, cx_r, cx_peer))
    first("col", 0)

    pltpu.make_async_copy(row_ref(1, 0), row_ref(1, 0), rx_r).wait()
    first("row", 1)
    forward("row", 1)
    pltpu.make_async_copy(col_ref(1, 0), col_ref(1, 0), cx_r).wait()
    first("col", 1)
    forward("col", 1)
    for step in range(2, 5):
        forward("row", step)
        forward("col", step)

    scale = 1.0 / (FRAMES - 1)

    def split(value):
        hi = value.astype(jnp.bfloat16)
        lo = (value - hi.astype(jnp.float32)).astype(jnp.bfloat16)
        return hi, lo

    for i in range(4):
        hi, lo = split(cols[pl.ds(2 * i, 2)].reshape(TILE, FRAMES) * scale)
        rhs[pl.ds(i * TILE, TILE), :] = jnp.concatenate([hi, hi, lo], axis=1)

    for slot in range(16):
        if slot < 2:
            k = (xh if slot == 0 else 1 - xh) * RING + z
        elif slot < 14:
            step, i, u = (slot - 2) // 4 + 1, ((slot - 2) % 4) // 2, slot % 2
            k = (xh if u == 0 else 1 - xh) * RING + mod8(z - (step if i == 0 else -step))
        else:
            k = (xh if slot == 14 else 1 - xh) * RING + mod8(z + 4)
        ref = rows.at[k, other]
        pltpu.make_async_copy(ref, ref, sib_r.at[slot]).wait()

    @pl.loop(0, 8)
    def _(i):
        hi, lo = split(rows[pl.ds(2 * i, 2)].reshape(TILE, FRAMES))
        lhs = jnp.concatenate([hi, lo, hi], axis=1)
        out_ref[pl.ds(pl.multiple_of(i * TILE, TILE), TILE), :] = lax.dot_general(
            lhs, rhs[...], (((1,), (1,)), ((), ())), preferred_element_type=jnp.float32)

    for copy in pending:
        copy.wait_send()
    swap.wait_send()
    for s in range(2):
        @pl.when(jnp.logical_not(t_self[s]))
        def _():
            t_copies[s].wait_send()


def body(frames):
    dma = pltpu.SemaphoreType.DMA
    return pl.pallas_call(
        kernel,
        out_shape=jax.ShapeDtypeStruct((1024, 512), jnp.float32),
        in_specs=[pl.BlockSpec(memory_space=pltpu.VMEM)],
        out_specs=pl.BlockSpec(memory_space=pltpu.VMEM),
        scratch_shapes=[
            pltpu.VMEM((2, 32, 256), jnp.float32),
            pltpu.VMEM((2, 32, 256), jnp.float32),
            pltpu.VMEM((16, 2, 32, FRAMES), jnp.float32),
            pltpu.VMEM((8, 2, 32, FRAMES), jnp.float32),
            pltpu.VMEM((512, 3 * FRAMES), jnp.bfloat16),
            dma, dma, dma((2,)), dma((2,)), dma, dma, dma, dma,
            dma((2, 4, 2)), dma((2, 4, 2)), dma((2, 4, 2)), dma((2, 4, 2)), dma((16,)), dma((16,)),
        ],
        compiler_params=pltpu.CompilerParams(
            collective_id=0, has_side_effects=True, vmem_limit_bytes=40 * 1024 * 1024),
        cost_estimate=pl.CostEstimate(flops=3 * 2 * 1024 * 512 * 512, bytes_accessed=2 << 20, transcendentals=0),
    )(frames.T)


def solution(mesh):
    in_specs = (P("half", ("row", "col")),)
    out_specs = P("row", ("col", "half"))
    return jax.shard_map(body, mesh=mesh, in_specs=in_specs, out_specs=out_specs, check_vma=False)
```

```python
import jax
import jax.numpy as jnp
from jax import lax
from jax.experimental import pallas as pl
from jax.experimental.pallas import tpu as pltpu
from jax.sharding import PartitionSpec as P

MESH = pl.DeviceIdType.MESH
FRAMES = 512
RING = 8
TILE = 128


def mod8(value):
    return lax.rem(value + 16, RING)


def kernel(stage, out_ref, raw, traw, rows, cols, lhs, rhs,
           swap_s, swap_r, t_s, t_r, rx_s, rx_r, cx_s, cx_r,
           rr_s, rr_r, cr_s, cr_r, sib_s, sib_r):
    row = lax.axis_index("row")
    col = lax.axis_index("col")
    half = lax.axis_index("half")
    y, xl = row // 2, lax.rem(row, 2)
    xh, z = col // RING, lax.rem(col, RING)
    other = 1 - half

    sibling = (row, col, other)
    rx_peer = (row, (1 - xh) * RING + z, half)
    cx_peer = (y * 2 + 1 - xl, col, half)
    z_peer = {1: (row, xh * RING + mod8(z + 1), half), -1: (row, xh * RING + mod8(z - 1), half)}
    y_peer = {1: (mod8(y + 1) * 2 + xl, col, half), -1: (mod8(y - 1) * 2 + xl, col, half)}

    yy = mod8(z + lax.rem(row, RING) + 4 * xh)
    t_dest = [(yy * 2 + s, row, xh) for s in range(2)]
    t_self = [(yy * 2 + s == row) & (row == col) & (xh == half) for s in range(2)]

    def part(yy):
        return mod8(yy - z + 4 * half)

    t_col = RING * half + part(y)
    from_self = (row == col) & (col == t_col)

    barrier = pltpu.get_barrier_semaphore()
    for peer in (sibling, rx_peer, cx_peer, z_peer[1], z_peer[-1], y_peer[1], y_peer[-1], (col, t_col, other)):
        pl.semaphore_signal(barrier, inc=1, device_id=peer, device_id_type=MESH)

    @pl.when(jnp.logical_not(from_self))
    def _():
        pl.semaphore_signal(barrier, inc=1, device_id=(col, t_col, half), device_id_type=MESH)

    raw[half] = stage[pl.ds(pl.multiple_of(half * 32, 32), 32), :]
    pl.semaphore_wait(barrier, jnp.where(from_self, 8, 9))

    def remote(src, dst, send, recv, peer):
        return pltpu.make_async_remote_copy(
            src_ref=src, dst_ref=dst, send_sem=send, recv_sem=recv, device_id=peer, device_id_type=MESH)

    pending = []

    def start(copy):
        copy.start()
        pending.append(copy)

    t_copies = []
    for s in range(2):
        src = stage.at[pl.ds(s * 32, 32)]
        far = remote(src, traw.at[half], t_s.at[s], t_r.at[half], t_dest[s])
        near = pltpu.make_async_copy(src, traw.at[half], t_r.at[half])

        @pl.when(t_self[s])
        def _():
            near.start()

        @pl.when(jnp.logical_not(t_self[s]))
        def _():
            far.start()

        t_copies.append(far)
    swap = remote(stage.at[pl.ds(pl.multiple_of(other * 32, 32), 32)], raw.at[half], swap_s, swap_r, sibling)
    swap.start()

    def center(src, dst):
        total = jnp.sum(src[0], axis=1, keepdims=True) + jnp.sum(src[1], axis=1, keepdims=True)
        mean = total / FRAMES
        dst[:, :256] = src[0] - mean
        dst[:, 256:] = src[1] - mean

    def row_ref(u, d):
        k = (xh if u == 0 else 1 - xh) * RING + mod8(z + d)
        return rows.at[k, half]

    def col_ref(u, d):
        s = xl if u == 0 else 1 - xl
        return cols.at[part(mod8(y + d)), s]

    def to_sibling(ref, slot):
        start(remote(ref, ref, sib_s.at[slot], sib_r.at[slot], sibling))

    def hop(which, direction, step, u):
        d = -direction * (step - 1)
        i = 0 if direction == 1 else 1
        if which == "row":
            ref, send, recv, peer = row_ref(u, d), rr_s, rr_r, z_peer[direction]
        else:
            ref, send, recv, peer = col_ref(u, d), cr_s, cr_r, y_peer[direction]
        return remote(ref, ref, send.at[i, step - 1, u], recv.at[i, step - 1, u], peer)

    def sends(direction, step, u):
        return step < 4 or (step == 4 and (direction == 1) == (u == 0))

    def slot_of(direction, step, u):
        if step == 4:
            return 14 + u
        return 2 + (step - 1) * 4 + (0 if direction == 1 else 2) + u

    def first(which, u):
        for direction in (1, -1):
            start(hop(which, direction, 1, u))
        if which == "row":
            to_sibling(row_ref(u, 0), u)

    def forward(which, step):
        for u in range(2):
            for direction in (1, -1):
                if not sends(direction, step, u):
                    continue
                d = -direction * step
                ref = row_ref(u, d) if which == "row" else col_ref(u, d)
                recv = rr_r if which == "row" else cr_r
                i = 0 if direction == 1 else 1
                pltpu.make_async_copy(ref, ref, recv.at[i, step - 1, u]).wait()
                if sends(direction, step + 1, u):
                    start(hop(which, direction, step + 1, u))
                if which == "row":
                    to_sibling(ref, slot_of(direction, step, u))

    def split(value):
        hi = value.astype(jnp.bfloat16)
        lo = (value - hi.astype(jnp.float32)).astype(jnp.bfloat16)
        return hi, lo

    def k_of(slot):
        if slot < 2:
            u, d = slot, 0
        elif slot < 14:
            step, u = (slot - 2) // 4 + 1, slot % 2
            d = -step if (slot - 2) % 4 < 2 else step
        else:
            u, d = slot - 14, 4
        return (xh if u == 0 else 1 - xh) * RING + mod8(z + d)

    def to_lhs(k, s):
        hi, lo = split(rows[k, s])
        here = pl.ds(pl.multiple_of(k * 64 + s * 32, 32), 32)
        lhs[here, :FRAMES] = hi
        lhs[here, FRAMES:2 * FRAMES] = lo
        lhs[here, 2 * FRAMES:] = hi

    def own_lhs(slots):
        for slot in slots:
            to_lhs(k_of(slot), half)

    def sibling_lhs(slots):
        for slot in slots:
            ref = rows.at[k_of(slot), other]
            pltpu.make_async_copy(ref, ref, sib_r.at[slot]).wait()
            to_lhs(k_of(slot), other)

    base = part(y)
    odd = lax.rem(base, 2)
    sign = 1 - 2 * odd

    def multiply(step):
        t = mod8(base + sign * (1, -2, 3, 4)[step - 1]) // 2
        value = cols[pl.ds(2 * t, 2)].reshape(TILE, FRAMES) * (1.0 / (FRAMES - 1))
        hi, lo = split(value)
        rhs[:, :FRAMES] = hi
        rhs[:, FRAMES:2 * FRAMES] = hi
        rhs[:, 2 * FRAMES:] = lo
        out_ref[:, pl.ds(pl.multiple_of(t * TILE, TILE), TILE)] = lax.dot_general(
            lhs[...], rhs[...], (((1,), (1,)), ((), ())), preferred_element_type=jnp.float32)

    pltpu.make_async_copy(raw.at[other], raw.at[other], swap_r).wait()
    center(raw, row_ref(0, 0))
    start(remote(row_ref(0, 0), row_ref(0, 0), rx_s, rx_r, rx_peer))
    first("row", 0)
    pltpu.make_async_copy(row_ref(1, 0), row_ref(1, 0), rx_r).wait()
    first("row", 1)
    own_lhs((0, 1))
    forward("row", 1)

    for g in range(2):
        pltpu.make_async_copy(traw.at[g], traw.at[g], t_r.at[g]).wait()
    center(traw, col_ref(0, 0))
    start(remote(col_ref(0, 0), col_ref(0, 0), cx_s, cx_r, cx_peer))
    first("col", 0)
    own_lhs(range(2, 6))
    sibling_lhs((0, 1))
    forward("row", 2)
    pltpu.make_async_copy(col_ref(1, 0), col_ref(1, 0), cx_r).wait()
    first("col", 1)
    own_lhs(range(6, 10))
    sibling_lhs(range(2, 6))
    forward("col", 1)
    forward("row", 3)
    own_lhs(range(10, 14))
    sibling_lhs(range(6, 10))
    forward("col", 2)
    forward("row", 4)
    own_lhs((14, 15))
    sibling_lhs(range(10, 16))
    multiply(1)
    forward("col", 3)
    multiply(2)
    multiply(3)
    forward("col", 4)
    multiply(4)

    for copy in pending:
        copy.wait_send()
    swap.wait_send()
    for s in range(2):
        @pl.when(jnp.logical_not(t_self[s]))
        def _():
            t_copies[s].wait_send()


def body(frames):
    dma = pltpu.SemaphoreType.DMA
    return pl.pallas_call(
        kernel,
        out_shape=jax.ShapeDtypeStruct((1024, 512), jnp.float32),
        in_specs=[pl.BlockSpec(memory_space=pltpu.VMEM)],
        out_specs=pl.BlockSpec(memory_space=pltpu.VMEM),
        scratch_shapes=[
            pltpu.VMEM((2, 32, 256), jnp.float32),
            pltpu.VMEM((2, 32, 256), jnp.float32),
            pltpu.VMEM((16, 2, 32, FRAMES), jnp.float32),
            pltpu.VMEM((8, 2, 32, FRAMES), jnp.float32),
            pltpu.VMEM((1024, 3 * FRAMES), jnp.bfloat16),
            pltpu.VMEM((TILE, 3 * FRAMES), jnp.bfloat16),
            dma, dma, dma((2,)), dma((2,)), dma, dma, dma, dma,
            dma((2, 4, 2)), dma((2, 4, 2)), dma((2, 4, 2)), dma((2, 4, 2)), dma((16,)), dma((16,)),
        ],
        compiler_params=pltpu.CompilerParams(
            collective_id=0, has_side_effects=True, vmem_limit_bytes=40 * 1024 * 1024),
        cost_estimate=pl.CostEstimate(flops=3 * 2 * 1024 * 512 * 512, bytes_accessed=2 << 20, transcendentals=0),
    )(frames.T)


def solution(mesh):
    in_specs = (P("half", ("row", "col")),)
    out_specs = P("row", ("col", "half"))
    return jax.shard_map(body, mesh=mesh, in_specs=in_specs, out_specs=out_specs, check_vma=False)
```

```python
import jax
import jax.numpy as jnp
from jax import lax
from jax.experimental import pallas as pl
from jax.experimental.pallas import tpu as pltpu
from jax.sharding import PartitionSpec as P

MESH = pl.DeviceIdType.MESH
FRAMES = 512
RING = 8
TILE = 128


def mod8(value):
    return lax.rem(value + 16, RING)


def kernel(stage, out_ref, passed, raw, traw, rows, cols, lhs, rhs,
           swap_s, swap_r, y_s, y_r, t_s, t_r, rx_s, rx_r, cx_s, cx_r,
           rr_s, rr_r, cr_s, cr_r, sib_s, sib_r):
    row = lax.axis_index("row")
    col = lax.axis_index("col")
    half = lax.axis_index("half")
    y, xl = row // 2, lax.rem(row, 2)
    xh, z = col // RING, lax.rem(col, RING)
    other = 1 - half

    sibling = (row, col, other)
    rx_peer = (row, (1 - xh) * RING + z, half)
    cx_peer = (y * 2 + 1 - xl, col, half)
    z_peer = {1: (row, xh * RING + mod8(z + 1), half), -1: (row, xh * RING + mod8(z - 1), half)}
    y_peer = {1: (mod8(y + 1) * 2 + xl, col, half), -1: (mod8(y - 1) * 2 + xl, col, half)}

    block_zc = lax.rem(row, RING)
    relay_y = mod8(y + z + block_zc + 4 * xh)
    relay = (relay_y * 2 + xl, col, half)
    relay_self = relay_y == y
    from_y = lax.rem(3 * (y + 16 - xl - z - 4 * xh + 8), RING)
    feeder = (from_y * 2 + xl, col, half)
    block = from_y * 2 + xl
    t_dest = [(y * 2 + s, block, xh) for s in range(2)]
    t_self = [(s == xl) & (block == col) & (xh == half) for s in range(2)]

    def part(yy):
        return mod8(yy - col // 2 - z + 4 * half + 8)

    t_row, t_col = y * 2 + lax.rem(col, 2), RING * half + part(y)
    from_self = (row == t_row) & (col == t_col)

    barrier = pltpu.get_barrier_semaphore()
    for peer in (sibling, rx_peer, cx_peer, z_peer[1], z_peer[-1], y_peer[1], y_peer[-1], (t_row, t_col, other)):
        pl.semaphore_signal(barrier, inc=1, device_id=peer, device_id_type=MESH)

    @pl.when(jnp.logical_not(from_self))
    def _():
        pl.semaphore_signal(barrier, inc=1, device_id=(t_row, t_col, half), device_id_type=MESH)

    @pl.when(jnp.logical_not(relay_self))
    def _():
        pl.semaphore_signal(barrier, inc=1, device_id=feeder, device_id_type=MESH)

    raw[half] = stage[pl.ds(pl.multiple_of(half * 32, 32), 32), :]
    pl.semaphore_wait(barrier, 10 - from_self.astype(jnp.int32) - relay_self.astype(jnp.int32))

    def remote(src, dst, send, recv, peer):
        return pltpu.make_async_remote_copy(
            src_ref=src, dst_ref=dst, send_sem=send, recv_sem=recv, device_id=peer, device_id_type=MESH)

    pending = []

    def start(copy):
        copy.start()
        pending.append(copy)

    swap = remote(stage.at[pl.ds(pl.multiple_of(other * 32, 32), 32)], raw.at[half], swap_s, swap_r, sibling)
    swap.start()
    far_relay = remote(stage, passed, y_s, y_r, relay)

    @pl.when(relay_self)
    def _():
        pltpu.make_async_copy(stage, passed, y_r).start()

    @pl.when(jnp.logical_not(relay_self))
    def _():
        far_relay.start()

    t_copies = []

    def pass_on():
        pltpu.make_async_copy(passed, passed, y_r).wait()
        for s in range(2):
            src = passed.at[pl.ds(s * 32, 32)]
            far = remote(src, traw.at[half], t_s.at[s], t_r.at[half], t_dest[s])
            near = pltpu.make_async_copy(src, traw.at[half], t_r.at[half])

            @pl.when(t_self[s])
            def _():
                near.start()

            @pl.when(jnp.logical_not(t_self[s]))
            def _():
                far.start()

            t_copies.append(far)

    def center(src, dst):
        total = jnp.sum(src[0], axis=1, keepdims=True) + jnp.sum(src[1], axis=1, keepdims=True)
        mean = total / FRAMES
        dst[:, :256] = src[0] - mean
        dst[:, 256:] = src[1] - mean

    def row_ref(u, d):
        k = (xh if u == 0 else 1 - xh) * RING + mod8(z + d)
        return rows.at[k, half]

    def col_ref(u, d):
        s = xl if u == 0 else 1 - xl
        return cols.at[part(mod8(y + d)), s]

    def to_sibling(ref, slot):
        start(remote(ref, ref, sib_s.at[slot], sib_r.at[slot], sibling))

    def hop(which, direction, step, u):
        d = -direction * (step - 1)
        i = 0 if direction == 1 else 1
        if which == "row":
            ref, send, recv, peer = row_ref(u, d), rr_s, rr_r, z_peer[direction]
        else:
            ref, send, recv, peer = col_ref(u, d), cr_s, cr_r, y_peer[direction]
        return remote(ref, ref, send.at[i, step - 1, u], recv.at[i, step - 1, u], peer)

    def sends(direction, step, u):
        return step < 4 or (step == 4 and (direction == 1) == (u == 0))

    def slot_of(direction, step, u):
        if step == 4:
            return 14 + u
        return 2 + (step - 1) * 4 + (0 if direction == 1 else 2) + u

    def first(which, u):
        for direction in (1, -1):
            start(hop(which, direction, 1, u))
        if which == "row":
            to_sibling(row_ref(u, 0), u)

    def forward(which, step):
        for u in range(2):
            for direction in (1, -1):
                if not sends(direction, step, u):
                    continue
                d = -direction * step
                ref = row_ref(u, d) if which == "row" else col_ref(u, d)
                recv = rr_r if which == "row" else cr_r
                i = 0 if direction == 1 else 1
                pltpu.make_async_copy(ref, ref, recv.at[i, step - 1, u]).wait()
                if sends(direction, step + 1, u):
                    start(hop(which, direction, step + 1, u))
                if which == "row":
                    to_sibling(ref, slot_of(direction, step, u))

    def split(value):
        hi = value.astype(jnp.bfloat16)
        lo = (value - hi.astype(jnp.float32)).astype(jnp.bfloat16)
        return hi, lo

    def k_of(slot):
        if slot < 2:
            u, d = slot, 0
        elif slot < 14:
            step, u = (slot - 2) // 4 + 1, slot % 2
            d = -step if (slot - 2) % 4 < 2 else step
        else:
            u, d = slot - 14, 4
        return (xh if u == 0 else 1 - xh) * RING + mod8(z + d)

    def to_lhs(k, s):
        hi, lo = split(rows[k, s])
        here = pl.ds(pl.multiple_of(k * 64 + s * 32, 32), 32)
        lhs[here, :FRAMES] = hi
        lhs[here, FRAMES:2 * FRAMES] = lo
        lhs[here, 2 * FRAMES:] = hi

    def own_lhs(slots):
        for slot in slots:
            to_lhs(k_of(slot), half)

    def sibling_lhs(slots):
        for slot in slots:
            ref = rows.at[k_of(slot), other]
            pltpu.make_async_copy(ref, ref, sib_r.at[slot]).wait()
            to_lhs(k_of(slot), other)

    base = part(y)
    odd = lax.rem(base, 2)
    sign = 1 - 2 * odd

    def multiply(step):
        t = mod8(base + sign * (1, -2, 3, 4)[step - 1]) // 2
        value = cols[pl.ds(2 * t, 2)].reshape(TILE, FRAMES) * (1.0 / (FRAMES - 1))
        hi, lo = split(value)
        rhs[:, :FRAMES] = hi
        rhs[:, FRAMES:2 * FRAMES] = hi
        rhs[:, 2 * FRAMES:] = lo
        out_ref[:, pl.ds(pl.multiple_of(t * TILE, TILE), TILE)] = lax.dot_general(
            lhs[...], rhs[...], (((1,), (1,)), ((), ())), preferred_element_type=jnp.float32)

    pltpu.make_async_copy(raw.at[other], raw.at[other], swap_r).wait()
    center(raw, row_ref(0, 0))
    start(remote(row_ref(0, 0), row_ref(0, 0), rx_s, rx_r, rx_peer))
    first("row", 0)
    pass_on()
    pltpu.make_async_copy(row_ref(1, 0), row_ref(1, 0), rx_r).wait()
    first("row", 1)
    own_lhs((0, 1))
    forward("row", 1)

    for g in range(2):
        pltpu.make_async_copy(traw.at[g], traw.at[g], t_r.at[g]).wait()
    center(traw, col_ref(0, 0))
    start(remote(col_ref(0, 0), col_ref(0, 0), cx_s, cx_r, cx_peer))
    first("col", 0)
    own_lhs(range(2, 6))
    sibling_lhs((0, 1))
    forward("row", 2)
    pltpu.make_async_copy(col_ref(1, 0), col_ref(1, 0), cx_r).wait()
    first("col", 1)
    own_lhs(range(6, 10))
    sibling_lhs(range(2, 6))
    forward("col", 1)
    forward("row", 3)
    own_lhs(range(10, 14))
    sibling_lhs(range(6, 10))
    forward("col", 2)
    forward("row", 4)
    own_lhs((14, 15))
    sibling_lhs(range(10, 16))
    multiply(1)
    forward("col", 3)
    multiply(2)
    multiply(3)
    forward("col", 4)
    multiply(4)

    for copy in pending:
        copy.wait_send()
    swap.wait_send()

    @pl.when(jnp.logical_not(relay_self))
    def _():
        far_relay.wait_send()

    for s in range(2):
        @pl.when(jnp.logical_not(t_self[s]))
        def _():
            t_copies[s].wait_send()


def body(frames):
    dma = pltpu.SemaphoreType.DMA
    return pl.pallas_call(
        kernel,
        out_shape=jax.ShapeDtypeStruct((1024, 512), jnp.float32),
        in_specs=[pl.BlockSpec(memory_space=pltpu.VMEM)],
        out_specs=pl.BlockSpec(memory_space=pltpu.VMEM),
        scratch_shapes=[
            pltpu.VMEM((64, 256), jnp.float32),
            pltpu.VMEM((2, 32, 256), jnp.float32),
            pltpu.VMEM((2, 32, 256), jnp.float32),
            pltpu.VMEM((16, 2, 32, FRAMES), jnp.float32),
            pltpu.VMEM((8, 2, 32, FRAMES), jnp.float32),
            pltpu.VMEM((1024, 3 * FRAMES), jnp.bfloat16),
            pltpu.VMEM((TILE, 3 * FRAMES), jnp.bfloat16),
            dma, dma, dma, dma, dma((2,)), dma((2,)), dma, dma, dma, dma,
            dma((2, 4, 2)), dma((2, 4, 2)), dma((2, 4, 2)), dma((2, 4, 2)), dma((16,)), dma((16,)),
        ],
        compiler_params=pltpu.CompilerParams(
            collective_id=0, has_side_effects=True, vmem_limit_bytes=40 * 1024 * 1024),
        cost_estimate=pl.CostEstimate(flops=3 * 2 * 1024 * 512 * 512, bytes_accessed=2 << 20, transcendentals=0),
    )(frames.T)


def solution(mesh):
    in_specs = (P("half", ("row", "col")),)
    out_specs = P("row", ("col", "half"))
    return jax.shard_map(body, mesh=mesh, in_specs=in_specs, out_specs=out_specs, check_vma=False)
```

```python
import jax
import jax.numpy as jnp
from jax import lax
from jax.experimental import pallas as pl
from jax.experimental.pallas import tpu as pltpu
from jax.sharding import PartitionSpec as P

MESH = pl.DeviceIdType.MESH
FRAMES = 512
RING = 8
TILE = 128


def mod8(value):
    return lax.rem(value + 16, RING)


def kernel(stage, out_ref, raw, traw, rows, cols, lhs, rhs,
           swap_s, swap_r, t_s, t_r, rx_s, rx_r, cx_s, cx_r,
           rr_s, rr_r, cr_s, cr_r, sib_s, sib_r):
    row = lax.axis_index("row")
    col = lax.axis_index("col")
    half = lax.axis_index("half")
    y, xl = row // 2, lax.rem(row, 2)
    xh, z = col // RING, lax.rem(col, RING)
    other = 1 - half

    sibling = (row, col, other)
    rx_peer = (row, (1 - xh) * RING + z, half)
    cx_peer = (y * 2 + 1 - xl, col, half)
    z_peer = {1: (row, xh * RING + mod8(z + 1), half), -1: (row, xh * RING + mod8(z - 1), half)}
    y_peer = {1: (mod8(y + 1) * 2 + xl, col, half), -1: (mod8(y - 1) * 2 + xl, col, half)}

    yy = mod8(z + lax.rem(row, RING) + 4 * xh)
    t_dest = [(yy * 2 + s, row, xh) for s in range(2)]
    t_self = [(yy * 2 + s == row) & (row == col) & (xh == half) for s in range(2)]

    def part(yy):
        return mod8(yy - z + 4 * half)

    t_col = RING * half + part(y)
    from_self = (row == col) & (col == t_col)

    barrier = pltpu.get_barrier_semaphore()
    for peer in (sibling, rx_peer, cx_peer, z_peer[1], z_peer[-1], y_peer[1], y_peer[-1], (col, t_col, other)):
        pl.semaphore_signal(barrier, inc=1, device_id=peer, device_id_type=MESH)

    @pl.when(jnp.logical_not(from_self))
    def _():
        pl.semaphore_signal(barrier, inc=1, device_id=(col, t_col, half), device_id_type=MESH)

    raw[half] = stage[pl.ds(pl.multiple_of(half * 32, 32), 32), :]
    pl.semaphore_wait(barrier, jnp.where(from_self, 8, 9))

    def remote(src, dst, send, recv, peer):
        return pltpu.make_async_remote_copy(
            src_ref=src, dst_ref=dst, send_sem=send, recv_sem=recv, device_id=peer, device_id_type=MESH)

    pending = []

    def start(copy):
        copy.start()
        pending.append(copy)

    t_copies = []
    for s in range(2):
        src = stage.at[pl.ds(s * 32, 32)]
        far = remote(src, traw.at[half], t_s.at[s], t_r.at[half], t_dest[s])
        near = pltpu.make_async_copy(src, traw.at[half], t_r.at[half])

        @pl.when(t_self[s])
        def _():
            near.start()

        @pl.when(jnp.logical_not(t_self[s]))
        def _():
            far.start()

        t_copies.append(far)
    swap = remote(stage.at[pl.ds(pl.multiple_of(other * 32, 32), 32)], raw.at[half], swap_s, swap_r, sibling)
    swap.start()

    def center(src, dst):
        total = jnp.sum(src[0], axis=1, keepdims=True) + jnp.sum(src[1], axis=1, keepdims=True)
        mean = total / FRAMES
        dst[:, :256] = src[0] - mean
        dst[:, 256:] = src[1] - mean

    def row_ref(u, d):
        k = (xh if u == 0 else 1 - xh) * RING + mod8(z + d)
        return rows.at[k, half]

    def col_ref(u, d):
        s = xl if u == 0 else 1 - xl
        return cols.at[part(mod8(y + d)), s]

    def to_sibling(ref, slot):
        start(remote(ref, ref, sib_s.at[slot], sib_r.at[slot], sibling))

    def hop(which, direction, step, u):
        d = -direction * (step - 1)
        i = 0 if direction == 1 else 1
        if which == "row":
            ref, send, recv, peer = row_ref(u, d), rr_s, rr_r, z_peer[direction]
        else:
            ref, send, recv, peer = col_ref(u, d), cr_s, cr_r, y_peer[direction]
        return remote(ref, ref, send.at[i, step - 1, u], recv.at[i, step - 1, u], peer)

    def sends(direction, step, u):
        return step < 4 or (step == 4 and (direction == 1) == (u == 0))

    def slot_of(direction, step, u):
        if step == 4:
            return 14 + u
        return 2 + (step - 1) * 4 + (0 if direction == 1 else 2) + u

    def first(which, u):
        for direction in (1, -1):
            start(hop(which, direction, 1, u))
        if which == "row":
            to_sibling(row_ref(u, 0), u)

    def forward(which, step, u):
        for direction in (1, -1):
            if not sends(direction, step, u):
                continue
            d = -direction * step
            ref = row_ref(u, d) if which == "row" else col_ref(u, d)
            recv = rr_r if which == "row" else cr_r
            i = 0 if direction == 1 else 1
            pltpu.make_async_copy(ref, ref, recv.at[i, step - 1, u]).wait()
            if sends(direction, step + 1, u):
                start(hop(which, direction, step + 1, u))
            if which == "row":
                to_sibling(ref, slot_of(direction, step, u))

    def split(value):
        hi = value.astype(jnp.bfloat16)
        lo = (value - hi.astype(jnp.float32)).astype(jnp.bfloat16)
        return hi, lo

    def k_of(slot):
        if slot < 2:
            u, d = slot, 0
        elif slot < 14:
            step, u = (slot - 2) // 4 + 1, slot % 2
            d = -step if (slot - 2) % 4 < 2 else step
        else:
            u, d = slot - 14, 4
        return (xh if u == 0 else 1 - xh) * RING + mod8(z + d)

    def to_lhs(k, s):
        hi, lo = split(rows[k, s])
        here = pl.ds(pl.multiple_of(k * 64 + s * 32, 32), 32)
        lhs[here, :FRAMES] = hi
        lhs[here, FRAMES:2 * FRAMES] = lo
        lhs[here, 2 * FRAMES:] = hi

    def own_lhs(slots):
        for slot in slots:
            to_lhs(k_of(slot), half)

    def sibling_lhs(slots):
        for slot in slots:
            ref = rows.at[k_of(slot), other]
            pltpu.make_async_copy(ref, ref, sib_r.at[slot]).wait()
            to_lhs(k_of(slot), other)

    base = part(y)
    odd = lax.rem(base, 2)
    sign = 1 - 2 * odd

    def tile_of(step):
        return mod8(base + sign * (1, -2, 3, 4)[step - 1]) // 2

    def to_rhs(steps):
        for i, step in enumerate(steps):
            value = cols[pl.ds(2 * tile_of(step), 2)].reshape(TILE, FRAMES) * (1.0 / (FRAMES - 1))
            hi, lo = split(value)
            here = pl.ds(i * TILE, TILE)
            rhs[here, :FRAMES] = hi
            rhs[here, FRAMES:2 * FRAMES] = hi
            rhs[here, 2 * FRAMES:] = lo

    def multiply(steps, u):
        here = pl.ds(pl.multiple_of((xh if u == 0 else 1 - xh) * 512, 512), 512)
        product = lax.dot_general(
            lhs[here, :], rhs[...], (((1,), (1,)), ((), ())), preferred_element_type=jnp.float32)
        for i, step in enumerate(steps):
            there = pl.ds(pl.multiple_of(tile_of(step) * TILE, TILE), TILE)
            out_ref[here, there] = product[:, i * TILE:(i + 1) * TILE]

    def slots(step, u):
        if step == 0:
            return (u,)
        if step == 4:
            return (14 + u,)
        return (slot_of(1, step, u), slot_of(-1, step, u))

    def begin(which, u):
        if which == "row" and u == 0:
            pltpu.make_async_copy(raw.at[other], raw.at[other], swap_r).wait()
            center(raw, row_ref(0, 0))
            first("row", 0)
            start(remote(row_ref(0, 0), row_ref(0, 0), rx_s, rx_r, rx_peer))
        elif which == "row":
            pltpu.make_async_copy(row_ref(1, 0), row_ref(1, 0), rx_r).wait()
            first("row", 1)
        elif u == 0:
            for g in range(2):
                pltpu.make_async_copy(traw.at[g], traw.at[g], t_r.at[g]).wait()
            center(traw, col_ref(0, 0))
            first("col", 0)
            start(remote(col_ref(0, 0), col_ref(0, 0), cx_s, cx_r, cx_peer))
        else:
            pltpu.make_async_copy(col_ref(1, 0), col_ref(1, 0), cx_r).wait()
            first("col", 1)

    order = (
        ("row", 0, 0), ("col", 0, 0), ("row", 1, 0), ("row", 0, 1), ("col", 0, 1), ("row", 2, 0), ("col", 1, 0),
        ("row", 1, 1), ("col", 1, 1), ("col", 2, 0), ("row", 2, 1), ("col", 2, 1), ("row", 3, 0), ("col", 3, 0),
        ("row", 3, 1), ("col", 3, 1), ("row", 4, 0), ("col", 4, 0))
    near, far = (1, 2), (3, 4)
    waiting = []
    for which, step, u in order:
        if step == 0:
            begin(which, u)
        else:
            forward(which, step, u)
        if which == "row":
            own_lhs(slots(step, u))
            waiting.append((step, u))
            if len(waiting) > 2:
                sibling_lhs(slots(*waiting.pop(0)))
    to_rhs(near)
    for step, u in waiting:
        if u == 0:
            sibling_lhs(slots(step, u))
    multiply(near, 0)
    forward("row", 4, 1)
    own_lhs(slots(4, 1))
    for step, u in waiting:
        if u == 1:
            sibling_lhs(slots(step, u))
    sibling_lhs(slots(4, 1))
    multiply(near, 1)
    forward("col", 4, 1)
    to_rhs(far)
    multiply(far, 0)
    multiply(far, 1)

    for copy in pending:
        copy.wait_send()
    swap.wait_send()
    for s in range(2):
        @pl.when(jnp.logical_not(t_self[s]))
        def _():
            t_copies[s].wait_send()


def body(frames):
    dma = pltpu.SemaphoreType.DMA
    return pl.pallas_call(
        kernel,
        out_shape=jax.ShapeDtypeStruct((1024, 512), jnp.float32),
        in_specs=[pl.BlockSpec(memory_space=pltpu.VMEM)],
        out_specs=pl.BlockSpec(memory_space=pltpu.VMEM),
        scratch_shapes=[
            pltpu.VMEM((2, 32, 256), jnp.float32),
            pltpu.VMEM((2, 32, 256), jnp.float32),
            pltpu.VMEM((16, 2, 32, FRAMES), jnp.float32),
            pltpu.VMEM((8, 2, 32, FRAMES), jnp.float32),
            pltpu.VMEM((1024, 3 * FRAMES), jnp.bfloat16),
            pltpu.VMEM((2 * TILE, 3 * FRAMES), jnp.bfloat16),
            dma, dma, dma((2,)), dma((2,)), dma, dma, dma, dma,
            dma((2, 4, 2)), dma((2, 4, 2)), dma((2, 4, 2)), dma((2, 4, 2)), dma((16,)), dma((16,)),
        ],
        compiler_params=pltpu.CompilerParams(
            collective_id=0, has_side_effects=True, vmem_limit_bytes=40 * 1024 * 1024),
        cost_estimate=pl.CostEstimate(flops=3 * 2 * 1024 * 512 * 512, bytes_accessed=2 << 20, transcendentals=0),
    )(frames.T)


def solution(mesh):
    in_specs = (P("half", ("row", "col")),)
    out_specs = P("row", ("col", "half"))
    return jax.shard_map(body, mesh=mesh, in_specs=in_specs, out_specs=out_specs, check_vma=False)
```

```python
import jax
import jax.numpy as jnp
from jax import lax
from jax.experimental import pallas as pl
from jax.experimental.pallas import tpu as pltpu
from jax.sharding import PartitionSpec as P

MESH = pl.DeviceIdType.MESH
FRAMES = 512
RING = 8
TILE = 128


def mod8(value):
    return lax.rem(value + 16, RING)


def kernel(x_ref, out_ref, stage, raw, traw, rows, cols, lhs, rhs,
           in_s, swap_s, swap_r, t_s, t_r, rx_s, rx_r, cx_s, cx_r,
           rr_s, rr_r, cr_s, cr_r, sib_s, sib_r):
    row = lax.axis_index("row")
    col = lax.axis_index("col")
    half = lax.axis_index("half")
    y, xl = row // 2, lax.rem(row, 2)
    xh, z = col // RING, lax.rem(col, RING)
    other = 1 - half

    fetch = pltpu.make_async_copy(x_ref, stage, in_s)
    fetch.start()

    sibling = (row, col, other)
    rx_peer = (row, (1 - xh) * RING + z, half)
    cx_peer = (y * 2 + 1 - xl, col, half)
    jumps = (1, -1, 2, -2)
    z_peer = {n: (row, xh * RING + mod8(z + n), half) for n in jumps}
    y_peer = {n: (mod8(y + n) * 2 + xl, col, half) for n in jumps}

    yy = mod8(z + lax.rem(row, RING) + 4 * xh)
    t_dest = [(yy * 2 + s, row, xh) for s in range(2)]
    t_self = [(yy * 2 + s == row) & (row == col) & (xh == half) for s in range(2)]

    def part(yy):
        return mod8(yy - z + 4 * half)

    t_col = RING * half + part(y)
    from_self = (row == col) & (col == t_col)

    barrier = pltpu.get_barrier_semaphore()
    for peer in (sibling, rx_peer, cx_peer, *z_peer.values(), *y_peer.values(), (col, t_col, other)):
        pl.semaphore_signal(barrier, inc=1, device_id=peer, device_id_type=MESH)

    @pl.when(jnp.logical_not(from_self))
    def _():
        pl.semaphore_signal(barrier, inc=1, device_id=(col, t_col, half), device_id_type=MESH)

    fetch.wait()
    raw[half] = stage[pl.ds(pl.multiple_of(half * 32, 32), 32), :]
    pl.semaphore_wait(barrier, jnp.where(from_self, 12, 13))

    def remote(src, dst, send, recv, peer):
        return pltpu.make_async_remote_copy(
            src_ref=src, dst_ref=dst, send_sem=send, recv_sem=recv, device_id=peer, device_id_type=MESH)

    pending = []

    def start(copy):
        copy.start()
        pending.append(copy)

    t_copies = []
    for s in range(2):
        src = stage.at[pl.ds(s * 32, 32)]
        far = remote(src, traw.at[half], t_s.at[s], t_r.at[half], t_dest[s])
        near = pltpu.make_async_copy(src, traw.at[half], t_r.at[half])

        @pl.when(t_self[s])
        def _():
            near.start()

        @pl.when(jnp.logical_not(t_self[s]))
        def _():
            far.start()

        t_copies.append(far)
    swap = remote(stage.at[pl.ds(pl.multiple_of(other * 32, 32), 32)], raw.at[half], swap_s, swap_r, sibling)
    swap.start()

    def center(src, dst):
        total = jnp.sum(src[0], axis=1, keepdims=True) + jnp.sum(src[1], axis=1, keepdims=True)
        mean = total / FRAMES
        dst[:, :256] = src[0] - mean
        dst[:, 256:] = src[1] - mean

    def row_ref(u, d):
        k = (xh if u == 0 else 1 - xh) * RING + mod8(z + d)
        return rows.at[k, half]

    def col_ref(u, d):
        s = xl if u == 0 else 1 - xl
        return cols.at[part(mod8(y + d)), s]

    def to_sibling(ref, slot):
        start(remote(ref, ref, sib_s.at[slot], sib_r.at[slot], sibling))

    def hop(which, direction, step, u):
        behind, ahead = ((0, 1), (0, 2), (2, 1), (2, 2))[step - 1]
        i = 0 if direction == 1 else 1
        if which == "row":
            ref, send, recv, peer = row_ref(u, -direction * behind), rr_s, rr_r, z_peer[direction * ahead]
        else:
            ref, send, recv, peer = col_ref(u, -direction * behind), cr_s, cr_r, y_peer[direction * ahead]
        return remote(ref, ref, send.at[i, step - 1, u], recv.at[i, step - 1, u], peer)

    def sends(direction, step, u):
        return step < 4 or (step == 4 and (direction == 1) == (u == 0))

    def slot_of(direction, step, u):
        if step == 4:
            return 14 + u
        return 2 + (step - 1) * 4 + (0 if direction == 1 else 2) + u

    def first(which, u):
        for step in (2, 1):
            for direction in (1, -1):
                start(hop(which, direction, step, u))
        if which == "row":
            to_sibling(row_ref(u, 0), u)

    def forward(which, step, u):
        for direction in (1, -1):
            if not sends(direction, step, u):
                continue
            d = -direction * step
            ref = row_ref(u, d) if which == "row" else col_ref(u, d)
            recv = rr_r if which == "row" else cr_r
            i = 0 if direction == 1 else 1
            pltpu.make_async_copy(ref, ref, recv.at[i, step - 1, u]).wait()
            for later in (4, 3) if step == 2 else ():
                if sends(direction, later, u):
                    start(hop(which, direction, later, u))
            if which == "row":
                to_sibling(ref, slot_of(direction, step, u))

    def split(value):
        hi = value.astype(jnp.bfloat16)
        lo = (value - hi.astype(jnp.float32)).astype(jnp.bfloat16)
        return hi, lo

    def k_of(slot):
        if slot < 2:
            u, d = slot, 0
        elif slot < 14:
            step, u = (slot - 2) // 4 + 1, slot % 2
            d = -step if (slot - 2) % 4 < 2 else step
        else:
            u, d = slot - 14, 4
        return (xh if u == 0 else 1 - xh) * RING + mod8(z + d)

    def to_lhs(k, s):
        hi, lo = split(rows[k, s])
        here = pl.ds(pl.multiple_of(k * 64 + s * 32, 32), 32)
        lhs[here, :FRAMES] = hi
        lhs[here, FRAMES:2 * FRAMES] = lo
        lhs[here, 2 * FRAMES:] = hi

    def own_lhs(slots):
        for slot in slots:
            to_lhs(k_of(slot), half)

    def sibling_lhs(slots):
        for slot in slots:
            ref = rows.at[k_of(slot), other]
            pltpu.make_async_copy(ref, ref, sib_r.at[slot]).wait()
            to_lhs(k_of(slot), other)

    base = part(y)
    odd = lax.rem(base, 2)
    sign = 1 - 2 * odd

    def tile_of(step):
        return mod8(base + sign * (1, -2, 3, 4)[step - 1]) // 2

    def to_rhs(steps):
        for i, step in enumerate(steps):
            value = cols[pl.ds(2 * tile_of(step), 2)].reshape(TILE, FRAMES) * (1.0 / (FRAMES - 1))
            hi, lo = split(value)
            here = pl.ds(i * TILE, TILE)
            rhs[here, :FRAMES] = hi
            rhs[here, FRAMES:2 * FRAMES] = hi
            rhs[here, 2 * FRAMES:] = lo

    def multiply(steps, u):
        here = pl.ds(pl.multiple_of((xh if u == 0 else 1 - xh) * 512, 512), 512)
        product = lax.dot_general(
            lhs[here, :], rhs[...], (((1,), (1,)), ((), ())), preferred_element_type=jnp.float32)
        for i, step in enumerate(steps):
            there = pl.ds(pl.multiple_of(tile_of(step) * TILE, TILE), TILE)
            out_ref[here, there] = product[:, i * TILE:(i + 1) * TILE]

    def slots(step, u):
        if step == 0:
            return (u,)
        if step == 4:
            return (14 + u,)
        return (slot_of(1, step, u), slot_of(-1, step, u))

    def begin(which, u):
        if which == "row" and u == 0:
            pltpu.make_async_copy(raw.at[other], raw.at[other], swap_r).wait()
            center(raw, row_ref(0, 0))
            first("row", 0)
            start(remote(row_ref(0, 0), row_ref(0, 0), rx_s, rx_r, rx_peer))
        elif which == "row":
            pltpu.make_async_copy(row_ref(1, 0), row_ref(1, 0), rx_r).wait()
            first("row", 1)
        elif u == 0:
            for g in range(2):
                pltpu.make_async_copy(traw.at[g], traw.at[g], t_r.at[g]).wait()
            center(traw, col_ref(0, 0))
            first("col", 0)
            start(remote(col_ref(0, 0), col_ref(0, 0), cx_s, cx_r, cx_peer))
        else:
            pltpu.make_async_copy(col_ref(1, 0), col_ref(1, 0), cx_r).wait()
            first("col", 1)

    order = (
        ("row", 0, 0), ("col", 0, 0), ("row", 0, 1), ("col", 0, 1), ("row", 2, 0), ("col", 2, 0), ("row", 1, 0),
        ("row", 2, 1), ("col", 1, 0), ("col", 2, 1), ("row", 1, 1), ("col", 1, 1), ("row", 3, 0), ("row", 4, 0))
    near, far = (1, 2), (3, 4)
    waiting = []
    for which, step, u in order:
        if step == 0:
            begin(which, u)
        else:
            forward(which, step, u)
        if which == "row":
            own_lhs(slots(step, u))
            waiting.append((step, u))
            if len(waiting) > 2:
                sibling_lhs(slots(*waiting.pop(0)))
    to_rhs(near)
    for step, u in waiting:
        sibling_lhs(slots(step, u))
    multiply(near, 0)
    for step in (3, 4):
        forward("row", step, 1)
        own_lhs(slots(step, 1))
    for step in (3, 4):
        sibling_lhs(slots(step, 1))
    multiply(near, 1)
    for u in range(2):
        for step in (3, 4):
            forward("col", step, u)
    to_rhs(far)
    multiply(far, 0)
    multiply(far, 1)

    for copy in pending:
        copy.wait_send()
    swap.wait_send()
    for s in range(2):
        @pl.when(jnp.logical_not(t_self[s]))
        def _():
            t_copies[s].wait_send()


def body(frames):
    dma = pltpu.SemaphoreType.DMA
    return pl.pallas_call(
        kernel,
        out_shape=jax.ShapeDtypeStruct((1024, 512), jnp.float32),
        in_specs=[pl.BlockSpec(memory_space=pltpu.HBM)],
        out_specs=pl.BlockSpec(memory_space=pltpu.VMEM),
        scratch_shapes=[
            pltpu.VMEM((64, 256), jnp.float32),
            pltpu.VMEM((2, 32, 256), jnp.float32),
            pltpu.VMEM((2, 32, 256), jnp.float32),
            pltpu.VMEM((16, 2, 32, FRAMES), jnp.float32),
            pltpu.VMEM((8, 2, 32, FRAMES), jnp.float32),
            pltpu.VMEM((1024, 3 * FRAMES), jnp.bfloat16),
            pltpu.VMEM((2 * TILE, 3 * FRAMES), jnp.bfloat16),
            dma, dma, dma, dma((2,)), dma((2,)), dma, dma, dma, dma,
            dma((2, 4, 2)), dma((2, 4, 2)), dma((2, 4, 2)), dma((2, 4, 2)), dma((16,)), dma((16,)),
        ],
        compiler_params=pltpu.CompilerParams(
            collective_id=0, has_side_effects=True, vmem_limit_bytes=40 * 1024 * 1024),
        cost_estimate=pl.CostEstimate(flops=3 * 2 * 1024 * 512 * 512, bytes_accessed=2 << 20, transcendentals=0),
    )(frames.T)


def solution(mesh):
    in_specs = (P("half", ("row", "col")),)
    out_specs = P("row", ("col", "half"))
    return jax.shard_map(body, mesh=mesh, in_specs=in_specs, out_specs=out_specs, check_vma=False)
```

```python
import jax
import jax.numpy as jnp
from jax import lax
from jax.experimental import pallas as pl
from jax.experimental.pallas import tpu as pltpu
from jax.sharding import PartitionSpec as P

MESH = pl.DeviceIdType.MESH
FRAMES = 512
HALF = FRAMES // 2
RING = 8
TILE = 128


def mod8(value):
    return lax.rem(value + 16, RING)


def split(value):
    hi = value.astype(jnp.bfloat16)
    lo = (value - hi.astype(jnp.float32)).astype(jnp.bfloat16)
    return hi, lo


def kernel(stage, out_ref, traw, rows, cols, lhs, rhs,
           t_s, t_r, rx_s, rx_r, rr_s, rr_r, c_s, c_r, sib_s, sib_r):
    row = lax.axis_index("row")
    col = lax.axis_index("col")
    half = lax.axis_index("half")
    y, xl = row // 2, lax.rem(row, 2)
    xh, z = col // RING, lax.rem(col, RING)
    other = 1 - half

    sibling = (row, col, other)
    rx_peer = (row, (1 - xh) * RING + z, half)
    z_peer = {n: (row, xh * RING + mod8(z + n), half) for n in (1, -1, 2, -2)}
    near_places = ((2, 0), (-2, 0), (0, 1), (1, 0), (-1, 0), (1, 1), (-1, 1))
    y_peer = [(mod8(y + n) * 2 + (xl if across == 0 else 1 - xl), col, half) for n, across in near_places]

    yy = mod8(z + lax.rem(row, RING) + 4 * xh)
    t_dest, t_self = [], []
    for s in range(2):
        for p in range(2):
            there = mod8(yy + 4 * p) * 2 + (s if p == 0 else 1 - s)
            t_dest.append((there, row, xh))
            t_self.append((there == row) & (row == col) & (xh == half))

    def part(place):
        return mod8(place - z + 4 * half)

    t_col = [RING * half + part(y + 4 * p) for p in range(2)]
    from_self = (row == col) & ((col == t_col[0]) | (col == t_col[1]))

    barrier = pltpu.get_barrier_semaphore()
    for peer in (sibling, rx_peer, *z_peer.values(), *y_peer, (col, t_col[0], other), (col, t_col[1], other)):
        pl.semaphore_signal(barrier, inc=1, device_id=peer, device_id_type=MESH)
    for p in range(2):
        @pl.when(jnp.logical_not((row == col) & (col == t_col[p])))
        def _():
            pl.semaphore_signal(barrier, inc=1, device_id=(col, t_col[p], half), device_id_type=MESH)

    rows[half, col] = stage[...]
    pl.semaphore_wait(barrier, jnp.where(from_self, 16, 17))

    def remote(src, dst, send, recv, peer):
        return pltpu.make_async_remote_copy(
            src_ref=src, dst_ref=dst, send_sem=send, recv_sem=recv, device_id=peer, device_id_type=MESH)

    def arrived(ref, sem):
        pltpu.make_async_copy(ref, ref, sem).wait()

    pending = []

    def start(copy):
        copy.start()
        pending.append(copy)

    t_copies = []

    def transpose_out(p):
        for s in range(2):
            src = stage.at[pl.ds(s * 32, 32)]
            far = remote(src, traw.at[p, half], t_s.at[p, s], t_r.at[p, half], t_dest[2 * s + p])
            near = pltpu.make_async_copy(src, traw.at[p, half], t_r.at[p, half])

            @pl.when(t_self[2 * s + p])
            def _():
                near.start()

            @pl.when(jnp.logical_not(t_self[2 * s + p]))
            def _():
                far.start()

            t_copies.append((t_self[2 * s + p], far))

    def k_of(u, d):
        return (xh if u == 0 else 1 - xh) * RING + mod8(z + d)

    def row_ref(u, d):
        return rows.at[half, k_of(u, d)]

    def hop(direction, step, u):
        behind, ahead = ((0, 1), (0, 2), (2, 1), (2, 2))[step - 1]
        i = 0 if direction == 1 else 1
        ref = row_ref(u, -direction * behind)
        return remote(ref, ref, rr_s.at[i, step - 1, u], rr_r.at[i, step - 1, u], z_peer[direction * ahead])

    def sends(direction, step, u):
        return step < 4 or (direction == 1) == (u == 0)

    def slots(step, u):
        if step == 0:
            return ((u, 0),)
        if step == 4:
            return ((14 + u, 4),)
        return tuple((2 + (step - 1) * 4 + (0 if n == 1 else 2) + u, -n * step) for n in (1, -1))

    def to_sibling(slot, u, d):
        start(remote(row_ref(u, d), row_ref(u, d), sib_s.at[slot], sib_r.at[slot], sibling))

    def begin_row(u):
        if u == 1:
            arrived(row_ref(1, 0), rx_r)
        for step in (2, 1):
            for direction in (1, -1):
                start(hop(direction, step, u))
        to_sibling(u, u, 0)

    def forward_row(step, u):
        n = 0
        for direction in (1, -1):
            if not sends(direction, step, u):
                continue
            i = 0 if direction == 1 else 1
            slot, d = slots(step, u)[n]
            n += 1
            arrived(row_ref(u, d), rr_r.at[i, step - 1, u])
            for later in (4, 3) if step == 2 else ():
                if sends(direction, later, u):
                    start(hop(direction, later, u))
            to_sibling(slot, u, d)

    def to_lhs(step, u):
        for slot, d in slots(step, u):
            k = k_of(u, d)
            arrived(rows.at[other, k], sib_r.at[slot])
            first, second = rows[0, k], rows[1, k]
            total = jnp.sum(first, axis=1, keepdims=True) + jnp.sum(second, axis=1, keepdims=True)
            mean = total / FRAMES
            here = pl.ds(pl.multiple_of(k * 64, 64), 64)
            for j, value in enumerate((first, second)):
                hi, lo = split(value - mean)
                lhs[here, j * HALF:(j + 1) * HALF] = hi
                lhs[here, FRAMES + j * HALF:FRAMES + (j + 1) * HALF] = lo
                lhs[here, 2 * FRAMES + j * HALF:2 * FRAMES + (j + 1) * HALF] = hi

    def col_ref(place, across, p):
        s = xl if across == p else 1 - xl
        return cols.at[part(mod8(y + place) + 4 * p), s]

    def begin_col(p):
        for g in range(2):
            arrived(traw.at[p, g], t_r.at[p, g])
        first, second = traw[p, 0], traw[p, 1]
        total = jnp.sum(first, axis=1, keepdims=True) + jnp.sum(second, axis=1, keepdims=True)
        mean = total / FRAMES
        mine = col_ref(0, 0, p)
        mine[:, :HALF] = first - mean
        mine[:, HALF:] = second - mean
        for i in range(7):
            start(remote(mine, mine, c_s.at[p, i], c_r.at[p, i], y_peer[i]))

    def wait_col(p, i):
        n, across = near_places[i]
        arrived(col_ref(-n, across, p), c_r.at[p, i])

    base = part(y)
    sign = 1 - 2 * lax.rem(base, 2)

    def tile_of(step):
        return mod8(base + sign * (1, -2, 3, 4)[step - 1]) // 2

    def to_rhs(steps):
        for i, step in enumerate(steps):
            value = cols[pl.ds(2 * tile_of(step), 2)].reshape(TILE, FRAMES) * (1.0 / (FRAMES - 1))
            hi, lo = split(value)
            here = pl.ds(i * TILE, TILE)
            rhs[here, :FRAMES] = hi
            rhs[here, FRAMES:2 * FRAMES] = hi
            rhs[here, 2 * FRAMES:] = lo

    def multiply(steps, u):
        here = pl.ds(pl.multiple_of((xh if u == 0 else 1 - xh) * 512, 512), 512)
        product = lax.dot_general(
            lhs[here, :], rhs[...], (((1,), (1,)), ((), ())), preferred_element_type=jnp.float32)
        for i, step in enumerate(steps):
            there = pl.ds(pl.multiple_of(tile_of(step) * TILE, TILE), TILE)
            out_ref[here, there] = product[:, i * TILE:(i + 1) * TILE]

    transpose_out(0)
    start(remote(row_ref(0, 0), row_ref(0, 0), rx_s, rx_r, rx_peer))
    transpose_out(1)
    begin_row(0)
    begin_row(1)
    begin_col(0)
    forward_row(2, 0)
    begin_col(1)
    to_lhs(0, 0)
    forward_row(2, 1)
    forward_row(1, 0)
    forward_row(1, 1)
    to_lhs(0, 1)
    to_lhs(2, 0)
    to_lhs(1, 0)
    forward_row(3, 0)
    forward_row(4, 0)
    to_lhs(2, 1)
    to_lhs(1, 1)
    forward_row(3, 1)
    forward_row(4, 1)
    to_lhs(3, 0)
    to_lhs(4, 0)
    for i in range(7):
        wait_col(0, i)
    wait_col(1, 0)
    wait_col(1, 1)
    to_rhs((1, 2))
    multiply((1, 2), 0)
    to_lhs(3, 1)
    to_lhs(4, 1)
    multiply((1, 2), 1)
    for i in range(2, 7):
        wait_col(1, i)
    to_rhs((3, 4))
    multiply((3, 4), 0)
    multiply((3, 4), 1)

    for copy in pending:
        copy.wait_send()
    for local, copy in t_copies:
        @pl.when(jnp.logical_not(local))
        def _():
            copy.wait_send()


def body(frames):
    dma = pltpu.SemaphoreType.DMA
    return pl.pallas_call(
        kernel,
        out_shape=jax.ShapeDtypeStruct((1024, 512), jnp.float32),
        in_specs=[pl.BlockSpec(memory_space=pltpu.VMEM)],
        out_specs=pl.BlockSpec(memory_space=pltpu.VMEM),
        scratch_shapes=[
            pltpu.VMEM((2, 2, 32, HALF), jnp.float32),
            pltpu.VMEM((2, 16, 64, HALF), jnp.float32),
            pltpu.VMEM((8, 2, 32, FRAMES), jnp.float32),
            pltpu.VMEM((1024, 3 * FRAMES), jnp.bfloat16),
            pltpu.VMEM((2 * TILE, 3 * FRAMES), jnp.bfloat16),
            dma((2, 2)), dma((2, 2)), dma, dma, dma((2, 4, 2)), dma((2, 4, 2)), dma((2, 7)), dma((2, 7)),
            dma((16,)), dma((16,)),
        ],
        compiler_params=pltpu.CompilerParams(
            collective_id=0, has_side_effects=True, vmem_limit_bytes=40 * 1024 * 1024),
        cost_estimate=pl.CostEstimate(flops=3 * 2 * 1024 * 512 * 512, bytes_accessed=2 << 20, transcendentals=0),
    )(frames.T)


def solution(mesh):
    in_specs = (P("half", ("row", "col")),)
    out_specs = P("row", ("col", "half"))
    return jax.shard_map(body, mesh=mesh, in_specs=in_specs, out_specs=out_specs, check_vma=False)
```

```python
import jax
import jax.numpy as jnp
from jax import lax
from jax.experimental import pallas as pl
from jax.experimental.pallas import tpu as pltpu
from jax.sharding import PartitionSpec as P

MESH = pl.DeviceIdType.MESH
FRAMES = 512
HALF = FRAMES // 2
RING = 8
TILE = 128


def mod8(value):
    return lax.rem(value + 16, RING)


def split(value):
    hi = value.astype(jnp.bfloat16)
    lo = (value - hi.astype(jnp.float32)).astype(jnp.bfloat16)
    return hi, lo


def kernel(stage, out_ref, traw, rows, cols, lhs, rhs,
           t_s, t_r, rx_s, rx_r, cx_s, cx_r, rr_s, rr_r, c_s, c_r, sib_s, sib_r):
    row = lax.axis_index("row")
    col = lax.axis_index("col")
    half = lax.axis_index("half")
    y, xl = row // 2, lax.rem(row, 2)
    xh, z = col // RING, lax.rem(col, RING)
    other = 1 - half

    sibling = (row, col, other)
    rx_peer = (row, (1 - xh) * RING + z, half)
    z_peer = {n: (row, xh * RING + mod8(z + n), half) for n in (1, -1, 2, -2)}
    cx_peer = (y * 2 + 1 - xl, col, half)
    y_peer = {n: (mod8(y + n) * 2 + xl, col, half) for n in (1, -1, 2, -2)}

    yy = mod8(z + lax.rem(row, RING) + 4 * xh)
    t_dest = [(yy * 2 + s, row, xh) for s in range(2)]
    t_self = [(yy * 2 + s == row) & (row == col) & (xh == half) for s in range(2)]

    def part(place):
        return mod8(place - z + 4 * half)

    t_col = RING * half + part(y)
    from_self = (row == col) & (col == t_col)

    barrier = pltpu.get_barrier_semaphore()
    for peer in (sibling, rx_peer, cx_peer, *z_peer.values(), *y_peer.values(), (col, t_col, other)):
        pl.semaphore_signal(barrier, inc=1, device_id=peer, device_id_type=MESH)

    @pl.when(jnp.logical_not(from_self))
    def _():
        pl.semaphore_signal(barrier, inc=1, device_id=(col, t_col, half), device_id_type=MESH)

    rows[half, col] = stage[...]
    pl.semaphore_wait(barrier, jnp.where(from_self, 12, 13))

    def remote(src, dst, send, recv, peer):
        return pltpu.make_async_remote_copy(
            src_ref=src, dst_ref=dst, send_sem=send, recv_sem=recv, device_id=peer, device_id_type=MESH)

    def arrived(ref, sem):
        pltpu.make_async_copy(ref, ref, sem).wait()

    pending = []

    def start(copy):
        copy.start()
        pending.append(copy)

    t_copies = []

    def transpose_out():
        for s in range(2):
            src = stage.at[pl.ds(s * 32, 32)]
            far = remote(src, traw.at[half], t_s.at[s], t_r.at[half], t_dest[s])
            near = pltpu.make_async_copy(src, traw.at[half], t_r.at[half])

            @pl.when(t_self[s])
            def _():
                near.start()

            @pl.when(jnp.logical_not(t_self[s]))
            def _():
                far.start()

            t_copies.append((t_self[s], far))

    def k_of(u, d):
        return (xh if u == 0 else 1 - xh) * RING + mod8(z + d)

    def row_ref(u, d):
        return rows.at[half, k_of(u, d)]

    def col_ref(u, d):
        return cols.at[part(mod8(y + d)), xl if u == 0 else 1 - xl]

    def hop(which, direction, step, u):
        behind, ahead = ((0, 1), (0, 2), (2, 1), (2, 2))[step - 1]
        at = (0 if direction == 1 else 1, step - 1, u)
        if which == "row":
            ref, send, recv, peer = row_ref(u, -direction * behind), rr_s, rr_r, z_peer[direction * ahead]
        else:
            ref, send, recv, peer = col_ref(u, -direction * behind), c_s, c_r, y_peer[direction * ahead]
        return remote(ref, ref, send.at[at], recv.at[at], peer)

    def sends(direction, step, u):
        return step < 4 or (direction == 1) == (u == 0)

    def slots(step, u):
        if step == 0:
            return ((u, 0),)
        if step == 4:
            return ((14 + u, 4),)
        return tuple((2 + (step - 1) * 4 + (0 if n == 1 else 2) + u, -n * step) for n in (1, -1))

    def to_sibling(slot, u, d):
        start(remote(row_ref(u, d), row_ref(u, d), sib_s.at[slot], sib_r.at[slot], sibling))

    def first_hops(which, u):
        for step in (2, 1):
            for direction in (1, -1):
                start(hop(which, direction, step, u))

    def begin_row(u):
        if u == 1:
            arrived(row_ref(1, 0), rx_r)
        first_hops("row", u)
        to_sibling(u, u, 0)

    def forward(which, step, u):
        n = 0
        for direction in (1, -1):
            if not sends(direction, step, u):
                continue
            slot, d = slots(step, u)[n]
            n += 1
            ref, recv = (row_ref(u, d), rr_r) if which == "row" else (col_ref(u, d), c_r)
            arrived(ref, recv.at[0 if direction == 1 else 1, step - 1, u])
            for later in (4, 3) if step == 2 else ():
                if sends(direction, later, u):
                    start(hop(which, direction, later, u))
            if which == "row":
                to_sibling(slot, u, d)

    def to_lhs(step, u):
        for slot, d in slots(step, u):
            k = k_of(u, d)
            arrived(rows.at[other, k], sib_r.at[slot])
            first, second = rows[0, k], rows[1, k]
            total = jnp.sum(first, axis=1, keepdims=True) + jnp.sum(second, axis=1, keepdims=True)
            mean = total / FRAMES
            here = pl.ds(pl.multiple_of(k * 64, 64), 64)
            for j, value in enumerate((first, second)):
                hi, lo = split(value - mean)
                lhs[here, j * HALF:(j + 1) * HALF] = hi
                lhs[here, FRAMES + j * HALF:FRAMES + (j + 1) * HALF] = lo
                lhs[here, 2 * FRAMES + j * HALF:2 * FRAMES + (j + 1) * HALF] = hi

    def begin_col(u):
        if u == 1:
            arrived(col_ref(1, 0), cx_r)
            first_hops("col", 1)
            return
        for g in range(2):
            arrived(traw.at[g], t_r.at[g])
        first, second = traw[0], traw[1]
        total = jnp.sum(first, axis=1, keepdims=True) + jnp.sum(second, axis=1, keepdims=True)
        mean = total / FRAMES
        mine = col_ref(0, 0)
        mine[:, :HALF] = first - mean
        mine[:, HALF:] = second - mean
        start(remote(mine, mine, cx_s, cx_r, cx_peer))
        first_hops("col", 0)

    base = part(y)
    sign = 1 - 2 * lax.rem(base, 2)

    def tile_of(step):
        return mod8(base + sign * (1, -2, 3, 4)[step - 1]) // 2

    def to_rhs(steps):
        for i, step in enumerate(steps):
            value = cols[pl.ds(2 * tile_of(step), 2)].reshape(TILE, FRAMES) * (1.0 / (FRAMES - 1))
            hi, lo = split(value)
            here = pl.ds(i * TILE, TILE)
            rhs[here, :FRAMES] = hi
            rhs[here, FRAMES:2 * FRAMES] = hi
            rhs[here, 2 * FRAMES:] = lo

    def multiply(steps, u):
        here = pl.ds(pl.multiple_of((xh if u == 0 else 1 - xh) * 512, 512), 512)
        product = lax.dot_general(
            lhs[here, :], rhs[...], (((1,), (1,)), ((), ())), preferred_element_type=jnp.float32)
        for i, step in enumerate(steps):
            there = pl.ds(pl.multiple_of(tile_of(step) * TILE, TILE), TILE)
            out_ref[here, there] = product[:, i * TILE:(i + 1) * TILE]

    transpose_out()
    start(remote(row_ref(0, 0), row_ref(0, 0), rx_s, rx_r, rx_peer))
    begin_row(0)
    begin_row(1)
    begin_col(0)
    forward("row", 2, 0)
    begin_col(1)
    forward("row", 2, 1)
    forward("col", 2, 0)
    forward("row", 1, 0)
    to_lhs(0, 0)
    to_lhs(0, 1)
    forward("col", 2, 1)
    forward("row", 1, 1)
    to_lhs(2, 0)
    forward("row", 3, 0)
    forward("row", 4, 0)
    to_lhs(1, 0)
    to_lhs(2, 1)
    to_lhs(1, 1)
    forward("row", 3, 1)
    forward("row", 4, 1)
    to_lhs(3, 0)
    to_lhs(4, 0)
    for u in range(2):
        forward("col", 1, u)
    to_rhs((1, 2))
    multiply((1, 2), 0)
    to_lhs(3, 1)
    to_lhs(4, 1)
    multiply((1, 2), 1)
    for u in range(2):
        forward("col", 3, u)
        forward("col", 4, u)
    to_rhs((3, 4))
    multiply((3, 4), 0)
    multiply((3, 4), 1)

    for copy in pending:
        copy.wait_send()
    for local, copy in t_copies:
        @pl.when(jnp.logical_not(local))
        def _():
            copy.wait_send()


def body(frames):
    dma = pltpu.SemaphoreType.DMA
    return pl.pallas_call(
        kernel,
        out_shape=jax.ShapeDtypeStruct((1024, 512), jnp.float32),
        in_specs=[pl.BlockSpec(memory_space=pltpu.VMEM)],
        out_specs=pl.BlockSpec(memory_space=pltpu.VMEM),
        scratch_shapes=[
            pltpu.VMEM((2, 32, HALF), jnp.float32),
            pltpu.VMEM((2, 16, 64, HALF), jnp.float32),
            pltpu.VMEM((8, 2, 32, FRAMES), jnp.float32),
            pltpu.VMEM((1024, 3 * FRAMES), jnp.bfloat16),
            pltpu.VMEM((2 * TILE, 3 * FRAMES), jnp.bfloat16),
            dma((2,)), dma((2,)), dma, dma, dma, dma, dma((2, 4, 2)), dma((2, 4, 2)), dma((2, 4, 2)), dma((2, 4, 2)),
            dma((16,)), dma((16,)),
        ],
        compiler_params=pltpu.CompilerParams(
            collective_id=0, has_side_effects=True, vmem_limit_bytes=40 * 1024 * 1024),
        cost_estimate=pl.CostEstimate(flops=3 * 2 * 1024 * 512 * 512, bytes_accessed=2 << 20, transcendentals=0),
    )(frames.T)


def solution(mesh):
    in_specs = (P("half", ("row", "col")),)
    out_specs = P("row", ("col", "half"))
    return jax.shard_map(body, mesh=mesh, in_specs=in_specs, out_specs=out_specs, check_vma=False)
```

```python
import jax
import jax.numpy as jnp
from jax import lax
from jax.experimental import pallas as pl
from jax.experimental.pallas import tpu as pltpu
from jax.sharding import PartitionSpec as P

MESH = pl.DeviceIdType.MESH
FRAMES = 512
HALF = FRAMES // 2
RING = 8
TILE = 128


def mod8(value):
    return lax.rem(value + 16, RING)


def split(value):
    hi = value.astype(jnp.bfloat16)
    lo = (value - hi.astype(jnp.float32)).astype(jnp.bfloat16)
    return hi, lo


def kernel(stage, out_ref, traw, rows, cols, lhs, rhs,
           t_s, t_r, rx_s, rx_r, cx_s, cx_r, rr_s, rr_r, c_s, c_r, sib_s, sib_r):
    row = lax.axis_index("row")
    col = lax.axis_index("col")
    half = lax.axis_index("half")
    y, xl = row // 2, lax.rem(row, 2)
    xh, z = col // RING, lax.rem(col, RING)
    other = 1 - half

    sibling = (row, col, other)
    rx_peer = (row, (1 - xh) * RING + z, half)
    z_peer = {n: (row, xh * RING + mod8(z + n), half) for n in (1, -1, 2, -2)}
    cx_peer = (y * 2 + 1 - xl, col, half)
    y_peer = {n: (mod8(y + n) * 2 + xl, col, half) for n in (1, -1, 2, -2)}
    diagonal = {n: (mod8(y + n) * 2 + 1 - xl, col, half) for n in (1, -1, 2, -2)}

    yy = mod8(z + lax.rem(row, RING) + 4 * xh)
    t_dest = [(yy * 2 + s, row, xh) for s in range(2)]
    t_self = [(yy * 2 + s == row) & (row == col) & (xh == half) for s in range(2)]

    def part(place):
        return mod8(place - z + 4 * half)

    t_col = RING * half + part(y)
    from_self = (row == col) & (col == t_col)

    barrier = pltpu.get_barrier_semaphore()
    for peer in (sibling, rx_peer, cx_peer, *z_peer.values(), *y_peer.values(), *diagonal.values(), (col, t_col, other)):
        pl.semaphore_signal(barrier, inc=1, device_id=peer, device_id_type=MESH)

    @pl.when(jnp.logical_not(from_self))
    def _():
        pl.semaphore_signal(barrier, inc=1, device_id=(col, t_col, half), device_id_type=MESH)

    rows[half, col] = stage[...]
    pl.semaphore_wait(barrier, jnp.where(from_self, 16, 17))

    def remote(src, dst, send, recv, peer):
        return pltpu.make_async_remote_copy(
            src_ref=src, dst_ref=dst, send_sem=send, recv_sem=recv, device_id=peer, device_id_type=MESH)

    def arrived(ref, sem):
        pltpu.make_async_copy(ref, ref, sem).wait()

    pending = []

    def start(copy):
        copy.start()
        pending.append(copy)

    t_copies = []

    def transpose_out():
        for s in range(2):
            src = stage.at[pl.ds(s * 32, 32)]
            far = remote(src, traw.at[half], t_s.at[s], t_r.at[half], t_dest[s])
            near = pltpu.make_async_copy(src, traw.at[half], t_r.at[half])

            @pl.when(t_self[s])
            def _():
                near.start()

            @pl.when(jnp.logical_not(t_self[s]))
            def _():
                far.start()

            t_copies.append((t_self[s], far))

    def k_of(u, d):
        return (xh if u == 0 else 1 - xh) * RING + mod8(z + d)

    def row_ref(u, d):
        return rows.at[half, k_of(u, d)]

    def col_ref(u, d):
        return cols.at[part(mod8(y + d)), xl if u == 0 else 1 - xl]

    def hop(which, direction, step, u):
        behind, ahead = ((0, 1), (0, 2), (2, 1), (2, 2))[step - 1]
        at = (0 if direction == 1 else 1, step - 1, u)
        if which == "row":
            ref, send, recv, peer = row_ref(u, -direction * behind), rr_s, rr_r, z_peer[direction * ahead]
        elif u == 1 and step < 3:
            ref, send, recv, peer = col_ref(0, 0), c_s, c_r, diagonal[direction * ahead]
        else:
            ref, send, recv, peer = col_ref(u, -direction * behind), c_s, c_r, y_peer[direction * ahead]
        return remote(ref, ref, send.at[at], recv.at[at], peer)

    def sends(direction, step, u):
        return step < 4 or (direction == 1) == (u == 0)

    def slots(step, u):
        if step == 0:
            return ((u, 0),)
        if step == 4:
            return ((14 + u, 4),)
        return tuple((2 + (step - 1) * 4 + (0 if n == 1 else 2) + u, -n * step) for n in (1, -1))

    def to_sibling(slot, u, d):
        start(remote(row_ref(u, d), row_ref(u, d), sib_s.at[slot], sib_r.at[slot], sibling))

    def begin_row(u):
        if u == 1:
            arrived(row_ref(1, 0), rx_r)
        for step in (2, 1):
            for direction in (1, -1):
                start(hop("row", direction, step, u))
        to_sibling(u, u, 0)

    def forward(which, step, u):
        n = 0
        for direction in (1, -1):
            if not sends(direction, step, u):
                continue
            slot, d = slots(step, u)[n]
            n += 1
            ref, recv = (row_ref(u, d), rr_r) if which == "row" else (col_ref(u, d), c_r)
            arrived(ref, recv.at[0 if direction == 1 else 1, step - 1, u])
            for later in (4, 3) if step == 2 else ():
                if sends(direction, later, u):
                    start(hop(which, direction, later, u))
            if which == "row":
                to_sibling(slot, u, d)

    def to_lhs(step, u):
        for slot, d in slots(step, u):
            k = k_of(u, d)
            arrived(rows.at[other, k], sib_r.at[slot])
            first, second = rows[0, k], rows[1, k]
            total = jnp.sum(first, axis=1, keepdims=True) + jnp.sum(second, axis=1, keepdims=True)
            mean = total / FRAMES
            here = pl.ds(pl.multiple_of(k * 64, 64), 64)
            for j, value in enumerate((first, second)):
                hi, lo = split(value - mean)
                lhs[here, j * HALF:(j + 1) * HALF] = hi
                lhs[here, FRAMES + j * HALF:FRAMES + (j + 1) * HALF] = lo
                lhs[here, 2 * FRAMES + j * HALF:2 * FRAMES + (j + 1) * HALF] = hi

    def begin_col():
        for g in range(2):
            arrived(traw.at[g], t_r.at[g])
        first, second = traw[0], traw[1]
        total = jnp.sum(first, axis=1, keepdims=True) + jnp.sum(second, axis=1, keepdims=True)
        mean = total / FRAMES
        mine = col_ref(0, 0)
        mine[:, :HALF] = first - mean
        mine[:, HALF:] = second - mean
        for step in (2, 1):
            for u in range(2):
                for direction in (1, -1):
                    start(hop("col", direction, step, u))
        start(remote(mine, mine, cx_s, cx_r, cx_peer))

    base = part(y)
    sign = 1 - 2 * lax.rem(base, 2)

    def tile_of(step):
        return mod8(base + sign * (1, -2, 3, 4)[step - 1]) // 2

    def to_rhs(steps):
        for i, step in enumerate(steps):
            value = cols[pl.ds(2 * tile_of(step), 2)].reshape(TILE, FRAMES) * (1.0 / (FRAMES - 1))
            hi, lo = split(value)
            here = pl.ds(i * TILE, TILE)
            rhs[here, :FRAMES] = hi
            rhs[here, FRAMES:2 * FRAMES] = hi
            rhs[here, 2 * FRAMES:] = lo

    def multiply(steps, u):
        here = pl.ds(pl.multiple_of((xh if u == 0 else 1 - xh) * 512, 512), 512)
        product = lax.dot_general(
            lhs[here, :], rhs[...], (((1,), (1,)), ((), ())), preferred_element_type=jnp.float32)
        for i, step in enumerate(steps):
            there = pl.ds(pl.multiple_of(tile_of(step) * TILE, TILE), TILE)
            out_ref[here, there] = product[:, i * TILE:(i + 1) * TILE]

    transpose_out()
    start(remote(row_ref(0, 0), row_ref(0, 0), rx_s, rx_r, rx_peer))
    begin_row(0)
    begin_row(1)
    begin_col()
    forward("row", 2, 0)
    forward("row", 1, 0)
    forward("row", 2, 1)
    to_lhs(0, 0)
    forward("col", 2, 0)
    forward("col", 2, 1)
    forward("row", 1, 1)
    to_lhs(0, 1)
    to_lhs(2, 0)
    to_lhs(1, 0)
    forward("row", 3, 0)
    forward("row", 4, 0)
    to_lhs(2, 1)
    to_lhs(1, 1)
    forward("row", 3, 1)
    forward("row", 4, 1)
    to_lhs(3, 0)
    to_lhs(4, 0)
    forward("col", 1, 0)
    forward("col", 1, 1)
    arrived(col_ref(1, 0), cx_r)
    to_rhs((1, 2))
    multiply((1, 2), 0)
    to_lhs(3, 1)
    to_lhs(4, 1)
    multiply((1, 2), 1)
    for u in range(2):
        forward("col", 3, u)
        forward("col", 4, u)
    to_rhs((3, 4))
    multiply((3, 4), 0)
    multiply((3, 4), 1)

    for copy in pending:
        copy.wait_send()
    for local, copy in t_copies:
        @pl.when(jnp.logical_not(local))
        def _():
            copy.wait_send()


def body(frames):
    dma = pltpu.SemaphoreType.DMA
    return pl.pallas_call(
        kernel,
        out_shape=jax.ShapeDtypeStruct((1024, 512), jnp.float32),
        in_specs=[pl.BlockSpec(memory_space=pltpu.VMEM)],
        out_specs=pl.BlockSpec(memory_space=pltpu.VMEM),
        scratch_shapes=[
            pltpu.VMEM((2, 32, HALF), jnp.float32),
            pltpu.VMEM((2, 16, 64, HALF), jnp.float32),
            pltpu.VMEM((8, 2, 32, FRAMES), jnp.float32),
            pltpu.VMEM((1024, 3 * FRAMES), jnp.bfloat16),
            pltpu.VMEM((2 * TILE, 3 * FRAMES), jnp.bfloat16),
            dma((2,)), dma((2,)), dma, dma, dma, dma, dma((2, 4, 2)), dma((2, 4, 2)), dma((2, 4, 2)), dma((2, 4, 2)),
            dma((16,)), dma((16,)),
        ],
        compiler_params=pltpu.CompilerParams(
            collective_id=0, has_side_effects=True, vmem_limit_bytes=40 * 1024 * 1024),
        cost_estimate=pl.CostEstimate(flops=3 * 2 * 1024 * 512 * 512, bytes_accessed=2 << 20, transcendentals=0),
    )(frames.T)


def solution(mesh):
    in_specs = (P("half", ("row", "col")),)
    out_specs = P("row", ("col", "half"))
    return jax.shard_map(body, mesh=mesh, in_specs=in_specs, out_specs=out_specs, check_vma=False)
```

```python
import jax
import jax.numpy as jnp
from jax import lax
from jax.experimental import pallas as pl
from jax.experimental.pallas import tpu as pltpu
from jax.sharding import PartitionSpec as P

MESH = pl.DeviceIdType.MESH
FRAMES = 512
HALF = FRAMES // 2
RING = 8
TILE = 128


def mod8(value):
    return lax.rem(value + 16, RING)


def split(value):
    hi = value.astype(jnp.bfloat16)
    lo = (value - hi.astype(jnp.float32)).astype(jnp.bfloat16)
    return hi, lo


def kernel(stage, out_ref, traw, rows, cols, lhs, rhs,
           t_s, t_r, rx_s, rx_r, cx_s, cx_r, rr_s, rr_r, c_s, c_r, sib_s, sib_r):
    row = lax.axis_index("row")
    col = lax.axis_index("col")
    half = lax.axis_index("half")
    y, xl = row // 2, lax.rem(row, 2)
    xh, z = col // RING, lax.rem(col, RING)
    other = 1 - half

    sibling = (row, col, other)
    rx_peer = (row, (1 - xh) * RING + z, half)
    z_peer = {n: (row, xh * RING + mod8(z + n), half) for n in (1, -1, 2, -2)}
    cx_peer = (y * 2 + 1 - xl, col, half)
    y_peer = {n: (mod8(y + n) * 2 + xl, col, half) for n in (1, -1, 2, -2)}
    diagonal = {n: (mod8(y + n) * 2 + 1 - xl, col, half) for n in (1, -1, 2, -2)}

    yy = mod8(z + lax.rem(row, RING) + 4 * xh)
    t_dest = [(yy * 2 + s, row, xh) for s in range(2)]
    t_self = [(yy * 2 + s == row) & (row == col) & (xh == half) for s in range(2)]

    def part(place):
        return mod8(place - z + 4 * half)

    t_col = RING * half + part(y)
    from_self = (row == col) & (col == t_col)

    barrier = pltpu.get_barrier_semaphore()
    for peer in (sibling, rx_peer, cx_peer, *z_peer.values(), *y_peer.values(), *diagonal.values(), (col, t_col, other)):
        pl.semaphore_signal(barrier, inc=1, device_id=peer, device_id_type=MESH)

    @pl.when(jnp.logical_not(from_self))
    def _():
        pl.semaphore_signal(barrier, inc=1, device_id=(col, t_col, half), device_id_type=MESH)

    rows[half, col] = stage[...]
    pl.semaphore_wait(barrier, jnp.where(from_self, 16, 17))

    def remote(src, dst, send, recv, peer):
        return pltpu.make_async_remote_copy(
            src_ref=src, dst_ref=dst, send_sem=send, recv_sem=recv, device_id=peer, device_id_type=MESH)

    def arrived(ref, sem):
        pltpu.make_async_copy(ref, ref, sem).wait()

    pending = []

    def start(copy):
        copy.start()
        pending.append(copy)

    t_copies = []

    def transpose_out():
        for s in range(2):
            src = stage.at[pl.ds(s * 32, 32)]
            far = remote(src, traw.at[half], t_s.at[s], t_r.at[half], t_dest[s])
            near = pltpu.make_async_copy(src, traw.at[half], t_r.at[half])

            @pl.when(t_self[s])
            def _():
                near.start()

            @pl.when(jnp.logical_not(t_self[s]))
            def _():
                far.start()

            t_copies.append((t_self[s], far))

    def k_of(u, d):
        return (xh if u == 0 else 1 - xh) * RING + mod8(z + d)

    def row_ref(u, d):
        return rows.at[half, k_of(u, d)]

    def col_ref(u, d):
        return cols.at[part(mod8(y + d)), xl if u == 0 else 1 - xl]

    def hop(which, direction, step, u):
        behind, ahead = ((0, 1), (0, 2), (2, 1), (2, 2))[step - 1]
        at = (0 if direction == 1 else 1, step - 1, u)
        if which == "row":
            ref, send, recv, peer = row_ref(u, -direction * behind), rr_s, rr_r, z_peer[direction * ahead]
            return remote(ref, ref, send.at[at], recv.at[at], peer)
        if u == 0:
            peer = y_peer[direction * ahead]
        elif step == 2:
            behind, peer = 2, cx_peer
        else:
            peer = diagonal[direction * ahead]
        ref = col_ref(0, -direction * behind)
        return remote(ref, ref, c_s.at[at], c_r.at[at], peer)

    def sends(direction, step, u):
        return step < 4 or (direction == 1) == (u == 0)

    def slots(step, u):
        if step == 0:
            return ((u, 0),)
        if step == 4:
            return ((14 + u, 4),)
        return tuple((2 + (step - 1) * 4 + (0 if n == 1 else 2) + u, -n * step) for n in (1, -1))

    def to_sibling(slot, u, d):
        start(remote(row_ref(u, d), row_ref(u, d), sib_s.at[slot], sib_r.at[slot], sibling))

    def begin_row(u):
        if u == 1:
            arrived(row_ref(1, 0), rx_r)
        for step in (2, 1):
            for direction in (1, -1):
                start(hop("row", direction, step, u))
        to_sibling(u, u, 0)

    def forward(which, step, u):
        n = 0
        for direction in (1, -1):
            if not sends(direction, step, u):
                continue
            slot, d = slots(step, u)[n]
            n += 1
            ref, recv = (row_ref(u, d), rr_r) if which == "row" else (col_ref(u, d), c_r)
            arrived(ref, recv.at[0 if direction == 1 else 1, step - 1, u])
            if which == "row" and step == 2:
                onward = ((4, u), (3, u))
            elif step == 2 and u == 0:
                onward = ((4, 0), (4, 1), (3, 0), (3, 1), (2, 1))
            else:
                onward = ()
            for later, v in onward:
                if sends(direction, later, v):
                    start(hop(which, direction, later, v))
            if which == "row":
                to_sibling(slot, u, d)

    def to_lhs(step, u):
        for slot, d in slots(step, u):
            k = k_of(u, d)
            arrived(rows.at[other, k], sib_r.at[slot])
            first, second = rows[0, k], rows[1, k]
            total = jnp.sum(first, axis=1, keepdims=True) + jnp.sum(second, axis=1, keepdims=True)
            mean = total / FRAMES
            here = pl.ds(pl.multiple_of(k * 64, 64), 64)
            for j, value in enumerate((first, second)):
                hi, lo = split(value - mean)
                lhs[here, j * HALF:(j + 1) * HALF] = hi
                lhs[here, FRAMES + j * HALF:FRAMES + (j + 1) * HALF] = lo
                lhs[here, 2 * FRAMES + j * HALF:2 * FRAMES + (j + 1) * HALF] = hi

    def begin_col():
        for g in range(2):
            arrived(traw.at[g], t_r.at[g])
        first, second = traw[0], traw[1]
        total = jnp.sum(first, axis=1, keepdims=True) + jnp.sum(second, axis=1, keepdims=True)
        mean = total / FRAMES
        mine = col_ref(0, 0)
        mine[:, :HALF] = first - mean
        mine[:, HALF:] = second - mean
        for step, u in ((2, 0), (1, 0), (1, 1)):
            for direction in (1, -1):
                start(hop("col", direction, step, u))
        start(remote(mine, mine, cx_s, cx_r, cx_peer))

    base = part(y)
    sign = 1 - 2 * lax.rem(base, 2)

    def tile_of(step):
        return mod8(base + sign * (1, -2, 3, 4)[step - 1]) // 2

    def to_rhs(steps):
        for i, step in enumerate(steps):
            value = cols[pl.ds(2 * tile_of(step), 2)].reshape(TILE, FRAMES) * (1.0 / (FRAMES - 1))
            hi, lo = split(value)
            here = pl.ds(i * TILE, TILE)
            rhs[here, :FRAMES] = hi
            rhs[here, FRAMES:2 * FRAMES] = hi
            rhs[here, 2 * FRAMES:] = lo

    def multiply(steps, u):
        here = pl.ds(pl.multiple_of((xh if u == 0 else 1 - xh) * 512, 512), 512)
        product = lax.dot_general(
            lhs[here, :], rhs[...], (((1,), (1,)), ((), ())), preferred_element_type=jnp.float32)
        for i, step in enumerate(steps):
            there = pl.ds(pl.multiple_of(tile_of(step) * TILE, TILE), TILE)
            out_ref[here, there] = product[:, i * TILE:(i + 1) * TILE]

    transpose_out()
    start(remote(row_ref(0, 0), row_ref(0, 0), rx_s, rx_r, rx_peer))
    begin_row(0)
    begin_row(1)
    begin_col()
    forward("row", 2, 0)
    forward("row", 1, 0)
    forward("row", 2, 1)
    to_lhs(0, 0)
    forward("col", 2, 0)
    forward("row", 1, 1)
    to_lhs(0, 1)
    to_lhs(2, 0)
    to_lhs(1, 0)
    forward("row", 3, 0)
    forward("row", 4, 0)
    to_lhs(2, 1)
    to_lhs(1, 1)
    forward("row", 3, 1)
    forward("row", 4, 1)
    to_lhs(3, 0)
    to_lhs(4, 0)
    forward("col", 1, 0)
    forward("col", 1, 1)
    forward("col", 2, 1)
    arrived(col_ref(1, 0), cx_r)
    to_rhs((1, 2))
    multiply((1, 2), 0)
    to_lhs(3, 1)
    to_lhs(4, 1)
    multiply((1, 2), 1)
    for u in range(2):
        forward("col", 3, u)
        forward("col", 4, u)
    to_rhs((3, 4))
    multiply((3, 4), 0)
    multiply((3, 4), 1)

    for copy in pending:
        copy.wait_send()
    for local, copy in t_copies:
        @pl.when(jnp.logical_not(local))
        def _():
            copy.wait_send()


def body(frames):
    dma = pltpu.SemaphoreType.DMA
    return pl.pallas_call(
        kernel,
        out_shape=jax.ShapeDtypeStruct((1024, 512), jnp.float32),
        in_specs=[pl.BlockSpec(memory_space=pltpu.VMEM)],
        out_specs=pl.BlockSpec(memory_space=pltpu.VMEM),
        scratch_shapes=[
            pltpu.VMEM((2, 32, HALF), jnp.float32),
            pltpu.VMEM((2, 16, 64, HALF), jnp.float32),
            pltpu.VMEM((8, 2, 32, FRAMES), jnp.float32),
            pltpu.VMEM((1024, 3 * FRAMES), jnp.bfloat16),
            pltpu.VMEM((2 * TILE, 3 * FRAMES), jnp.bfloat16),
            dma((2,)), dma((2,)), dma, dma, dma, dma, dma((2, 4, 2)), dma((2, 4, 2)), dma((2, 4, 2)), dma((2, 4, 2)),
            dma((16,)), dma((16,)),
        ],
        compiler_params=pltpu.CompilerParams(
            collective_id=0, has_side_effects=True, vmem_limit_bytes=40 * 1024 * 1024),
        cost_estimate=pl.CostEstimate(flops=3 * 2 * 1024 * 512 * 512, bytes_accessed=2 << 20, transcendentals=0),
    )(frames.T)


def solution(mesh):
    in_specs = (P("half", ("row", "col")),)
    out_specs = P("row", ("col", "half"))
    return jax.shard_map(body, mesh=mesh, in_specs=in_specs, out_specs=out_specs, check_vma=False)
```

```python
import jax
import jax.numpy as jnp
from jax import lax
from jax.experimental import pallas as pl
from jax.experimental.pallas import tpu as pltpu
from jax.sharding import PartitionSpec as P

MESH = pl.DeviceIdType.MESH
FRAMES = 512
HALF = FRAMES // 2
RING = 8
TILE = 128


def mod8(value):
    return lax.rem(value + 16, RING)


def split(value):
    hi = value.astype(jnp.bfloat16)
    lo = (value - hi.astype(jnp.float32)).astype(jnp.bfloat16)
    return hi, lo


def kernel(stage, out_ref, traw, rows, cols, lhs, rhs,
           t_s, t_r, rx_s, rx_r, cx_s, cx_r, rr_s, rr_r, c_s, c_r, sib_s, sib_r):
    row = lax.axis_index("row")
    col = lax.axis_index("col")
    half = lax.axis_index("half")
    y, xl = row // 2, lax.rem(row, 2)
    xh, z = col // RING, lax.rem(col, RING)
    other = 1 - half

    sibling = (row, col, other)
    rx_peer = (row, (1 - xh) * RING + z, half)
    z_peer = {n: (row, xh * RING + mod8(z + n), half) for n in (1, -1, 2, -2)}
    cx_peer = (y * 2 + 1 - xl, col, half)
    y_peer = {n: (mod8(y + n) * 2 + xl, col, half) for n in (1, -1, 2, -2)}
    diagonal = {n: (mod8(y + n) * 2 + 1 - xl, col, half) for n in (1, -1, 2, -2)}

    yy = mod8(z + lax.rem(row, RING) + 4 * xh)
    t_dest = [(yy * 2 + s, row, xh) for s in range(2)]
    t_self = [(yy * 2 + s == row) & (row == col) & (xh == half) for s in range(2)]

    def part(place):
        return mod8(place - z + 4 * half)

    t_col = RING * half + part(y)
    from_self = (row == col) & (col == t_col)

    barrier = pltpu.get_barrier_semaphore()
    for peer in (sibling, rx_peer, cx_peer, *z_peer.values(), *y_peer.values(), *diagonal.values(), (col, t_col, other)):
        pl.semaphore_signal(barrier, inc=1, device_id=peer, device_id_type=MESH)

    @pl.when(jnp.logical_not(from_self))
    def _():
        pl.semaphore_signal(barrier, inc=1, device_id=(col, t_col, half), device_id_type=MESH)

    rows[half, xh, z] = stage[...]
    pl.semaphore_wait(barrier, jnp.where(from_self, 16, 17))

    def remote(src, dst, send, recv, peer):
        return pltpu.make_async_remote_copy(
            src_ref=src, dst_ref=dst, send_sem=send, recv_sem=recv, device_id=peer, device_id_type=MESH)

    def arrived(ref, sem):
        pltpu.make_async_copy(ref, ref, sem).wait()

    pending = []

    def start(copy):
        copy.start()
        pending.append(copy)

    t_copies = []

    def transpose_out():
        for s in range(2):
            src = stage.at[pl.ds(s * 32, 32)]
            far = remote(src, traw.at[half], t_s.at[s], t_r.at[half], t_dest[s])
            near = pltpu.make_async_copy(src, traw.at[half], t_r.at[half])

            @pl.when(t_self[s])
            def _():
                near.start()

            @pl.when(jnp.logical_not(t_self[s]))
            def _():
                far.start()

            t_copies.append((t_self[s], far))

    signs = (1, -1)
    distances = (0, -1, 1, -2, 2, -3, 3, 4)

    def row_ref(u, d):
        return rows.at[half, xh if u == 0 else 1 - xh, mod8(z + d)]

    def row_pair(d, core):
        return rows.at[core, :, mod8(z + d)]

    def col_ref(u, d):
        return cols.at[part(mod8(y + d)), xl if u == 0 else 1 - xl]

    def col_pair(d):
        return cols.at[part(mod8(y + d))]

    def hop(which, direction, step, u):
        behind, ahead = ((0, 1), (0, 2), (2, 1), (2, 2))[step - 1]
        at = (0 if direction == 1 else 1, step - 1, u)
        d = -direction * behind
        if which == "row":
            ref = row_pair(d, half) if step == 3 else row_ref(u, d)
            return remote(ref, ref, rr_s.at[at], rr_r.at[at], z_peer[direction * ahead])
        peer = y_peer[direction * ahead]
        if step == 3:
            ref = col_pair(d)
        elif u == 1 and step < 3:
            ref, peer = col_ref(0, 0), diagonal[direction * ahead]
        else:
            ref = col_ref(u, d)
        return remote(ref, ref, c_s.at[at], c_r.at[at], peer)

    def to_sibling(d):
        slot = distances.index(d)
        start(remote(row_pair(d, half), row_pair(d, half), sib_s.at[slot], sib_r.at[slot], sibling))

    def begin_row(u):
        if u == 1:
            arrived(row_ref(1, 0), rx_r)
        for step in (2, 1):
            for direction in signs:
                start(hop("row", direction, step, u))
        if u == 1:
            to_sibling(0)

    def come(which, direction, step):
        recv = rr_r if which == "row" else c_r
        i = 0 if direction == 1 else 1
        d = -direction * step
        if step == 3:
            arrived(row_pair(d, half) if which == "row" else col_pair(d), recv.at[i, 2, 0])
        elif step == 4:
            u = i
            arrived(row_ref(u, 4) if which == "row" else col_ref(u, 4), recv.at[i, 3, u])
        else:
            for u in range(2):
                arrived(row_ref(u, d) if which == "row" else col_ref(u, d), recv.at[i, step - 1, u])

    def forward(which, step):
        for direction in signs:
            come(which, direction, step)
            if step == 2:
                start(hop(which, direction, 4, 0 if direction == 1 else 1))
                start(hop(which, direction, 3, 0))
            if which == "row" and step < 4:
                to_sibling(-direction * step)
        if which == "row" and step == 4:
            to_sibling(4)

    def to_lhs(*ds):
        for d in ds:
            arrived(row_pair(d, other), sib_r.at[distances.index(d)])
            for x in range(2):
                first, second = rows[0, x, mod8(z + d)], rows[1, x, mod8(z + d)]
                total = jnp.sum(first, axis=1, keepdims=True) + jnp.sum(second, axis=1, keepdims=True)
                mean = total / FRAMES
                here = pl.ds(pl.multiple_of(x * 512 + mod8(z + d) * 64, 64), 64)
                for j, value in enumerate((first, second)):
                    hi, lo = split(value - mean)
                    lhs[here, j * HALF:(j + 1) * HALF] = hi
                    lhs[here, FRAMES + j * HALF:FRAMES + (j + 1) * HALF] = lo
                    lhs[here, 2 * FRAMES + j * HALF:2 * FRAMES + (j + 1) * HALF] = hi

    def begin_col():
        for g in range(2):
            arrived(traw.at[g], t_r.at[g])
        first, second = traw[0], traw[1]
        total = jnp.sum(first, axis=1, keepdims=True) + jnp.sum(second, axis=1, keepdims=True)
        mean = total / FRAMES
        mine = col_ref(0, 0)
        mine[:, :HALF] = first - mean
        mine[:, HALF:] = second - mean
        for step in (2, 1):
            for u in range(2):
                for direction in (1, -1):
                    start(hop("col", direction, step, u))
        start(remote(mine, mine, cx_s, cx_r, cx_peer))

    base = part(y)
    sign = 1 - 2 * lax.rem(base, 2)

    def tile_of(step):
        return mod8(base + sign * (1, -2, 3, 4)[step - 1]) // 2

    def to_rhs(steps):
        for i, step in enumerate(steps):
            value = cols[pl.ds(2 * tile_of(step), 2)].reshape(TILE, FRAMES) * (1.0 / (FRAMES - 1))
            hi, lo = split(value)
            here = pl.ds(i * TILE, TILE)
            rhs[here, :FRAMES] = hi
            rhs[here, FRAMES:2 * FRAMES] = hi
            rhs[here, 2 * FRAMES:] = lo

    def multiply(steps, u):
        here = pl.ds(u * 512, 512)
        product = lax.dot_general(
            lhs[here, :], rhs[...], (((1,), (1,)), ((), ())), preferred_element_type=jnp.float32)
        for i, step in enumerate(steps):
            there = pl.ds(pl.multiple_of(tile_of(step) * TILE, TILE), TILE)
            out_ref[here, there] = product[:, i * TILE:(i + 1) * TILE]

    transpose_out()
    start(remote(row_ref(0, 0), row_ref(0, 0), rx_s, rx_r, rx_peer))
    begin_row(0)
    begin_row(1)
    begin_col()
    forward("row", 2)
    to_lhs(0)
    forward("col", 2)
    forward("row", 1)
    to_lhs(-2, 2)
    forward("row", 3)
    forward("row", 4)
    to_lhs(-1, 1)
    forward("col", 1)
    arrived(col_ref(1, 0), cx_r)
    to_rhs((1, 2))
    to_lhs(-3, 3, 4)
    multiply((1, 2), 0)
    multiply((1, 2), 1)
    forward("col", 3)
    forward("col", 4)
    to_rhs((3, 4))
    multiply((3, 4), 0)
    multiply((3, 4), 1)

    for copy in pending:
        copy.wait_send()
    for local, copy in t_copies:
        @pl.when(jnp.logical_not(local))
        def _():
            copy.wait_send()


def body(frames):
    dma = pltpu.SemaphoreType.DMA
    return pl.pallas_call(
        kernel,
        out_shape=jax.ShapeDtypeStruct((1024, 512), jnp.float32),
        in_specs=[pl.BlockSpec(memory_space=pltpu.VMEM)],
        out_specs=pl.BlockSpec(memory_space=pltpu.VMEM),
        scratch_shapes=[
            pltpu.VMEM((2, 32, HALF), jnp.float32),
            pltpu.VMEM((2, 2, 8, 64, HALF), jnp.float32),
            pltpu.VMEM((8, 2, 32, FRAMES), jnp.float32),
            pltpu.VMEM((1024, 3 * FRAMES), jnp.bfloat16),
            pltpu.VMEM((2 * TILE, 3 * FRAMES), jnp.bfloat16),
            dma((2,)), dma((2,)), dma, dma, dma, dma, dma((2, 4, 2)), dma((2, 4, 2)), dma((2, 4, 2)), dma((2, 4, 2)),
            dma((8,)), dma((8,)),
        ],
        compiler_params=pltpu.CompilerParams(
            collective_id=0, has_side_effects=True, vmem_limit_bytes=40 * 1024 * 1024),
        cost_estimate=pl.CostEstimate(flops=3 * 2 * 1024 * 512 * 512, bytes_accessed=2 << 20, transcendentals=0),
    )(frames.T)


def solution(mesh):
    in_specs = (P("half", ("row", "col")),)
    out_specs = P("row", ("col", "half"))
    return jax.shard_map(body, mesh=mesh, in_specs=in_specs, out_specs=out_specs, check_vma=False)
```

```python
import jax
import jax.numpy as jnp
from jax import lax
from jax.experimental import pallas as pl
from jax.experimental.pallas import tpu as pltpu
from jax.sharding import PartitionSpec as P

MESH = pl.DeviceIdType.MESH
FRAMES = 512
HALF = FRAMES // 2
RING = 8
TILE = 128


def mod8(value):
    return lax.rem(value + 16, RING)


def split(value):
    hi = value.astype(jnp.bfloat16)
    lo = (value - hi.astype(jnp.float32)).astype(jnp.bfloat16)
    return hi, lo


def kernel(stage, out_ref, traw, rows, cols, lhs, rhs,
           t_s, t_r, rx_s, rx_r, cx_s, cx_r, rr_s, rr_r, c_s, c_r, sib_s, sib_r):
    row = lax.axis_index("row")
    col = lax.axis_index("col")
    half = lax.axis_index("half")
    y, xl = row // 2, lax.rem(row, 2)
    xh, z = col // RING, lax.rem(col, RING)
    other = 1 - half

    sibling = (row, col, other)
    rx_peer = (row, (1 - xh) * RING + z, half)
    z_peer = {n: (row, xh * RING + mod8(z + n), half) for n in (1, -1, 2, -2)}
    cx_peer = (y * 2 + 1 - xl, col, half)
    y_peer = {n: (mod8(y + n) * 2 + xl, col, half) for n in (1, -1, 2, -2)}
    diagonal = {n: (mod8(y + n) * 2 + 1 - xl, col, half) for n in (1, -1, 2, -2)}

    yy = mod8(z + lax.rem(row, RING) + 4 * xh)
    t_dest = [(yy * 2 + s, row, xh) for s in range(2)]
    t_self = [(yy * 2 + s == row) & (row == col) & (xh == half) for s in range(2)]

    def part(place):
        return mod8(place - z + 4 * half)

    t_col = RING * half + part(y)
    from_self = (row == col) & (col == t_col)

    barrier = pltpu.get_barrier_semaphore()
    for peer in (sibling, rx_peer, cx_peer, *z_peer.values(), *y_peer.values(), *diagonal.values(), (col, t_col, other)):
        pl.semaphore_signal(barrier, inc=1, device_id=peer, device_id_type=MESH)

    @pl.when(jnp.logical_not(from_self))
    def _():
        pl.semaphore_signal(barrier, inc=1, device_id=(col, t_col, half), device_id_type=MESH)

    rows[half, xh, z] = stage[...]
    pl.semaphore_wait(barrier, jnp.where(from_self, 16, 17))

    def remote(src, dst, send, recv, peer):
        return pltpu.make_async_remote_copy(
            src_ref=src, dst_ref=dst, send_sem=send, recv_sem=recv, device_id=peer, device_id_type=MESH)

    def arrived(ref, sem):
        pltpu.make_async_copy(ref, ref, sem).wait()

    pending = []

    def start(copy):
        copy.start()
        pending.append(copy)

    t_copies = []

    def transpose_out():
        for s in range(2):
            src = stage.at[pl.ds(s * 32, 32)]
            far = remote(src, traw.at[half], t_s.at[s], t_r.at[half], t_dest[s])
            near = pltpu.make_async_copy(src, traw.at[half], t_r.at[half])

            @pl.when(t_self[s])
            def _():
                near.start()

            @pl.when(jnp.logical_not(t_self[s]))
            def _():
                far.start()

            t_copies.append((t_self[s], far))

    signs = (1, -1)
    distances = (0, -1, 1, -2, 2, -3, 3, 4)

    def row_ref(u, d):
        return rows.at[half, xh if u == 0 else 1 - xh, mod8(z + d)]

    def row_pair(d, core):
        return rows.at[core, :, mod8(z + d)]

    def col_ref(u, d):
        return cols.at[part(mod8(y + d)), xl if u == 0 else 1 - xl]

    def col_pair(d):
        return cols.at[part(mod8(y + d))]

    def hop(which, direction, step, u):
        behind, ahead = ((0, 1), (0, 2), (2, 1), (2, 2))[step - 1]
        if which == "row" and u == 0:
            behind, ahead = step - 1, 1
        at = (0 if direction == 1 else 1, step - 1, u)
        d = -direction * behind
        if which == "row":
            ref = row_ref(u, d)
            return remote(ref, ref, rr_s.at[at], rr_r.at[at], z_peer[direction * ahead])
        peer = y_peer[direction * ahead]
        if step == 3:
            ref = col_pair(d)
        elif u == 1 and step < 3:
            ref, peer = col_ref(0, 0), diagonal[direction * ahead]
        else:
            ref = col_ref(u, d)
        return remote(ref, ref, c_s.at[at], c_r.at[at], peer)

    def to_sibling(d):
        slot = distances.index(d)
        start(remote(row_pair(d, half), row_pair(d, half), sib_s.at[slot], sib_r.at[slot], sibling))

    def begin_row(u):
        if u == 1:
            arrived(row_ref(1, 0), rx_r)
        for step in (1,) if u == 0 else (2, 1):
            for direction in signs:
                start(hop("row", direction, step, u))
        if u == 1:
            to_sibling(0)

    def sends(direction, step, u):
        return step < 4 or (direction == 1) == (u == 0)

    def forward_row(step, u, share=False):
        for direction in signs:
            if not sends(direction, step, u):
                continue
            d = -direction * step
            arrived(row_ref(u, d), rr_r.at[0 if direction == 1 else 1, step - 1, u])
            if u == 0:
                onward = (step + 1,) if step < 4 else ()
            else:
                onward = (4, 3) if step == 2 else ()
            for later in onward:
                if sends(direction, later, u):
                    start(hop("row", direction, later, u))
            if share and step < 4:
                to_sibling(d)
        if share and step == 4:
            to_sibling(4)

    def forward_col(step):
        for direction in signs:
            i = 0 if direction == 1 else 1
            d = -direction * step
            if step == 3:
                arrived(col_pair(d), c_r.at[i, 2, 0])
            elif step == 4:
                arrived(col_ref(i, 4), c_r.at[i, 3, i])
            else:
                for u in range(2):
                    arrived(col_ref(u, d), c_r.at[i, step - 1, u])
            if step == 2:
                start(hop("col", direction, 4, i))
                start(hop("col", direction, 3, 0))

    def to_lhs(*ds):
        for d in ds:
            arrived(row_pair(d, other), sib_r.at[distances.index(d)])
            for x in range(2):
                first, second = rows[0, x, mod8(z + d)], rows[1, x, mod8(z + d)]
                total = jnp.sum(first, axis=1, keepdims=True) + jnp.sum(second, axis=1, keepdims=True)
                mean = total / FRAMES
                here = pl.ds(pl.multiple_of(x * 512 + mod8(z + d) * 64, 64), 64)
                for j, value in enumerate((first, second)):
                    hi, lo = split(value - mean)
                    lhs[here, j * HALF:(j + 1) * HALF] = hi
                    lhs[here, FRAMES + j * HALF:FRAMES + (j + 1) * HALF] = lo
                    lhs[here, 2 * FRAMES + j * HALF:2 * FRAMES + (j + 1) * HALF] = hi

    def begin_col():
        for g in range(2):
            arrived(traw.at[g], t_r.at[g])
        first, second = traw[0], traw[1]
        total = jnp.sum(first, axis=1, keepdims=True) + jnp.sum(second, axis=1, keepdims=True)
        mean = total / FRAMES
        mine = col_ref(0, 0)
        mine[:, :HALF] = first - mean
        mine[:, HALF:] = second - mean
        for step in (2, 1):
            for u in range(2):
                for direction in (1, -1):
                    start(hop("col", direction, step, u))
        start(remote(mine, mine, cx_s, cx_r, cx_peer))

    base = part(y)
    sign = 1 - 2 * lax.rem(base, 2)

    def tile_of(step):
        return mod8(base + sign * (1, -2, 3, 4)[step - 1]) // 2

    def to_rhs(steps):
        for i, step in enumerate(steps):
            value = cols[pl.ds(2 * tile_of(step), 2)].reshape(TILE, FRAMES) * (1.0 / (FRAMES - 1))
            hi, lo = split(value)
            here = pl.ds(i * TILE, TILE)
            rhs[here, :FRAMES] = hi
            rhs[here, FRAMES:2 * FRAMES] = hi
            rhs[here, 2 * FRAMES:] = lo

    def multiply(steps, u):
        here = pl.ds(u * 512, 512)
        product = lax.dot_general(
            lhs[here, :], rhs[...], (((1,), (1,)), ((), ())), preferred_element_type=jnp.float32)
        for i, step in enumerate(steps):
            there = pl.ds(pl.multiple_of(tile_of(step) * TILE, TILE), TILE)
            out_ref[here, there] = product[:, i * TILE:(i + 1) * TILE]

    transpose_out()
    start(remote(row_ref(0, 0), row_ref(0, 0), rx_s, rx_r, rx_peer))
    begin_row(0)
    forward_row(1, 0)
    begin_row(1)
    begin_col()
    forward_row(2, 0)
    to_lhs(0)
    forward_row(2, 1, True)
    forward_col(2)
    forward_row(1, 1, True)
    forward_row(3, 0)
    to_lhs(-2, 2)
    forward_row(3, 1, True)
    to_lhs(-1, 1)
    forward_row(4, 0)
    forward_row(4, 1, True)
    forward_col(1)
    arrived(col_ref(1, 0), cx_r)
    to_rhs((1, 2))
    to_lhs(-3, 3, 4)
    multiply((1, 2), 0)
    multiply((1, 2), 1)
    forward_col(3)
    forward_col(4)
    to_rhs((3, 4))
    multiply((3, 4), 0)
    multiply((3, 4), 1)

    for copy in pending:
        copy.wait_send()
    for local, copy in t_copies:
        @pl.when(jnp.logical_not(local))
        def _():
            copy.wait_send()


def body(frames):
    dma = pltpu.SemaphoreType.DMA
    return pl.pallas_call(
        kernel,
        out_shape=jax.ShapeDtypeStruct((1024, 512), jnp.float32),
        in_specs=[pl.BlockSpec(memory_space=pltpu.VMEM)],
        out_specs=pl.BlockSpec(memory_space=pltpu.VMEM),
        scratch_shapes=[
            pltpu.VMEM((2, 32, HALF), jnp.float32),
            pltpu.VMEM((2, 2, 8, 64, HALF), jnp.float32),
            pltpu.VMEM((8, 2, 32, FRAMES), jnp.float32),
            pltpu.VMEM((1024, 3 * FRAMES), jnp.bfloat16),
            pltpu.VMEM((2 * TILE, 3 * FRAMES), jnp.bfloat16),
            dma((2,)), dma((2,)), dma, dma, dma, dma, dma((2, 4, 2)), dma((2, 4, 2)), dma((2, 4, 2)), dma((2, 4, 2)),
            dma((8,)), dma((8,)),
        ],
        compiler_params=pltpu.CompilerParams(
            collective_id=0, has_side_effects=True, vmem_limit_bytes=40 * 1024 * 1024),
        cost_estimate=pl.CostEstimate(flops=3 * 2 * 1024 * 512 * 512, bytes_accessed=2 << 20, transcendentals=0),
    )(frames.T)


def solution(mesh):
    in_specs = (P("half", ("row", "col")),)
    out_specs = P("row", ("col", "half"))
    return jax.shard_map(body, mesh=mesh, in_specs=in_specs, out_specs=out_specs, check_vma=False)
```

```python
import jax
import jax.numpy as jnp
from jax import lax
from jax.experimental import pallas as pl
from jax.experimental.pallas import tpu as pltpu
from jax.sharding import PartitionSpec as P

MESH = pl.DeviceIdType.MESH
FRAMES = 512
HALF = FRAMES // 2
RING = 8
TILE = 128


def mod8(value):
    return lax.rem(value + 16, RING)


def split(value):
    hi = value.astype(jnp.bfloat16)
    lo = (value - hi.astype(jnp.float32)).astype(jnp.bfloat16)
    return hi, lo


def kernel(stage, out_ref, traw, rows, cols, lhs, rhs,
           t_s, t_r, rx_s, rx_r, cx_s, cx_r, rr_s, rr_r, c_s, c_r, sib_s, sib_r):
    row = lax.axis_index("row")
    col = lax.axis_index("col")
    half = lax.axis_index("half")
    y, xl = row // 2, lax.rem(row, 2)
    xh, z = col // RING, lax.rem(col, RING)
    other = 1 - half

    sibling = (row, col, other)
    rx_peer = (row, (1 - xh) * RING + z, half)
    z_peer = {n: (row, xh * RING + mod8(z + n), half) for n in (1, -1, 2, -2)}
    cx_peer = (y * 2 + 1 - xl, col, half)
    y_peer = {n: (mod8(y + n) * 2 + xl, col, half) for n in (1, -1, 2, -2)}
    diagonal = {n: (mod8(y + n) * 2 + 1 - xl, col, half) for n in (1, -1, 2, -2)}

    yy = mod8(z + lax.rem(row, RING) + 4 * xh)
    t_dest = [(yy * 2 + s, row, xh) for s in range(2)]
    t_self = [(yy * 2 + s == row) & (row == col) & (xh == half) for s in range(2)]

    def part(place):
        return mod8(place - z + 4 * half)

    t_col = RING * half + part(y)
    from_self = (row == col) & (col == t_col)

    barrier = pltpu.get_barrier_semaphore()
    for peer in (sibling, rx_peer, cx_peer, *z_peer.values(), *y_peer.values(), *diagonal.values(), (col, t_col, other)):
        pl.semaphore_signal(barrier, inc=1, device_id=peer, device_id_type=MESH)

    @pl.when(jnp.logical_not(from_self))
    def _():
        pl.semaphore_signal(barrier, inc=1, device_id=(col, t_col, half), device_id_type=MESH)

    rows[half, xh, z] = stage[...]
    pl.semaphore_wait(barrier, jnp.where(from_self, 16, 17))

    def remote(src, dst, send, recv, peer):
        return pltpu.make_async_remote_copy(
            src_ref=src, dst_ref=dst, send_sem=send, recv_sem=recv, device_id=peer, device_id_type=MESH)

    def arrived(ref, sem):
        pltpu.make_async_copy(ref, ref, sem).wait()

    pending = []

    def start(copy):
        copy.start()
        pending.append(copy)

    t_copies = []

    def transpose_out():
        for s in range(2):
            src = stage.at[pl.ds(s * 32, 32)]
            far = remote(src, traw.at[half], t_s.at[s], t_r.at[half], t_dest[s])
            near = pltpu.make_async_copy(src, traw.at[half], t_r.at[half])

            @pl.when(t_self[s])
            def _():
                near.start()

            @pl.when(jnp.logical_not(t_self[s]))
            def _():
                far.start()

            t_copies.append((t_self[s], far))

    signs = (1, -1)
    distances = (0, -1, 1, -2, 2, -3, 3, 4)

    def row_ref(u, d):
        return rows.at[half, xh if u == 0 else 1 - xh, mod8(z + d)]

    def row_pair(d, core):
        return rows.at[core, :, mod8(z + d)]

    def col_ref(u, d):
        return cols.at[part(mod8(y + d)), xl if u == 0 else 1 - xl]

    def col_pair(d):
        return cols.at[part(mod8(y + d))]

    def hop(which, direction, step, u):
        behind, ahead = ((0, 1), (0, 2), (2, 1), (2, 2))[step - 1]
        at = (0 if direction == 1 else 1, step - 1, u)
        d = -direction * behind
        if which == "row":
            ref = row_pair(d, half) if step == 3 else row_ref(u, d)
            return remote(ref, ref, rr_s.at[at], rr_r.at[at], z_peer[direction * ahead])
        peer = y_peer[direction * ahead]
        if step == 3:
            ref = col_pair(d)
        elif u == 1 and step < 3:
            ref, peer = col_ref(0, 0), diagonal[direction * ahead]
        else:
            ref = col_ref(u, d)
        return remote(ref, ref, c_s.at[at], c_r.at[at], peer)

    def to_sibling(d):
        slot = distances.index(d)
        start(remote(row_pair(d, half), row_pair(d, half), sib_s.at[slot], sib_r.at[slot], sibling))

    def begin_row(u):
        if u == 1:
            arrived(row_ref(1, 0), rx_r)
        for step in (2, 1):
            for direction in signs:
                start(hop("row", direction, step, u))
        if u == 1:
            to_sibling(0)

    def come(which, direction, step):
        recv = rr_r if which == "row" else c_r
        i = 0 if direction == 1 else 1
        d = -direction * step
        if step == 3:
            arrived(row_pair(d, half) if which == "row" else col_pair(d), recv.at[i, 2, 0])
        elif step == 4:
            u = i
            arrived(row_ref(u, 4) if which == "row" else col_ref(u, 4), recv.at[i, 3, u])
        else:
            for u in range(2):
                arrived(row_ref(u, d) if which == "row" else col_ref(u, d), recv.at[i, step - 1, u])

    def forward(which, step):
        for direction in signs:
            come(which, direction, step)
            if step == 2:
                start(hop(which, direction, 4, 0 if direction == 1 else 1))
                start(hop(which, direction, 3, 0))
            if which == "row" and step < 4:
                to_sibling(-direction * step)
        if which == "row" and step == 4:
            to_sibling(4)

    def to_lhs(*ds):
        for d in ds:
            arrived(row_pair(d, other), sib_r.at[distances.index(d)])
            for x in range(2):
                first, second = rows[0, x, mod8(z + d)], rows[1, x, mod8(z + d)]
                total = jnp.sum(first, axis=1, keepdims=True) + jnp.sum(second, axis=1, keepdims=True)
                mean = total / FRAMES
                here = pl.ds((distances.index(d) * 2 + x) * 64, 64)
                for j, value in enumerate((first, second)):
                    hi, lo = split(value - mean)
                    lhs[here, j * HALF:(j + 1) * HALF] = hi
                    lhs[here, FRAMES + j * HALF:FRAMES + (j + 1) * HALF] = lo
                    lhs[here, 2 * FRAMES + j * HALF:2 * FRAMES + (j + 1) * HALF] = hi

    def begin_col():
        for g in range(2):
            arrived(traw.at[g], t_r.at[g])
        first, second = traw[0], traw[1]
        total = jnp.sum(first, axis=1, keepdims=True) + jnp.sum(second, axis=1, keepdims=True)
        mean = total / FRAMES
        mine = col_ref(0, 0)
        mine[:, :HALF] = first - mean
        mine[:, HALF:] = second - mean
        for step in (2, 1):
            for u in range(2):
                for direction in (1, -1):
                    start(hop("col", direction, step, u))
        start(remote(mine, mine, cx_s, cx_r, cx_peer))

    base = part(y)
    sign = 1 - 2 * lax.rem(base, 2)

    def tile_of(step):
        return mod8(base + sign * (1, -2, 3, 4)[step - 1]) // 2

    def to_rhs(steps):
        for step in steps:
            value = cols[pl.ds(2 * tile_of(step), 2)].reshape(TILE, FRAMES) * (1.0 / (FRAMES - 1))
            hi, lo = split(value)
            here = pl.ds((step - 1) * TILE, TILE)
            rhs[here, :FRAMES] = hi
            rhs[here, FRAMES:2 * FRAMES] = hi
            rhs[here, 2 * FRAMES:] = lo

    def multiply(ds, steps):
        first, tiles = distances.index(ds[0]) * TILE, pl.ds((steps[0] - 1) * TILE, len(steps) * TILE)
        product = lax.dot_general(
            lhs[first:first + len(ds) * TILE, :], rhs[tiles, :], (((1,), (1,)), ((), ())),
            preferred_element_type=jnp.float32)
        for m, d in enumerate(ds):
            for x in range(2):
                here = pl.ds(pl.multiple_of(x * 512 + mod8(z + d) * 64, 64), 64)
                for n, step in enumerate(steps):
                    there = pl.ds(pl.multiple_of(tile_of(step) * TILE, TILE), TILE)
                    out_ref[here, there] = product[(2 * m + x) * 64:(2 * m + x + 1) * 64, n * TILE:(n + 1) * TILE]

    transpose_out()
    start(remote(row_ref(0, 0), row_ref(0, 0), rx_s, rx_r, rx_peer))
    begin_row(0)
    begin_row(1)
    begin_col()
    forward("row", 2)
    to_lhs(0)
    forward("col", 2)
    forward("row", 1)
    to_lhs(-2, 2)
    forward("row", 3)
    forward("row", 4)
    to_lhs(-1, 1)
    forward("col", 1)
    arrived(col_ref(1, 0), cx_r)
    to_rhs((1, 2))
    multiply((0, -1, 1, -2, 2), (1, 2))
    forward("col", 3)
    forward("col", 4)
    to_rhs((3, 4))
    multiply((0, -1, 1, -2, 2), (3, 4))
    to_lhs(-3, 3, 4)
    multiply((-3, 3, 4), (1, 2))
    multiply((-3, 3, 4), (3, 4))

    for copy in pending:
        copy.wait_send()
    for local, copy in t_copies:
        @pl.when(jnp.logical_not(local))
        def _():
            copy.wait_send()


def body(frames):
    dma = pltpu.SemaphoreType.DMA
    return pl.pallas_call(
        kernel,
        out_shape=jax.ShapeDtypeStruct((1024, 512), jnp.float32),
        in_specs=[pl.BlockSpec(memory_space=pltpu.VMEM)],
        out_specs=pl.BlockSpec(memory_space=pltpu.VMEM),
        scratch_shapes=[
            pltpu.VMEM((2, 32, HALF), jnp.float32),
            pltpu.VMEM((2, 2, 8, 64, HALF), jnp.float32),
            pltpu.VMEM((8, 2, 32, FRAMES), jnp.float32),
            pltpu.VMEM((1024, 3 * FRAMES), jnp.bfloat16),
            pltpu.VMEM((4 * TILE, 3 * FRAMES), jnp.bfloat16),
            dma((2,)), dma((2,)), dma, dma, dma, dma, dma((2, 4, 2)), dma((2, 4, 2)), dma((2, 4, 2)), dma((2, 4, 2)),
            dma((8,)), dma((8,)),
        ],
        compiler_params=pltpu.CompilerParams(
            collective_id=0, has_side_effects=True, vmem_limit_bytes=40 * 1024 * 1024),
        cost_estimate=pl.CostEstimate(flops=3 * 2 * 1024 * 512 * 512, bytes_accessed=2 << 20, transcendentals=0),
    )(frames.T)


def solution(mesh):
    in_specs = (P("half", ("row", "col")),)
    out_specs = P("row", ("col", "half"))
    return jax.shard_map(body, mesh=mesh, in_specs=in_specs, out_specs=out_specs, check_vma=False)
```

```python
import jax
import jax.numpy as jnp
from jax import lax
from jax.experimental import pallas as pl
from jax.experimental.pallas import tpu as pltpu
from jax.sharding import PartitionSpec as P

MESH = pl.DeviceIdType.MESH
FRAMES = 512
HALF = FRAMES // 2
RING = 8
TILE = 128


def mod8(value):
    return lax.rem(value + 16, RING)


def split(value):
    hi = value.astype(jnp.bfloat16)
    lo = (value - hi.astype(jnp.float32)).astype(jnp.bfloat16)
    return hi, lo


def kernel(x_ref, out_ref, stage, traw, rows, cols, lhs, rhs,
           in_s, t_s, t_r, rx_s, rx_r, cx_s, cx_r, rr_s, rr_r, c_s, c_r, sib_s, sib_r):
    row = lax.axis_index("row")
    col = lax.axis_index("col")
    half = lax.axis_index("half")
    y, xl = row // 2, lax.rem(row, 2)
    xh, z = col // RING, lax.rem(col, RING)
    other = 1 - half

    fetch = pltpu.make_async_copy(x_ref, stage, in_s)
    fetch.start()

    sibling = (row, col, other)
    rx_peer = (row, (1 - xh) * RING + z, half)
    z_peer = {n: (row, xh * RING + mod8(z + n), half) for n in (1, -1, 2, -2)}
    cx_peer = (y * 2 + 1 - xl, col, half)
    y_peer = {n: (mod8(y + n) * 2 + xl, col, half) for n in (1, -1, 2, -2)}
    diagonal = {n: (mod8(y + n) * 2 + 1 - xl, col, half) for n in (1, -1, 2, -2)}

    yy = mod8(z + lax.rem(row, RING) + 4 * xh)
    t_dest = [(yy * 2 + s, row, xh) for s in range(2)]
    t_self = [(yy * 2 + s == row) & (row == col) & (xh == half) for s in range(2)]

    def part(place):
        return mod8(place - z + 4 * half)

    t_col = RING * half + part(y)
    from_self = (row == col) & (col == t_col)

    barrier = pltpu.get_barrier_semaphore()
    for peer in (sibling, rx_peer, cx_peer, *z_peer.values(), *y_peer.values(), *diagonal.values(), (col, t_col, other)):
        pl.semaphore_signal(barrier, inc=1, device_id=peer, device_id_type=MESH)

    @pl.when(jnp.logical_not(from_self))
    def _():
        pl.semaphore_signal(barrier, inc=1, device_id=(col, t_col, half), device_id_type=MESH)

    fetch.wait()
    rows[half, xh, z] = stage[...]
    pl.semaphore_wait(barrier, jnp.where(from_self, 16, 17))

    def remote(src, dst, send, recv, peer):
        return pltpu.make_async_remote_copy(
            src_ref=src, dst_ref=dst, send_sem=send, recv_sem=recv, device_id=peer, device_id_type=MESH)

    def arrived(ref, sem):
        pltpu.make_async_copy(ref, ref, sem).wait()

    pending = []

    def start(copy):
        copy.start()
        pending.append(copy)

    t_copies = []

    def transpose_out():
        for s in range(2):
            src = stage.at[pl.ds(s * 32, 32)]
            far = remote(src, traw.at[half], t_s.at[s], t_r.at[half], t_dest[s])
            near = pltpu.make_async_copy(src, traw.at[half], t_r.at[half])

            @pl.when(t_self[s])
            def _():
                near.start()

            @pl.when(jnp.logical_not(t_self[s]))
            def _():
                far.start()

            t_copies.append((t_self[s], far))

    signs = (1, -1)
    distances = (0, -1, 1, -2, 2, -3, 3, 4)

    def row_ref(u, d):
        return rows.at[half, xh if u == 0 else 1 - xh, mod8(z + d)]

    def row_pair(d, core):
        return rows.at[core, :, mod8(z + d)]

    def col_ref(u, d):
        return cols.at[part(mod8(y + d)), xl if u == 0 else 1 - xl]

    def col_pair(d):
        return cols.at[part(mod8(y + d))]

    def hop(which, direction, step, u):
        behind, ahead = ((0, 1), (0, 2), (2, 1), (2, 2))[step - 1]
        at = (0 if direction == 1 else 1, step - 1, u)
        d = -direction * behind
        if which == "row":
            ref = row_pair(d, half) if step == 3 else row_ref(u, d)
            return remote(ref, ref, rr_s.at[at], rr_r.at[at], z_peer[direction * ahead])
        peer = y_peer[direction * ahead]
        if step == 3:
            ref = col_pair(d)
        elif u == 1 and step < 3:
            ref, peer = col_ref(0, 0), diagonal[direction * ahead]
        else:
            ref = col_ref(u, d)
        return remote(ref, ref, c_s.at[at], c_r.at[at], peer)

    def to_sibling(d):
        slot = distances.index(d)
        start(remote(row_pair(d, half), row_pair(d, half), sib_s.at[slot], sib_r.at[slot], sibling))

    def begin_row(u):
        if u == 1:
            arrived(row_ref(1, 0), rx_r)
        for step in (2, 1):
            for direction in signs:
                start(hop("row", direction, step, u))
        if u == 1:
            to_sibling(0)

    def come(which, direction, step):
        recv = rr_r if which == "row" else c_r
        i = 0 if direction == 1 else 1
        d = -direction * step
        if step == 3:
            arrived(row_pair(d, half) if which == "row" else col_pair(d), recv.at[i, 2, 0])
        elif step == 4:
            u = i
            arrived(row_ref(u, 4) if which == "row" else col_ref(u, 4), recv.at[i, 3, u])
        else:
            for u in range(2):
                arrived(row_ref(u, d) if which == "row" else col_ref(u, d), recv.at[i, step - 1, u])

    def forward(which, step):
        for direction in signs:
            come(which, direction, step)
            if step == 2:
                start(hop(which, direction, 4, 0 if direction == 1 else 1))
                start(hop(which, direction, 3, 0))
            if which == "row" and step < 4:
                to_sibling(-direction * step)
        if which == "row" and step == 4:
            to_sibling(4)

    def to_lhs(*ds):
        for d in ds:
            arrived(row_pair(d, other), sib_r.at[distances.index(d)])
            for x in range(2):
                first, second = rows[0, x, mod8(z + d)], rows[1, x, mod8(z + d)]
                total = jnp.sum(first, axis=1, keepdims=True) + jnp.sum(second, axis=1, keepdims=True)
                mean = total / FRAMES
                here = pl.ds(pl.multiple_of(x * 512 + mod8(z + d) * 64, 64), 64)
                for j, value in enumerate((first, second)):
                    hi, lo = split(value - mean)
                    lhs[here, j * HALF:(j + 1) * HALF] = hi
                    lhs[here, FRAMES + j * HALF:FRAMES + (j + 1) * HALF] = lo
                    lhs[here, 2 * FRAMES + j * HALF:2 * FRAMES + (j + 1) * HALF] = hi

    def begin_col():
        for g in range(2):
            arrived(traw.at[g], t_r.at[g])
        first, second = traw[0], traw[1]
        total = jnp.sum(first, axis=1, keepdims=True) + jnp.sum(second, axis=1, keepdims=True)
        mean = total / FRAMES
        mine = col_ref(0, 0)
        mine[:, :HALF] = first - mean
        mine[:, HALF:] = second - mean
        for step in (2, 1):
            for u in range(2):
                for direction in (1, -1):
                    start(hop("col", direction, step, u))
        start(remote(mine, mine, cx_s, cx_r, cx_peer))

    base = part(y)
    sign = 1 - 2 * lax.rem(base, 2)

    def tile_of(step):
        return mod8(base + sign * (1, -2, 3, 4)[step - 1]) // 2

    def to_rhs(steps):
        for i, step in enumerate(steps):
            value = cols[pl.ds(2 * tile_of(step), 2)].reshape(TILE, FRAMES) * (1.0 / (FRAMES - 1))
            hi, lo = split(value)
            here = pl.ds(i * TILE, TILE)
            rhs[here, :FRAMES] = hi
            rhs[here, FRAMES:2 * FRAMES] = hi
            rhs[here, 2 * FRAMES:] = lo

    def multiply(steps, u):
        here = pl.ds(u * 512, 512)
        product = lax.dot_general(
            lhs[here, :], rhs[...], (((1,), (1,)), ((), ())), preferred_element_type=jnp.float32)
        for i, step in enumerate(steps):
            there = pl.ds(pl.multiple_of(tile_of(step) * TILE, TILE), TILE)
            out_ref[here, there] = product[:, i * TILE:(i + 1) * TILE]

    transpose_out()
    start(remote(row_ref(0, 0), row_ref(0, 0), rx_s, rx_r, rx_peer))
    begin_row(0)
    begin_row(1)
    begin_col()
    forward("row", 2)
    to_lhs(0)
    forward("col", 2)
    forward("row", 1)
    to_lhs(-2, 2)
    forward("row", 3)
    forward("row", 4)
    to_lhs(-1, 1)
    forward("col", 1)
    arrived(col_ref(1, 0), cx_r)
    to_rhs((1, 2))
    to_lhs(-3, 3, 4)
    multiply((1, 2), 0)
    multiply((1, 2), 1)
    forward("col", 3)
    forward("col", 4)
    to_rhs((3, 4))
    multiply((3, 4), 0)
    multiply((3, 4), 1)

    for copy in pending:
        copy.wait_send()
    for local, copy in t_copies:
        @pl.when(jnp.logical_not(local))
        def _():
            copy.wait_send()


def body(frames):
    dma = pltpu.SemaphoreType.DMA
    return pl.pallas_call(
        kernel,
        out_shape=jax.ShapeDtypeStruct((1024, 512), jnp.float32),
        in_specs=[pl.BlockSpec(memory_space=pltpu.HBM)],
        out_specs=pl.BlockSpec(memory_space=pltpu.VMEM),
        scratch_shapes=[
            pltpu.VMEM((64, HALF), jnp.float32),
            pltpu.VMEM((2, 32, HALF), jnp.float32),
            pltpu.VMEM((2, 2, 8, 64, HALF), jnp.float32),
            pltpu.VMEM((8, 2, 32, FRAMES), jnp.float32),
            pltpu.VMEM((1024, 3 * FRAMES), jnp.bfloat16),
            pltpu.VMEM((2 * TILE, 3 * FRAMES), jnp.bfloat16),
            dma, dma((2,)), dma((2,)), dma, dma, dma, dma, dma((2, 4, 2)), dma((2, 4, 2)), dma((2, 4, 2)), dma((2, 4, 2)),
            dma((8,)), dma((8,)),
        ],
        compiler_params=pltpu.CompilerParams(
            collective_id=0, has_side_effects=True, vmem_limit_bytes=40 * 1024 * 1024),
        cost_estimate=pl.CostEstimate(flops=3 * 2 * 1024 * 512 * 512, bytes_accessed=2 << 20, transcendentals=0),
    )(pltpu.with_memory_space_constraint(frames.T, pltpu.HBM))


def solution(mesh):
    in_specs = (P("half", ("row", "col")),)
    out_specs = P("row", ("col", "half"))
    return jax.shard_map(body, mesh=mesh, in_specs=in_specs, out_specs=out_specs, check_vma=False)
```

```python
import jax
import jax.numpy as jnp
from jax import lax
from jax.experimental import pallas as pl
from jax.experimental.pallas import tpu as pltpu
from jax.sharding import PartitionSpec as P

MESH = pl.DeviceIdType.MESH
FRAMES = 512
HALF = FRAMES // 2
RING = 8
TILE = 128


def mod8(value):
    return lax.rem(value + 16, RING)


def split(value):
    hi = value.astype(jnp.bfloat16)
    lo = (value - hi.astype(jnp.float32)).astype(jnp.bfloat16)
    return hi, lo


def kernel(x_ref, out_ref, stage, traw, rows, cols, lhs, rhs,
           in_s, t_s, t_r, rx_s, rx_r, cx_s, cx_r, rr_s, rr_r, c_s, c_r, sib_s, sib_r):
    row = lax.axis_index("row")
    col = lax.axis_index("col")
    half = lax.axis_index("half")
    y, xl = row // 2, lax.rem(row, 2)
    xh, z = col // RING, lax.rem(col, RING)
    other = 1 - half

    fetch = pltpu.make_async_copy(x_ref, stage, in_s)
    fetch.start()

    sibling = (row, col, other)
    rx_peer = (row, (1 - xh) * RING + z, half)
    z_peer = {n: (row, xh * RING + mod8(z + n), half) for n in (1, -1, 2, -2)}
    cx_peer = (y * 2 + 1 - xl, col, half)
    y_peer = {n: (mod8(y + n) * 2 + xl, col, half) for n in (1, -1, 2, -2)}
    diagonal = {n: (mod8(y + n) * 2 + 1 - xl, col, half) for n in (1, -1, 2, -2)}

    yy = mod8(z + lax.rem(row, RING) + 4 * xh)
    t_dest = [(yy * 2 + s, row, xh) for s in range(2)]
    t_self = [(yy * 2 + s == row) & (row == col) & (xh == half) for s in range(2)]

    def part(place):
        return mod8(place - z + 4 * half)

    t_col = RING * half + part(y)
    from_self = (row == col) & (col == t_col)

    barrier = pltpu.get_barrier_semaphore()
    for peer in (sibling, rx_peer, cx_peer, *z_peer.values(), *y_peer.values(), *diagonal.values(), (col, t_col, other)):
        pl.semaphore_signal(barrier, inc=1, device_id=peer, device_id_type=MESH)

    @pl.when(jnp.logical_not(from_self))
    def _():
        pl.semaphore_signal(barrier, inc=1, device_id=(col, t_col, half), device_id_type=MESH)

    fetch.wait()
    rows[half, xh, z] = stage[...]
    pl.semaphore_wait(barrier, jnp.where(from_self, 16, 17))

    def remote(src, dst, send, recv, peer):
        return pltpu.make_async_remote_copy(
            src_ref=src, dst_ref=dst, send_sem=send, recv_sem=recv, device_id=peer, device_id_type=MESH)

    def arrived(ref, sem):
        pltpu.make_async_copy(ref, ref, sem).wait()

    pending = []

    def start(copy):
        copy.start()
        pending.append(copy)

    t_copies = []

    def transpose_out():
        for s in range(2):
            src = stage.at[pl.ds(s * 32, 32)]
            far = remote(src, traw.at[half], t_s.at[s], t_r.at[half], t_dest[s])
            near = pltpu.make_async_copy(src, traw.at[half], t_r.at[half])

            @pl.when(t_self[s])
            def _():
                near.start()

            @pl.when(jnp.logical_not(t_self[s]))
            def _():
                far.start()

            t_copies.append((t_self[s], far))

    signs = (1, -1)
    distances = (0, -1, 1, -2, 2, -3, 3, 4)

    def row_ref(u, d):
        return rows.at[half, xh if u == 0 else 1 - xh, mod8(z + d)]

    def row_pair(d, core):
        return rows.at[core, :, mod8(z + d)]

    def col_ref(u, d):
        return cols.at[part(mod8(y + d)), xl if u == 0 else 1 - xl]

    def col_pair(d):
        return cols.at[part(mod8(y + d))]

    def hop(which, direction, step, u):
        behind, ahead = ((0, 1), (0, 2), (2, 1), (2, 2))[step - 1]
        at = (0 if direction == 1 else 1, step - 1, u)
        d = -direction * behind
        if which == "row":
            ref = row_pair(d, half) if step in (2, 3) else row_ref(u, d)
            return remote(ref, ref, rr_s.at[at], rr_r.at[at], z_peer[direction * ahead])
        peer = y_peer[direction * ahead]
        if step == 3:
            ref = col_pair(d)
        elif u == 1 and step < 3:
            ref, peer = col_ref(0, 0), diagonal[direction * ahead]
        else:
            ref = col_ref(u, d)
        return remote(ref, ref, c_s.at[at], c_r.at[at], peer)

    def to_sibling(d):
        slot = distances.index(d)
        start(remote(row_pair(d, half), row_pair(d, half), sib_s.at[slot], sib_r.at[slot], sibling))

    def begin_row(u):
        if u == 1:
            arrived(row_ref(1, 0), rx_r)
        for step in (1,) if u == 0 else (2, 1):
            for direction in signs:
                start(hop("row", direction, step, 0 if step == 2 else u))
        if u == 1:
            to_sibling(0)

    def come(which, direction, step):
        recv = rr_r if which == "row" else c_r
        i = 0 if direction == 1 else 1
        d = -direction * step
        if step == 3 or (which == "row" and step == 2):
            arrived(row_pair(d, half) if which == "row" else col_pair(d), recv.at[i, step - 1, 0])
        elif step == 4:
            u = i
            arrived(row_ref(u, 4) if which == "row" else col_ref(u, 4), recv.at[i, 3, u])
        else:
            for u in range(2):
                arrived(row_ref(u, d) if which == "row" else col_ref(u, d), recv.at[i, step - 1, u])

    def forward(which, step):
        for direction in signs:
            come(which, direction, step)
            if step == 2:
                start(hop(which, direction, 4, 0 if direction == 1 else 1))
                start(hop(which, direction, 3, 0))
            if which == "row" and step < 4:
                to_sibling(-direction * step)
        if which == "row" and step == 4:
            to_sibling(4)

    def to_lhs(*ds):
        for d in ds:
            arrived(row_pair(d, other), sib_r.at[distances.index(d)])
            for x in range(2):
                first, second = rows[0, x, mod8(z + d)], rows[1, x, mod8(z + d)]
                total = jnp.sum(first, axis=1, keepdims=True) + jnp.sum(second, axis=1, keepdims=True)
                mean = total / FRAMES
                here = pl.ds(pl.multiple_of(x * 512 + mod8(z + d) * 64, 64), 64)
                for j, value in enumerate((first, second)):
                    hi, lo = split(value - mean)
                    lhs[here, j * HALF:(j + 1) * HALF] = hi
                    lhs[here, FRAMES + j * HALF:FRAMES + (j + 1) * HALF] = lo
                    lhs[here, 2 * FRAMES + j * HALF:2 * FRAMES + (j + 1) * HALF] = hi

    def begin_col():
        for g in range(2):
            arrived(traw.at[g], t_r.at[g])
        first, second = traw[0], traw[1]
        total = jnp.sum(first, axis=1, keepdims=True) + jnp.sum(second, axis=1, keepdims=True)
        mean = total / FRAMES
        mine = col_ref(0, 0)
        mine[:, :HALF] = first - mean
        mine[:, HALF:] = second - mean
        for step in (2, 1):
            for u in range(2):
                for direction in (1, -1):
                    start(hop("col", direction, step, u))
        start(remote(mine, mine, cx_s, cx_r, cx_peer))

    base = part(y)
    sign = 1 - 2 * lax.rem(base, 2)

    def tile_of(step):
        return mod8(base + sign * (1, -2, 3, 4)[step - 1]) // 2

    def to_rhs(steps):
        for i, step in enumerate(steps):
            value = cols[pl.ds(2 * tile_of(step), 2)].reshape(TILE, FRAMES) * (1.0 / (FRAMES - 1))
            hi, lo = split(value)
            here = pl.ds(i * TILE, TILE)
            rhs[here, :FRAMES] = hi
            rhs[here, FRAMES:2 * FRAMES] = hi
            rhs[here, 2 * FRAMES:] = lo

    def multiply(steps, u):
        here = pl.ds(u * 512, 512)
        product = lax.dot_general(
            lhs[here, :], rhs[...], (((1,), (1,)), ((), ())), preferred_element_type=jnp.float32)
        for i, step in enumerate(steps):
            there = pl.ds(pl.multiple_of(tile_of(step) * TILE, TILE), TILE)
            out_ref[here, there] = product[:, i * TILE:(i + 1) * TILE]

    transpose_out()
    start(remote(row_ref(0, 0), row_ref(0, 0), rx_s, rx_r, rx_peer))
    begin_row(0)
    begin_row(1)
    begin_col()
    forward("row", 2)
    to_lhs(0)
    forward("col", 2)
    forward("row", 1)
    to_lhs(-2, 2)
    forward("row", 3)
    forward("row", 4)
    to_lhs(-1, 1)
    forward("col", 1)
    arrived(col_ref(1, 0), cx_r)
    to_rhs((1, 2))
    to_lhs(-3, 3, 4)
    multiply((1, 2), 0)
    multiply((1, 2), 1)
    forward("col", 3)
    forward("col", 4)
    to_rhs((3, 4))
    multiply((3, 4), 0)
    multiply((3, 4), 1)

    for copy in pending:
        copy.wait_send()
    for local, copy in t_copies:
        @pl.when(jnp.logical_not(local))
        def _():
            copy.wait_send()


def body(frames):
    dma = pltpu.SemaphoreType.DMA
    return pl.pallas_call(
        kernel,
        out_shape=jax.ShapeDtypeStruct((1024, 512), jnp.float32),
        in_specs=[pl.BlockSpec(memory_space=pltpu.HBM)],
        out_specs=pl.BlockSpec(memory_space=pltpu.VMEM),
        scratch_shapes=[
            pltpu.VMEM((64, HALF), jnp.float32),
            pltpu.VMEM((2, 32, HALF), jnp.float32),
            pltpu.VMEM((2, 2, 8, 64, HALF), jnp.float32),
            pltpu.VMEM((8, 2, 32, FRAMES), jnp.float32),
            pltpu.VMEM((1024, 3 * FRAMES), jnp.bfloat16),
            pltpu.VMEM((2 * TILE, 3 * FRAMES), jnp.bfloat16),
            dma, dma((2,)), dma((2,)), dma, dma, dma, dma, dma((2, 4, 2)), dma((2, 4, 2)), dma((2, 4, 2)), dma((2, 4, 2)),
            dma((8,)), dma((8,)),
        ],
        compiler_params=pltpu.CompilerParams(
            collective_id=0, has_side_effects=True, vmem_limit_bytes=40 * 1024 * 1024),
        cost_estimate=pl.CostEstimate(flops=3 * 2 * 1024 * 512 * 512, bytes_accessed=2 << 20, transcendentals=0),
    )(pltpu.with_memory_space_constraint(frames.T, pltpu.HBM))


def solution(mesh):
    in_specs = (P("half", ("row", "col")),)
    out_specs = P("row", ("col", "half"))
    return jax.shard_map(body, mesh=mesh, in_specs=in_specs, out_specs=out_specs, check_vma=False)
```

```python
import jax
import jax.numpy as jnp
from jax import lax
from jax.experimental import pallas as pl
from jax.experimental.pallas import tpu as pltpu
from jax.sharding import PartitionSpec as P

MESH = pl.DeviceIdType.MESH
FRAMES = 512
HALF = FRAMES // 2
RING = 8
TILE = 128


def mod8(value):
    return lax.rem(value + 16, RING)


def split(value):
    hi = value.astype(jnp.bfloat16)
    lo = (value - hi.astype(jnp.float32)).astype(jnp.bfloat16)
    return hi, lo


def kernel(x_ref, out_ref, stage, traw, rows, cols, lhs, rhs,
           in_s, t_s, t_r, rx_s, rx_r, cx_s, cx_r, rr_s, rr_r, c_s, c_r, sib_s, sib_r):
    row = lax.axis_index("row")
    col = lax.axis_index("col")
    half = lax.axis_index("half")
    y, xl = row // 2, lax.rem(row, 2)
    xh, z = col // RING, lax.rem(col, RING)
    other = 1 - half

    fetch = pltpu.make_async_copy(x_ref, stage, in_s)
    fetch.start()

    sibling = (row, col, other)
    rx_peer = (row, (1 - xh) * RING + z, half)
    z_peer = {n: (row, xh * RING + mod8(z + n), half) for n in (1, -1, 2, -2)}
    cx_peer = (y * 2 + 1 - xl, col, half)
    y_peer = {n: (mod8(y + n) * 2 + xl, col, half) for n in (1, -1, 2, -2)}
    diagonal = {n: (mod8(y + n) * 2 + 1 - xl, col, half) for n in (1, -1, 2, -2)}

    yy = mod8(z + lax.rem(row, RING) + 4 * xh)
    t_dest = [(yy * 2 + s, row, xh) for s in range(2)]
    t_self = [(yy * 2 + s == row) & (row == col) & (xh == half) for s in range(2)]

    def part(place):
        return mod8(place - z + 4 * half)

    t_col = RING * half + part(y)
    from_self = (row == col) & (col == t_col)

    barrier = pltpu.get_barrier_semaphore()
    for peer in (sibling, rx_peer, cx_peer, *z_peer.values(), *y_peer.values(), *diagonal.values(), (col, t_col, other)):
        pl.semaphore_signal(barrier, inc=1, device_id=peer, device_id_type=MESH)

    @pl.when(jnp.logical_not(from_self))
    def _():
        pl.semaphore_signal(barrier, inc=1, device_id=(col, t_col, half), device_id_type=MESH)

    fetch.wait()
    rows[half, xh, z] = stage[...]
    pl.semaphore_wait(barrier, jnp.where(from_self, 16, 17))

    def remote(src, dst, send, recv, peer):
        return pltpu.make_async_remote_copy(
            src_ref=src, dst_ref=dst, send_sem=send, recv_sem=recv, device_id=peer, device_id_type=MESH)

    def arrived(ref, sem):
        pltpu.make_async_copy(ref, ref, sem).wait()

    pending = []

    def start(copy):
        copy.start()
        pending.append(copy)

    t_copies = []

    def transpose_out():
        for s in range(2):
            src = stage.at[pl.ds(s * 32, 32)]
            far = remote(src, traw.at[half], t_s.at[s], t_r.at[half], t_dest[s])
            near = pltpu.make_async_copy(src, traw.at[half], t_r.at[half])

            @pl.when(t_self[s])
            def _():
                near.start()

            @pl.when(jnp.logical_not(t_self[s]))
            def _():
                far.start()

            t_copies.append((t_self[s], far))

    signs = (1, -1)
    distances = (0, -1, 1, -2, 2, -3, 3, 4)

    def row_ref(u, d):
        return rows.at[half, xh if u == 0 else 1 - xh, mod8(z + d)]

    def row_pair(d, core):
        return rows.at[core, :, mod8(z + d)]

    def col_ref(u, d):
        return cols.at[part(mod8(y + d)), xl if u == 0 else 1 - xl]

    def col_pair(d):
        return cols.at[part(mod8(y + d))]

    def hop(which, direction, step, u):
        behind, ahead = ((0, 1), (0, 2), (2, 1), (2, 2))[step - 1]
        at = (0 if direction == 1 else 1, step - 1, u)
        d = -direction * behind
        if which == "row":
            ref = row_ref(u, d)
            return remote(ref, ref, rr_s.at[at], rr_r.at[at], z_peer[direction * ahead])
        peer = y_peer[direction * ahead]
        if step == 3:
            ref = col_pair(d)
        elif u == 1 and step < 3:
            ref, peer = col_ref(0, 0), diagonal[direction * ahead]
        else:
            ref = col_ref(u, d)
        return remote(ref, ref, c_s.at[at], c_r.at[at], peer)

    def to_sibling(d):
        slot = distances.index(d)
        start(remote(row_pair(d, half), row_pair(d, half), sib_s.at[slot], sib_r.at[slot], sibling))

    def begin_row(u):
        if u == 1:
            arrived(row_ref(1, 0), rx_r)
        for step in (2, 1):
            for direction in signs:
                start(hop("row", direction, step, u))
        if u == 1:
            to_sibling(0)

    def come_row(direction, step, u):
        i = 0 if direction == 1 else 1
        arrived(row_ref(u, -direction * step), rr_r.at[i, step - 1, u])

    def pass_rows(u):
        for direction in signs:
            come_row(direction, 2, u)
            if (direction == 1) == (u == 0):
                start(hop("row", direction, 4, u))
            start(hop("row", direction, 3, u))

    def share_rows(step):
        for direction in signs:
            if step != 2:
                for u in range(2):
                    if step < 4 or (direction == 1) == (u == 0):
                        come_row(direction, step, u)
            if step < 4:
                to_sibling(-direction * step)
        if step == 4:
            to_sibling(4)

    def come_col(step):
        for direction in signs:
            i = 0 if direction == 1 else 1
            d = -direction * step
            if step == 3:
                arrived(col_pair(d), c_r.at[i, 2, 0])
            elif step == 4:
                arrived(col_ref(i, 4), c_r.at[i, 3, i])
            else:
                for u in range(2):
                    arrived(col_ref(u, d), c_r.at[i, step - 1, u])
            if step == 2:
                start(hop("col", direction, 4, i))
                start(hop("col", direction, 3, 0))

    def to_lhs(*ds):
        for d in ds:
            arrived(row_pair(d, other), sib_r.at[distances.index(d)])
            for x in range(2):
                first, second = rows[0, x, mod8(z + d)], rows[1, x, mod8(z + d)]
                total = jnp.sum(first, axis=1, keepdims=True) + jnp.sum(second, axis=1, keepdims=True)
                mean = total / FRAMES
                here = pl.ds(pl.multiple_of(x * 512 + mod8(z + d) * 64, 64), 64)
                for j, value in enumerate((first, second)):
                    hi, lo = split(value - mean)
                    lhs[here, j * HALF:(j + 1) * HALF] = hi
                    lhs[here, FRAMES + j * HALF:FRAMES + (j + 1) * HALF] = lo
                    lhs[here, 2 * FRAMES + j * HALF:2 * FRAMES + (j + 1) * HALF] = hi

    def begin_col():
        for g in range(2):
            arrived(traw.at[g], t_r.at[g])
        first, second = traw[0], traw[1]
        total = jnp.sum(first, axis=1, keepdims=True) + jnp.sum(second, axis=1, keepdims=True)
        mean = total / FRAMES
        mine = col_ref(0, 0)
        mine[:, :HALF] = first - mean
        mine[:, HALF:] = second - mean
        for step in (2, 1):
            for u in range(2):
                for direction in (1, -1):
                    start(hop("col", direction, step, u))
        start(remote(mine, mine, cx_s, cx_r, cx_peer))

    base = part(y)
    sign = 1 - 2 * lax.rem(base, 2)

    def tile_of(step):
        return mod8(base + sign * (1, -2, 3, 4)[step - 1]) // 2

    def to_rhs(steps):
        for i, step in enumerate(steps):
            value = cols[pl.ds(2 * tile_of(step), 2)].reshape(TILE, FRAMES) * (1.0 / (FRAMES - 1))
            hi, lo = split(value)
            here = pl.ds(i * TILE, TILE)
            rhs[here, :FRAMES] = hi
            rhs[here, FRAMES:2 * FRAMES] = hi
            rhs[here, 2 * FRAMES:] = lo

    def multiply(steps, u):
        here = pl.ds(u * 512, 512)
        product = lax.dot_general(
            lhs[here, :], rhs[...], (((1,), (1,)), ((), ())), preferred_element_type=jnp.float32)
        for i, step in enumerate(steps):
            there = pl.ds(pl.multiple_of(tile_of(step) * TILE, TILE), TILE)
            out_ref[here, there] = product[:, i * TILE:(i + 1) * TILE]

    transpose_out()
    start(remote(row_ref(0, 0), row_ref(0, 0), rx_s, rx_r, rx_peer))
    begin_row(0)
    begin_row(1)
    begin_col()
    pass_rows(0)
    come_col(2)
    pass_rows(1)
    share_rows(2)
    share_rows(1)
    to_lhs(0)
    to_lhs(-2, 2)
    share_rows(3)
    share_rows(4)
    to_lhs(-1, 1)
    come_col(1)
    arrived(col_ref(1, 0), cx_r)
    to_rhs((1, 2))
    to_lhs(-3, 3, 4)
    multiply((1, 2), 0)
    multiply((1, 2), 1)
    come_col(3)
    come_col(4)
    to_rhs((3, 4))
    multiply((3, 4), 0)
    multiply((3, 4), 1)

    for copy in pending:
        copy.wait_send()
    for local, copy in t_copies:
        @pl.when(jnp.logical_not(local))
        def _():
            copy.wait_send()


def body(frames):
    dma = pltpu.SemaphoreType.DMA
    return pl.pallas_call(
        kernel,
        out_shape=jax.ShapeDtypeStruct((1024, 512), jnp.float32),
        in_specs=[pl.BlockSpec(memory_space=pltpu.HBM)],
        out_specs=pl.BlockSpec(memory_space=pltpu.VMEM),
        scratch_shapes=[
            pltpu.VMEM((64, HALF), jnp.float32),
            pltpu.VMEM((2, 32, HALF), jnp.float32),
            pltpu.VMEM((2, 2, 8, 64, HALF), jnp.float32),
            pltpu.VMEM((8, 2, 32, FRAMES), jnp.float32),
            pltpu.VMEM((1024, 3 * FRAMES), jnp.bfloat16),
            pltpu.VMEM((2 * TILE, 3 * FRAMES), jnp.bfloat16),
            dma, dma((2,)), dma((2,)), dma, dma, dma, dma, dma((2, 4, 2)), dma((2, 4, 2)), dma((2, 4, 2)), dma((2, 4, 2)),
            dma((8,)), dma((8,)),
        ],
        compiler_params=pltpu.CompilerParams(
            collective_id=0, has_side_effects=True, vmem_limit_bytes=40 * 1024 * 1024),
        cost_estimate=pl.CostEstimate(flops=3 * 2 * 1024 * 512 * 512, bytes_accessed=2 << 20, transcendentals=0),
    )(pltpu.with_memory_space_constraint(frames.T, pltpu.HBM))


def solution(mesh):
    in_specs = (P("half", ("row", "col")),)
    out_specs = P("row", ("col", "half"))
    return jax.shard_map(body, mesh=mesh, in_specs=in_specs, out_specs=out_specs, check_vma=False)
```

```python
import jax
import jax.numpy as jnp
from jax import lax
from jax.experimental import pallas as pl
from jax.experimental.pallas import tpu as pltpu
from jax.sharding import PartitionSpec as P

MESH = pl.DeviceIdType.MESH
FRAMES = 512
HALF = FRAMES // 2
RING = 8
TILE = 128


def mod8(value):
    return lax.rem(value + 16, RING)


def split(value):
    hi = value.astype(jnp.bfloat16)
    lo = (value - hi.astype(jnp.float32)).astype(jnp.bfloat16)
    return hi, lo


def kernel(x_ref, out_ref, stage, traw, rows, cols, lhs, rhs,
           in_s, t_s, t_r, rx_s, rx_r, cx_s, cx_r, rr_s, rr_r, c_s, c_r, sib_s, sib_r):
    row = lax.axis_index("row")
    col = lax.axis_index("col")
    half = lax.axis_index("half")
    y, xl = row // 2, lax.rem(row, 2)
    xh, z = col // RING, lax.rem(col, RING)
    other = 1 - half

    fetch = pltpu.make_async_copy(x_ref, stage, in_s)
    fetch.start()

    sibling = (row, col, other)
    rx_peer = (row, (1 - xh) * RING + z, half)
    z_peer = {n: (row, xh * RING + mod8(z + n), half) for n in (1, -1, 2, -2)}
    cx_peer = (y * 2 + 1 - xl, col, half)
    y_peer = {n: (mod8(y + n) * 2 + xl, col, half) for n in (1, -1, 2, -2)}
    diagonal = {n: (mod8(y + n) * 2 + 1 - xl, col, half) for n in (1, -1, 2, -2)}

    yy = mod8(z + lax.rem(row, RING) + 4 * xh)
    t_dest = [(yy * 2 + s, row, xh) for s in range(2)]
    t_self = [(yy * 2 + s == row) & (row == col) & (xh == half) for s in range(2)]

    def part(place):
        return mod8(place - z + 4 * half)

    t_col = RING * half + part(y)
    from_self = (row == col) & (col == t_col)

    barrier = pltpu.get_barrier_semaphore()
    for peer in (sibling, rx_peer, cx_peer, *z_peer.values(), *y_peer.values(), *diagonal.values(), (col, t_col, other)):
        pl.semaphore_signal(barrier, inc=1, device_id=peer, device_id_type=MESH)

    @pl.when(jnp.logical_not(from_self))
    def _():
        pl.semaphore_signal(barrier, inc=1, device_id=(col, t_col, half), device_id_type=MESH)

    fetch.wait()
    rows[half, xh, z] = stage[...]
    pl.semaphore_wait(barrier, jnp.where(from_self, 16, 17))

    def remote(src, dst, send, recv, peer):
        return pltpu.make_async_remote_copy(
            src_ref=src, dst_ref=dst, send_sem=send, recv_sem=recv, device_id=peer, device_id_type=MESH)

    def arrived(ref, sem):
        pltpu.make_async_copy(ref, ref, sem).wait()

    pending = []

    def start(copy):
        copy.start()
        pending.append(copy)

    t_copies = []

    def transpose_out():
        for s in range(2):
            src = stage.at[pl.ds(s * 32, 32)]
            far = remote(src, traw.at[half], t_s.at[s], t_r.at[half], t_dest[s])
            near = pltpu.make_async_copy(src, traw.at[half], t_r.at[half])

            @pl.when(t_self[s])
            def _():
                near.start()

            @pl.when(jnp.logical_not(t_self[s]))
            def _():
                far.start()

            t_copies.append((t_self[s], far))

    signs = (1, -1)
    distances = (0, -1, 1, -2, 2, -3, 3, 4)

    def row_ref(u, d):
        return rows.at[half, xh if u == 0 else 1 - xh, mod8(z + d)]

    def row_pair(d, core):
        return rows.at[core, :, mod8(z + d)]

    def col_ref(u, d):
        return cols.at[part(mod8(y + d)), xl if u == 0 else 1 - xl]

    def col_pair(d):
        return cols.at[part(mod8(y + d))]

    def hop(which, direction, step, u):
        behind, ahead = ((0, 1), (0, 2), (2, 1), (2, 2))[step - 1]
        at = (0 if direction == 1 else 1, step - 1, u)
        d = -direction * behind
        if which == "row":
            ref = row_ref(u, d)
            return remote(ref, ref, rr_s.at[at], rr_r.at[at], z_peer[direction * ahead])
        peer = y_peer[direction * ahead]
        if step == 3:
            ref = col_pair(d)
        elif u == 1 and step < 3:
            ref, peer = col_ref(0, 0), diagonal[direction * ahead]
        else:
            ref = col_ref(u, d)
        return remote(ref, ref, c_s.at[at], c_r.at[at], peer)

    def to_sibling(d):
        slot = distances.index(d)
        start(remote(row_pair(d, half), row_pair(d, half), sib_s.at[slot], sib_r.at[slot], sibling))

    def begin_row(u):
        if u == 1:
            arrived(row_ref(1, 0), rx_r)
        for step in (2, 1):
            for direction in signs:
                start(hop("row", direction, step, u))
        if u == 1:
            to_sibling(0)

    def come_row(direction, step, u):
        i = 0 if direction == 1 else 1
        arrived(row_ref(u, -direction * step), rr_r.at[i, step - 1, u])

    def pass_rows(u):
        for direction in signs:
            come_row(direction, 2, u)
            if (direction == 1) == (u == 0):
                start(hop("row", direction, 4, u))
            start(hop("row", direction, 3, u))

    def share_rows(step):
        for direction in signs:
            if step != 2:
                for u in range(2):
                    if step < 4 or (direction == 1) == (u == 0):
                        come_row(direction, step, u)
            if step < 4:
                to_sibling(-direction * step)
        if step == 4:
            to_sibling(4)

    def come_col(step):
        for direction in signs:
            i = 0 if direction == 1 else 1
            d = -direction * step
            if step == 3:
                arrived(col_pair(d), c_r.at[i, 2, 0])
            elif step == 4:
                arrived(col_ref(i, 4), c_r.at[i, 3, i])
            else:
                for u in range(2):
                    arrived(col_ref(u, d), c_r.at[i, step - 1, u])
            if step == 2:
                start(hop("col", direction, 4, i))
                start(hop("col", direction, 3, 0))

    def to_lhs(*ds):
        for d in ds:
            arrived(row_pair(d, other), sib_r.at[distances.index(d)])
            for x in range(2):
                first, second = rows[0, x, mod8(z + d)], rows[1, x, mod8(z + d)]
                total = jnp.sum(first, axis=1, keepdims=True) + jnp.sum(second, axis=1, keepdims=True)
                mean = total / FRAMES
                here = pl.ds(pl.multiple_of(x * 512 + mod8(z + d) * 64, 64), 64)
                for j, value in enumerate((first, second)):
                    hi, lo = split(value - mean)
                    lhs[here, j * HALF:(j + 1) * HALF] = hi
                    lhs[here, FRAMES + j * HALF:FRAMES + (j + 1) * HALF] = lo
                    lhs[here, 2 * FRAMES + j * HALF:2 * FRAMES + (j + 1) * HALF] = hi

    def begin_col():
        for g in range(2):
            arrived(traw.at[g], t_r.at[g])
        first, second = traw[0], traw[1]
        total = jnp.sum(first, axis=1, keepdims=True) + jnp.sum(second, axis=1, keepdims=True)
        mean = total / FRAMES
        mine = col_ref(0, 0)
        mine[:, :HALF] = first - mean
        mine[:, HALF:] = second - mean
        for step in (2, 1):
            for u in range(2):
                for direction in (1, -1):
                    start(hop("col", direction, step, u))
        start(remote(mine, mine, cx_s, cx_r, cx_peer))

    base = part(y)
    sign = 1 - 2 * lax.rem(base, 2)

    def tile_of(step):
        return mod8(base + sign * (1, -2, 3, 4)[step - 1]) // 2

    def to_rhs(steps):
        for i, step in enumerate(steps):
            value = cols[pl.ds(2 * tile_of(step), 2)].reshape(TILE, FRAMES) * (1.0 / (FRAMES - 1))
            hi, lo = split(value)
            here = pl.ds(i * TILE, TILE)
            rhs[here, :FRAMES] = hi
            rhs[here, FRAMES:2 * FRAMES] = hi
            rhs[here, 2 * FRAMES:] = lo

    def multiply(steps, u):
        here = pl.ds(u * 512, 512)
        product = lax.dot_general(
            lhs[here, :], rhs[...], (((1,), (1,)), ((), ())), preferred_element_type=jnp.float32)
        for i, step in enumerate(steps):
            there = pl.ds(pl.multiple_of(tile_of(step) * TILE, TILE), TILE)
            out_ref[here, there] = product[:, i * TILE:(i + 1) * TILE]

    transpose_out()
    start(remote(row_ref(0, 0), row_ref(0, 0), rx_s, rx_r, rx_peer))
    begin_row(0)
    begin_row(1)
    pass_rows(0)
    begin_col()
    pass_rows(1)
    share_rows(2)
    share_rows(1)
    to_lhs(0)
    come_col(2)
    to_lhs(-2, 2)
    share_rows(3)
    share_rows(4)
    to_lhs(-1, 1)
    come_col(1)
    arrived(col_ref(1, 0), cx_r)
    to_rhs((1, 2))
    to_lhs(-3, 3, 4)
    multiply((1, 2), 0)
    multiply((1, 2), 1)
    come_col(3)
    come_col(4)
    to_rhs((3, 4))
    multiply((3, 4), 0)
    multiply((3, 4), 1)

    for copy in pending:
        copy.wait_send()
    for local, copy in t_copies:
        @pl.when(jnp.logical_not(local))
        def _():
            copy.wait_send()


def body(frames):
    dma = pltpu.SemaphoreType.DMA
    return pl.pallas_call(
        kernel,
        out_shape=jax.ShapeDtypeStruct((1024, 512), jnp.float32),
        in_specs=[pl.BlockSpec(memory_space=pltpu.HBM)],
        out_specs=pl.BlockSpec(memory_space=pltpu.VMEM),
        scratch_shapes=[
            pltpu.VMEM((64, HALF), jnp.float32),
            pltpu.VMEM((2, 32, HALF), jnp.float32),
            pltpu.VMEM((2, 2, 8, 64, HALF), jnp.float32),
            pltpu.VMEM((8, 2, 32, FRAMES), jnp.float32),
            pltpu.VMEM((1024, 3 * FRAMES), jnp.bfloat16),
            pltpu.VMEM((2 * TILE, 3 * FRAMES), jnp.bfloat16),
            dma, dma((2,)), dma((2,)), dma, dma, dma, dma, dma((2, 4, 2)), dma((2, 4, 2)), dma((2, 4, 2)), dma((2, 4, 2)),
            dma((8,)), dma((8,)),
        ],
        compiler_params=pltpu.CompilerParams(
            collective_id=0, has_side_effects=True, vmem_limit_bytes=40 * 1024 * 1024),
        cost_estimate=pl.CostEstimate(flops=3 * 2 * 1024 * 512 * 512, bytes_accessed=2 << 20, transcendentals=0),
    )(pltpu.with_memory_space_constraint(frames.T, pltpu.HBM))


def solution(mesh):
    in_specs = (P("half", ("row", "col")),)
    out_specs = P("row", ("col", "half"))
    return jax.shard_map(body, mesh=mesh, in_specs=in_specs, out_specs=out_specs, check_vma=False)
```

```python
import jax
import jax.numpy as jnp
from jax import lax
from jax.experimental import pallas as pl
from jax.experimental.pallas import tpu as pltpu
from jax.sharding import PartitionSpec as P

MESH = pl.DeviceIdType.MESH
FRAMES = 512
HALF = FRAMES // 2
RING = 8
TILE = 128


def mod8(value):
    return lax.rem(value + 16, RING)


def split(value):
    hi = value.astype(jnp.bfloat16)
    lo = (value - hi.astype(jnp.float32)).astype(jnp.bfloat16)
    return hi, lo


def kernel(x_ref, out_ref, stage, traw, rows, cols, lhs, rhs,
           in_s, t_s, t_r, rx_s, rx_r, cx_s, cx_r, rr_s, rr_r, c_s, c_r, sib_s, sib_r):
    row = lax.axis_index("row")
    col = lax.axis_index("col")
    half = lax.axis_index("half")
    y, xl = row // 2, lax.rem(row, 2)
    xh, z = col // RING, lax.rem(col, RING)
    other = 1 - half

    fetch = pltpu.make_async_copy(x_ref, stage, in_s)
    fetch.start()

    sibling = (row, col, other)
    rx_peer = (row, (1 - xh) * RING + z, half)
    z_peer = {n: (row, xh * RING + mod8(z + n), half) for n in (1, -1, 2, -2)}
    cx_peer = (y * 2 + 1 - xl, col, half)
    y_peer = {n: (mod8(y + n) * 2 + xl, col, half) for n in (1, -1, 2, -2)}
    diagonal = {n: (mod8(y + n) * 2 + 1 - xl, col, half) for n in (1, -1, 2, -2)}

    yy = mod8(z + lax.rem(row, RING) + 4 * xh)
    t_dest = [(yy * 2 + s, row, xh) for s in range(2)]
    t_self = [(yy * 2 + s == row) & (row == col) & (xh == half) for s in range(2)]

    def part(place):
        return mod8(place - z + 4 * half)

    t_col = RING * half + part(y)
    from_self = (row == col) & (col == t_col)

    barrier = pltpu.get_barrier_semaphore()
    for peer in (sibling, rx_peer, cx_peer, *z_peer.values(), *y_peer.values(), *diagonal.values(), (col, t_col, other)):
        pl.semaphore_signal(barrier, inc=1, device_id=peer, device_id_type=MESH)

    @pl.when(jnp.logical_not(from_self))
    def _():
        pl.semaphore_signal(barrier, inc=1, device_id=(col, t_col, half), device_id_type=MESH)

    fetch.wait()
    rows[half, xh, z] = stage[...]
    pl.semaphore_wait(barrier, jnp.where(from_self, 16, 17))

    def remote(src, dst, send, recv, peer):
        return pltpu.make_async_remote_copy(
            src_ref=src, dst_ref=dst, send_sem=send, recv_sem=recv, device_id=peer, device_id_type=MESH)

    def arrived(ref, sem):
        pltpu.make_async_copy(ref, ref, sem).wait()

    pending = []

    def start(copy):
        copy.start()
        pending.append(copy)

    t_copies = []

    def transpose_out():
        for s in range(2):
            src = stage.at[pl.ds(s * 32, 32)]
            far = remote(src, traw.at[half], t_s.at[s], t_r.at[half], t_dest[s])
            near = pltpu.make_async_copy(src, traw.at[half], t_r.at[half])

            @pl.when(t_self[s])
            def _():
                near.start()

            @pl.when(jnp.logical_not(t_self[s]))
            def _():
                far.start()

            t_copies.append((t_self[s], far))

    signs = (1, -1)
    distances = (0, -1, 1, -2, 2, -3, 3, 4)

    def row_ref(u, d):
        return rows.at[half, xh if u == 0 else 1 - xh, mod8(z + d)]

    def row_pair(d, core):
        return rows.at[core, :, mod8(z + d)]

    def col_ref(u, d):
        return cols.at[part(mod8(y + d)), xl if u == 0 else 1 - xl]

    def col_pair(d):
        return cols.at[part(mod8(y + d))]

    def hop(which, direction, step, u):
        behind, ahead = ((0, 1), (0, 2), (2, 1), (2, 2))[step - 1]
        at = (0 if direction == 1 else 1, step - 1, u)
        d = -direction * behind
        if which == "row":
            ref = row_pair(d, half) if step == 3 else row_ref(u, d)
            return remote(ref, ref, rr_s.at[at], rr_r.at[at], z_peer[direction * ahead])
        peer = y_peer[direction * ahead]
        if step == 3:
            ref = col_pair(d)
        elif u == 1 and step < 3:
            ref, peer = col_ref(0, 0), diagonal[direction * ahead]
        else:
            ref = col_ref(u, d)
        return remote(ref, ref, c_s.at[at], c_r.at[at], peer)

    def to_sibling(d):
        slot = distances.index(d)
        start(remote(row_pair(d, half), row_pair(d, half), sib_s.at[slot], sib_r.at[slot], sibling))

    def begin_row(u):
        if u == 1:
            arrived(row_ref(1, 0), rx_r)
        for step in (2, 1):
            for direction in signs:
                start(hop("row", direction, step, u))
        if u == 1:
            to_sibling(0)

    def come(which, direction, step):
        recv = rr_r if which == "row" else c_r
        i = 0 if direction == 1 else 1
        d = -direction * step
        if step == 3:
            arrived(row_pair(d, half) if which == "row" else col_pair(d), recv.at[i, 2, 0])
        elif step == 4:
            u = i
            arrived(row_ref(u, 4) if which == "row" else col_ref(u, 4), recv.at[i, 3, u])
        else:
            for u in range(2):
                arrived(row_ref(u, d) if which == "row" else col_ref(u, d), recv.at[i, step - 1, u])

    def forward(which, step):
        for direction in signs:
            come(which, direction, step)
            if step == 2:
                start(hop(which, direction, 4, 0 if direction == 1 else 1))
                start(hop(which, direction, 3, 0))
            if which == "row" and step < 4:
                to_sibling(-direction * step)
        if which == "row" and step == 4:
            to_sibling(4)

    def to_lhs(*ds):
        for d in ds:
            arrived(row_pair(d, other), sib_r.at[distances.index(d)])
            for x in range(2):
                first, second = rows[0, x, mod8(z + d)], rows[1, x, mod8(z + d)]
                total = jnp.sum(first, axis=1, keepdims=True) + jnp.sum(second, axis=1, keepdims=True)
                mean = total / FRAMES
                here = pl.ds(pl.multiple_of(x * 512 + mod8(z + d) * 64, 64), 64)
                for j, value in enumerate((first, second)):
                    hi, lo = split(value - mean)
                    lhs[here, j * HALF:(j + 1) * HALF] = hi
                    lhs[here, FRAMES + j * HALF:FRAMES + (j + 1) * HALF] = lo
                    lhs[here, 2 * FRAMES + j * HALF:2 * FRAMES + (j + 1) * HALF] = hi

    def begin_col():
        for g in range(2):
            arrived(traw.at[g], t_r.at[g])
        first, second = traw[0], traw[1]
        total = jnp.sum(first, axis=1, keepdims=True) + jnp.sum(second, axis=1, keepdims=True)
        mean = total / FRAMES
        mine = col_ref(0, 0)
        mine[:, :HALF] = first - mean
        mine[:, HALF:] = second - mean
        for step in (2, 1):
            for u in range(2):
                for direction in (1, -1):
                    start(hop("col", direction, step, u))
        start(remote(mine, mine, cx_s, cx_r, cx_peer))

    base = part(y)
    sign = 1 - 2 * lax.rem(base, 2)

    def tile_of(step):
        return mod8(base + sign * (1, -2, 3, 4)[step - 1]) // 2

    def to_rhs(steps):
        for i, step in enumerate(steps):
            value = cols[pl.ds(2 * tile_of(step), 2)].reshape(TILE, FRAMES) * (1.0 / (FRAMES - 1))
            hi, lo = split(value)
            here = pl.ds(i * TILE, TILE)
            rhs[here, :FRAMES] = hi
            rhs[here, FRAMES:2 * FRAMES] = hi
            rhs[here, 2 * FRAMES:] = lo

    def multiply(steps):
        product = lax.dot_general(
            lhs[...], rhs[...], (((1,), (1,)), ((), ())), preferred_element_type=jnp.float32)
        for i, step in enumerate(steps):
            there = pl.ds(pl.multiple_of(tile_of(step) * TILE, TILE), TILE)
            out_ref[:, there] = product[:, i * TILE:(i + 1) * TILE]

    transpose_out()
    start(remote(row_ref(0, 0), row_ref(0, 0), rx_s, rx_r, rx_peer))
    begin_row(0)
    begin_row(1)
    begin_col()
    forward("row", 2)
    to_lhs(0)
    forward("row", 1)
    forward("col", 2)
    to_lhs(-2, 2)
    forward("row", 3)
    forward("row", 4)
    to_lhs(-1, 1)
    forward("col", 1)
    arrived(col_ref(1, 0), cx_r)
    to_rhs((1, 2))
    to_lhs(-3, 3, 4)
    multiply((1, 2))
    forward("col", 3)
    forward("col", 4)
    to_rhs((3, 4))
    multiply((3, 4))

    for copy in pending:
        copy.wait_send()
    for local, copy in t_copies:
        @pl.when(jnp.logical_not(local))
        def _():
            copy.wait_send()


def body(frames):
    dma = pltpu.SemaphoreType.DMA
    return pl.pallas_call(
        kernel,
        out_shape=jax.ShapeDtypeStruct((1024, 512), jnp.float32),
        in_specs=[pl.BlockSpec(memory_space=pltpu.HBM)],
        out_specs=pl.BlockSpec(memory_space=pltpu.VMEM),
        scratch_shapes=[
            pltpu.VMEM((64, HALF), jnp.float32),
            pltpu.VMEM((2, 32, HALF), jnp.float32),
            pltpu.VMEM((2, 2, 8, 64, HALF), jnp.float32),
            pltpu.VMEM((8, 2, 32, FRAMES), jnp.float32),
            pltpu.VMEM((1024, 3 * FRAMES), jnp.bfloat16),
            pltpu.VMEM((2 * TILE, 3 * FRAMES), jnp.bfloat16),
            dma, dma((2,)), dma((2,)), dma, dma, dma, dma, dma((2, 4, 2)), dma((2, 4, 2)), dma((2, 4, 2)), dma((2, 4, 2)),
            dma((8,)), dma((8,)),
        ],
        compiler_params=pltpu.CompilerParams(
            collective_id=0, has_side_effects=True, vmem_limit_bytes=40 * 1024 * 1024),
        cost_estimate=pl.CostEstimate(flops=3 * 2 * 1024 * 512 * 512, bytes_accessed=2 << 20, transcendentals=0),
    )(pltpu.with_memory_space_constraint(frames.T, pltpu.HBM))


def solution(mesh):
    in_specs = (P("half", ("row", "col")),)
    out_specs = P("row", ("col", "half"))
    return jax.shard_map(body, mesh=mesh, in_specs=in_specs, out_specs=out_specs, check_vma=False)
```

```python
import jax
import jax.numpy as jnp
from jax import lax
from jax.experimental import pallas as pl
from jax.experimental.pallas import tpu as pltpu
from jax.sharding import PartitionSpec as P

MESH = pl.DeviceIdType.MESH
FRAMES = 512
HALF = FRAMES // 2
RING = 8
TILE = 128


def mod8(value):
    return lax.rem(value + 16, RING)


def split(value):
    hi = value.astype(jnp.bfloat16)
    lo = (value - hi.astype(jnp.float32)).astype(jnp.bfloat16)
    return hi, lo


def kernel(x_ref, out_ref, stage, traw, rows, cols, lhs, rhs,
           in_s, t_s, t_r, rx_s, rx_r, cx_s, cx_r, rr_s, rr_r, c_s, c_r, sib_s, sib_r):
    row = lax.axis_index("row")
    col = lax.axis_index("col")
    half = lax.axis_index("half")
    y, xl = row // 2, lax.rem(row, 2)
    xh, z = col // RING, lax.rem(col, RING)
    other = 1 - half

    fetch = pltpu.make_async_copy(x_ref, stage, in_s)
    fetch.start()

    sibling = (row, col, other)
    rx_peer = (row, (1 - xh) * RING + z, half)
    z_peer = {n: (row, xh * RING + mod8(z + n), half) for n in (1, -1, 2, -2)}
    cx_peer = (y * 2 + 1 - xl, col, half)
    y_peer = {n: (mod8(y + n) * 2 + xl, col, half) for n in (1, -1, 2, -2)}
    diagonal = {n: (mod8(y + n) * 2 + 1 - xl, col, half) for n in (1, -1, 2, -2)}

    yy = mod8(z + lax.rem(row, RING) + 4 * xh)
    t_dest = [(yy * 2 + s, row, xh) for s in range(2)]
    t_self = [(yy * 2 + s == row) & (row == col) & (xh == half) for s in range(2)]

    def part(place):
        return mod8(place - z + 4 * half)

    t_col = RING * half + part(y)
    from_self = (row == col) & (col == t_col)

    barrier = pltpu.get_barrier_semaphore()
    for peer in (sibling, rx_peer, cx_peer, *z_peer.values(), *y_peer.values(), *diagonal.values(), (col, t_col, other)):
        pl.semaphore_signal(barrier, inc=1, device_id=peer, device_id_type=MESH)

    @pl.when(jnp.logical_not(from_self))
    def _():
        pl.semaphore_signal(barrier, inc=1, device_id=(col, t_col, half), device_id_type=MESH)

    fetch.wait()
    rows[half, xh, z] = stage[...]
    pl.semaphore_wait(barrier, jnp.where(from_self, 16, 17))

    def remote(src, dst, send, recv, peer):
        return pltpu.make_async_remote_copy(
            src_ref=src, dst_ref=dst, send_sem=send, recv_sem=recv, device_id=peer, device_id_type=MESH)

    def arrived(ref, sem):
        pltpu.make_async_copy(ref, ref, sem).wait()

    pending = []

    def start(copy):
        copy.start()
        pending.append(copy)

    t_copies = []

    def transpose_out():
        for s in range(2):
            src = stage.at[pl.ds(s * 32, 32)]
            far = remote(src, traw.at[half], t_s.at[s], t_r.at[half], t_dest[s])
            near = pltpu.make_async_copy(src, traw.at[half], t_r.at[half])

            @pl.when(t_self[s])
            def _():
                near.start()

            @pl.when(jnp.logical_not(t_self[s]))
            def _():
                far.start()

            t_copies.append((t_self[s], far))

    signs = (1, -1)
    distances = (0, -1, 1, -2, 2, -3, 3, 4)

    def row_ref(u, d):
        return rows.at[half, xh if u == 0 else 1 - xh, mod8(z + d)]

    def row_pair(d, core):
        return rows.at[core, :, mod8(z + d)]

    def col_ref(u, d):
        return cols.at[part(mod8(y + d)), xl if u == 0 else 1 - xl]

    def col_pair(d):
        return cols.at[part(mod8(y + d))]

    def hop(which, direction, step, u):
        behind, ahead = ((0, 1), (0, 2), (2, 1), (2, 2))[step - 1]
        at = (0 if direction == 1 else 1, step - 1, u)
        d = -direction * behind
        if which == "row":
            ref = row_pair(d, half) if step == 3 else row_ref(u, d)
            return remote(ref, ref, rr_s.at[at], rr_r.at[at], z_peer[direction * ahead])
        peer = y_peer[direction * ahead]
        if step == 3:
            ref = col_pair(d)
        elif u == 1 and step < 3:
            ref, peer = col_ref(0, 0), diagonal[direction * ahead]
        else:
            ref = col_ref(u, d)
        return remote(ref, ref, c_s.at[at], c_r.at[at], peer)

    def to_sibling(d):
        slot = distances.index(d)
        start(remote(row_pair(d, half), row_pair(d, half), sib_s.at[slot], sib_r.at[slot], sibling))

    def begin_row(u):
        if u == 1:
            arrived(row_ref(1, 0), rx_r)
        for step in (2, 1):
            for direction in signs:
                start(hop("row", direction, step, u))
        if u == 1:
            to_sibling(0)

    def come(which, direction, step):
        recv = rr_r if which == "row" else c_r
        i = 0 if direction == 1 else 1
        d = -direction * step
        if step == 3:
            arrived(row_pair(d, half) if which == "row" else col_pair(d), recv.at[i, 2, 0])
        elif step == 4:
            u = i
            arrived(row_ref(u, 4) if which == "row" else col_ref(u, 4), recv.at[i, 3, u])
        else:
            for u in range(2):
                arrived(row_ref(u, d) if which == "row" else col_ref(u, d), recv.at[i, step - 1, u])

    def forward(which, step):
        for direction in signs:
            come(which, direction, step)
            if step == 2:
                start(hop(which, direction, 4, 0 if direction == 1 else 1))
                start(hop(which, direction, 3, 0))
            if which == "row" and step < 4:
                to_sibling(-direction * step)
        if which == "row" and step == 4:
            to_sibling(4)

    def to_lhs(*ds):
        for d in ds:
            arrived(row_pair(d, other), sib_r.at[distances.index(d)])
            for x in range(2):
                first, second = rows[0, x, mod8(z + d)], rows[1, x, mod8(z + d)]
                total = jnp.sum(first, axis=1, keepdims=True) + jnp.sum(second, axis=1, keepdims=True)
                mean = total / FRAMES
                here = pl.ds(pl.multiple_of(x * 512 + mod8(z + d) * 64, 64), 64)
                for j, value in enumerate((first, second)):
                    hi, lo = split(value - mean)
                    lhs[here, j * HALF:(j + 1) * HALF] = hi
                    lhs[here, FRAMES + j * HALF:FRAMES + (j + 1) * HALF] = lo
                    lhs[here, 2 * FRAMES + j * HALF:2 * FRAMES + (j + 1) * HALF] = hi

    def begin_col():
        for g in range(2):
            arrived(traw.at[g], t_r.at[g])
        first, second = traw[0], traw[1]
        total = jnp.sum(first, axis=1, keepdims=True) + jnp.sum(second, axis=1, keepdims=True)
        mean = total / FRAMES
        mine = col_ref(0, 0)
        mine[:, :HALF] = first - mean
        mine[:, HALF:] = second - mean
        for step in (2, 1):
            for u in range(2):
                for direction in (1, -1):
                    start(hop("col", direction, step, u))
        start(remote(mine, mine, cx_s, cx_r, cx_peer))

    base = part(y)
    sign = 1 - 2 * lax.rem(base, 2)

    def tile_of(step):
        return mod8(base + sign * (1, -2, 3, 4)[step - 1]) // 2

    def to_rhs(steps):
        for i, step in enumerate(steps):
            value = cols[pl.ds(2 * tile_of(step), 2)].reshape(TILE, FRAMES) * (1.0 / (FRAMES - 1))
            hi, lo = split(value)
            here = pl.ds(i * TILE, TILE)
            rhs[here, :FRAMES] = hi
            rhs[here, FRAMES:2 * FRAMES] = hi
            rhs[here, 2 * FRAMES:] = lo

    def multiply(steps, u):
        here = pl.ds(u * 512, 512)
        product = lax.dot_general(
            lhs[here, :], rhs[...], (((1,), (1,)), ((), ())), preferred_element_type=jnp.float32)
        for i, step in enumerate(steps):
            there = pl.ds(pl.multiple_of(tile_of(step) * TILE, TILE), TILE)
            out_ref[here, there] = product[:, i * TILE:(i + 1) * TILE]

    transpose_out()
    start(remote(row_ref(0, 0), row_ref(0, 0), rx_s, rx_r, rx_peer))
    begin_row(0)
    begin_col()
    begin_row(1)
    forward("row", 2)
    to_lhs(0)
    forward("col", 2)
    forward("row", 1)
    to_lhs(-2, 2)
    forward("row", 3)
    forward("row", 4)
    to_lhs(-1, 1)
    forward("col", 1)
    arrived(col_ref(1, 0), cx_r)
    to_rhs((1, 2))
    to_lhs(-3, 3, 4)
    multiply((1, 2), 0)
    multiply((1, 2), 1)
    forward("col", 3)
    forward("col", 4)
    to_rhs((3, 4))
    multiply((3, 4), 0)
    multiply((3, 4), 1)

    for copy in pending:
        copy.wait_send()
    for local, copy in t_copies:
        @pl.when(jnp.logical_not(local))
        def _():
            copy.wait_send()


def body(frames):
    dma = pltpu.SemaphoreType.DMA
    return pl.pallas_call(
        kernel,
        out_shape=jax.ShapeDtypeStruct((1024, 512), jnp.float32),
        in_specs=[pl.BlockSpec(memory_space=pltpu.HBM)],
        out_specs=pl.BlockSpec(memory_space=pltpu.VMEM),
        scratch_shapes=[
            pltpu.VMEM((64, HALF), jnp.float32),
            pltpu.VMEM((2, 32, HALF), jnp.float32),
            pltpu.VMEM((2, 2, 8, 64, HALF), jnp.float32),
            pltpu.VMEM((8, 2, 32, FRAMES), jnp.float32),
            pltpu.VMEM((1024, 3 * FRAMES), jnp.bfloat16),
            pltpu.VMEM((2 * TILE, 3 * FRAMES), jnp.bfloat16),
            dma, dma((2,)), dma((2,)), dma, dma, dma, dma, dma((2, 4, 2)), dma((2, 4, 2)), dma((2, 4, 2)), dma((2, 4, 2)),
            dma((8,)), dma((8,)),
        ],
        compiler_params=pltpu.CompilerParams(
            collective_id=0, has_side_effects=True, vmem_limit_bytes=40 * 1024 * 1024),
        cost_estimate=pl.CostEstimate(flops=3 * 2 * 1024 * 512 * 512, bytes_accessed=2 << 20, transcendentals=0),
    )(pltpu.with_memory_space_constraint(frames.T, pltpu.HBM))


def solution(mesh):
    in_specs = (P("half", ("row", "col")),)
    out_specs = P("row", ("col", "half"))
    return jax.shard_map(body, mesh=mesh, in_specs=in_specs, out_specs=out_specs, check_vma=False)
```

```python
import jax
import jax.numpy as jnp
from jax import lax
from jax.experimental import pallas as pl
from jax.experimental.pallas import tpu as pltpu
from jax.sharding import PartitionSpec as P

MESH = pl.DeviceIdType.MESH
FRAMES = 512
HALF = FRAMES // 2
RING = 8
TILE = 128


def mod8(value):
    return lax.rem(value + 16, RING)


def split(value):
    hi = value.astype(jnp.bfloat16)
    lo = (value - hi.astype(jnp.float32)).astype(jnp.bfloat16)
    return hi, lo


def kernel(x_ref, out_ref, stage, traw, rows, cols, lhs, rhs,
           in_s, t_s, t_r, rx_s, rx_r, cx_s, cx_r, rr_s, rr_r, c_s, c_r, sib_s, sib_r):
    row = lax.axis_index("row")
    col = lax.axis_index("col")
    half = lax.axis_index("half")
    y, xl = row // 2, lax.rem(row, 2)
    xh, z = col // RING, lax.rem(col, RING)
    other = 1 - half

    fetch = pltpu.make_async_copy(x_ref, stage, in_s)
    fetch.start()

    sibling = (row, col, other)
    rx_peer = (row, (1 - xh) * RING + z, half)
    z_peer = {n: (row, xh * RING + mod8(z + n), half) for n in (1, -1, 2, -2)}
    cx_peer = (y * 2 + 1 - xl, col, half)
    y_peer = {n: (mod8(y + n) * 2 + xl, col, half) for n in (1, -1, 2, -2)}
    diagonal = {n: (mod8(y + n) * 2 + 1 - xl, col, half) for n in (1, -1, 2, -2)}

    yy = mod8(z + lax.rem(row, RING) + 4 * xh)
    t_dest = [(yy * 2 + s, row, xh) for s in range(2)]
    t_self = [(yy * 2 + s == row) & (row == col) & (xh == half) for s in range(2)]

    def part(place):
        return mod8(place - z + 4 * half)

    t_col = RING * half + part(y)
    from_self = (row == col) & (col == t_col)

    barrier = pltpu.get_barrier_semaphore()
    for peer in (sibling, rx_peer, cx_peer, *z_peer.values(), *y_peer.values(), *diagonal.values(), (col, t_col, other)):
        pl.semaphore_signal(barrier, inc=1, device_id=peer, device_id_type=MESH)

    @pl.when(jnp.logical_not(from_self))
    def _():
        pl.semaphore_signal(barrier, inc=1, device_id=(col, t_col, half), device_id_type=MESH)

    fetch.wait()
    rows[half, xh, z] = stage[...]
    pl.semaphore_wait(barrier, jnp.where(from_self, 16, 17))

    def remote(src, dst, send, recv, peer):
        return pltpu.make_async_remote_copy(
            src_ref=src, dst_ref=dst, send_sem=send, recv_sem=recv, device_id=peer, device_id_type=MESH)

    def arrived(ref, sem):
        pltpu.make_async_copy(ref, ref, sem).wait()

    pending = []

    def start(copy):
        copy.start()
        pending.append(copy)

    t_copies = []

    def transpose_out():
        for s in range(2):
            src = stage.at[pl.ds(s * 32, 32)]
            far = remote(src, traw.at[half], t_s.at[s], t_r.at[half], t_dest[s])
            near = pltpu.make_async_copy(src, traw.at[half], t_r.at[half])

            @pl.when(t_self[s])
            def _():
                near.start()

            @pl.when(jnp.logical_not(t_self[s]))
            def _():
                far.start()

            t_copies.append((t_self[s], far))

    signs = (1, -1)
    distances = (0, -1, 1, -2, 2, -3, 3, 4)

    def row_ref(u, d):
        return rows.at[half, xh if u == 0 else 1 - xh, mod8(z + d)]

    def row_pair(d, core):
        return rows.at[core, :, mod8(z + d)]

    def col_ref(u, d):
        return cols.at[part(mod8(y + d)), xl if u == 0 else 1 - xl]

    def col_pair(d):
        return cols.at[part(mod8(y + d))]

    def hop(which, direction, step, u):
        behind, ahead = ((0, 1), (0, 2), (2, 1), (2, 2))[step - 1]
        at = (0 if direction == 1 else 1, step - 1, u)
        d = -direction * behind
        if which == "row":
            ref = row_ref(u, d)
            return remote(ref, ref, rr_s.at[at], rr_r.at[at], z_peer[direction * ahead])
        peer = y_peer[direction * ahead]
        if step == 3:
            ref = col_pair(d)
        elif u == 1 and step < 3:
            ref, peer = col_ref(0, 0), diagonal[direction * ahead]
        else:
            ref = col_ref(u, d)
        return remote(ref, ref, c_s.at[at], c_r.at[at], peer)

    def to_sibling(d):
        slot = distances.index(d)
        start(remote(row_pair(d, half), row_pair(d, half), sib_s.at[slot], sib_r.at[slot], sibling))

    def begin_row(u):
        if u == 1:
            arrived(row_ref(1, 0), rx_r)
        for step in (2, 1):
            for direction in signs:
                start(hop("row", direction, step, u))
        if u == 1:
            to_sibling(0)

    def come_row(direction, step, u):
        i = 0 if direction == 1 else 1
        arrived(row_ref(u, -direction * step), rr_r.at[i, step - 1, u])

    def pass_rows(u):
        for direction in signs:
            come_row(direction, 2, u)
            if (direction == 1) == (u == 0):
                start(hop("row", direction, 4, u))
            start(hop("row", direction, 3, u))

    def share_rows(step):
        for direction in signs:
            if step != 2:
                for u in range(2):
                    if step < 4 or (direction == 1) == (u == 0):
                        come_row(direction, step, u)
            if step < 4:
                to_sibling(-direction * step)
        if step == 4:
            to_sibling(4)

    def come_col(step):
        for direction in signs:
            i = 0 if direction == 1 else 1
            d = -direction * step
            if step == 3:
                arrived(col_pair(d), c_r.at[i, 2, 0])
            elif step == 4:
                arrived(col_ref(i, 4), c_r.at[i, 3, i])
            else:
                for u in range(2):
                    arrived(col_ref(u, d), c_r.at[i, step - 1, u])
            if step == 2:
                start(hop("col", direction, 4, i))
                start(hop("col", direction, 3, 0))

    def to_lhs(*ds):
        for d in ds:
            arrived(row_pair(d, other), sib_r.at[distances.index(d)])
            for x in range(2):
                first, second = rows[0, x, mod8(z + d)], rows[1, x, mod8(z + d)]
                total = jnp.sum(first, axis=1, keepdims=True) + jnp.sum(second, axis=1, keepdims=True)
                mean = total / FRAMES
                here = pl.ds(pl.multiple_of(x * 512 + mod8(z + d) * 64, 64), 64)
                for j, value in enumerate((first, second)):
                    hi, lo = split(value - mean)
                    lhs[here, j * HALF:(j + 1) * HALF] = hi
                    lhs[here, FRAMES + j * HALF:FRAMES + (j + 1) * HALF] = lo
                    lhs[here, 2 * FRAMES + j * HALF:2 * FRAMES + (j + 1) * HALF] = hi

    def begin_col():
        for g in range(2):
            arrived(traw.at[g], t_r.at[g])
        first, second = traw[0], traw[1]
        total = jnp.sum(first, axis=1, keepdims=True) + jnp.sum(second, axis=1, keepdims=True)
        mean = total / FRAMES
        mine = col_ref(0, 0)
        mine[:, :HALF] = first - mean
        mine[:, HALF:] = second - mean
        for step in (2, 1):
            for u in range(2):
                for direction in (1, -1):
                    start(hop("col", direction, step, u))
        start(remote(mine, mine, cx_s, cx_r, cx_peer))

    base = part(y)
    sign = 1 - 2 * lax.rem(base, 2)

    def tile_of(step):
        return mod8(base + sign * (1, -2, 3, 4)[step - 1]) // 2

    def to_rhs(steps):
        for i, step in enumerate(steps):
            value = cols[pl.ds(2 * tile_of(step), 2)].reshape(TILE, FRAMES) * (1.0 / (FRAMES - 1))
            hi, lo = split(value)
            here = pl.ds(i * TILE, TILE)
            rhs[here, :FRAMES] = hi
            rhs[here, FRAMES:2 * FRAMES] = hi
            rhs[here, 2 * FRAMES:] = lo

    def multiply(steps, u):
        here = pl.ds(u * 512, 512)
        product = lax.dot_general(
            lhs[here, :], rhs[...], (((1,), (1,)), ((), ())), preferred_element_type=jnp.float32)
        for i, step in enumerate(steps):
            there = pl.ds(pl.multiple_of(tile_of(step) * TILE, TILE), TILE)
            out_ref[here, there] = product[:, i * TILE:(i + 1) * TILE]

    transpose_out()
    start(remote(row_ref(0, 0), row_ref(0, 0), rx_s, rx_r, rx_peer))
    begin_row(0)
    begin_row(1)
    pass_rows(0)
    begin_col()
    pass_rows(1)
    share_rows(2)
    to_lhs(0)
    come_col(2)
    share_rows(1)
    to_lhs(-2, 2)
    share_rows(3)
    share_rows(4)
    to_lhs(-1, 1)
    come_col(1)
    arrived(col_ref(1, 0), cx_r)
    to_rhs((1, 2))
    to_lhs(-3, 3, 4)
    multiply((1, 2), 0)
    multiply((1, 2), 1)
    come_col(3)
    come_col(4)
    to_rhs((3, 4))
    multiply((3, 4), 0)
    multiply((3, 4), 1)

    for copy in pending:
        copy.wait_send()
    for local, copy in t_copies:
        @pl.when(jnp.logical_not(local))
        def _():
            copy.wait_send()


def body(frames):
    dma = pltpu.SemaphoreType.DMA
    return pl.pallas_call(
        kernel,
        out_shape=jax.ShapeDtypeStruct((1024, 512), jnp.float32),
        in_specs=[pl.BlockSpec(memory_space=pltpu.HBM)],
        out_specs=pl.BlockSpec(memory_space=pltpu.VMEM),
        scratch_shapes=[
            pltpu.VMEM((64, HALF), jnp.float32),
            pltpu.VMEM((2, 32, HALF), jnp.float32),
            pltpu.VMEM((2, 2, 8, 64, HALF), jnp.float32),
            pltpu.VMEM((8, 2, 32, FRAMES), jnp.float32),
            pltpu.VMEM((1024, 3 * FRAMES), jnp.bfloat16),
            pltpu.VMEM((2 * TILE, 3 * FRAMES), jnp.bfloat16),
            dma, dma((2,)), dma((2,)), dma, dma, dma, dma, dma((2, 4, 2)), dma((2, 4, 2)), dma((2, 4, 2)), dma((2, 4, 2)),
            dma((8,)), dma((8,)),
        ],
        compiler_params=pltpu.CompilerParams(
            collective_id=0, has_side_effects=True, vmem_limit_bytes=40 * 1024 * 1024),
        cost_estimate=pl.CostEstimate(flops=3 * 2 * 1024 * 512 * 512, bytes_accessed=2 << 20, transcendentals=0),
    )(pltpu.with_memory_space_constraint(frames.T, pltpu.HBM))


def solution(mesh):
    in_specs = (P("half", ("row", "col")),)
    out_specs = P("row", ("col", "half"))
    return jax.shard_map(body, mesh=mesh, in_specs=in_specs, out_specs=out_specs, check_vma=False)
```

```python
import jax
import jax.numpy as jnp
from jax import lax
from jax.experimental import pallas as pl
from jax.experimental.pallas import tpu as pltpu
from jax.sharding import PartitionSpec as P

MESH = pl.DeviceIdType.MESH
FRAMES = 512
HALF = FRAMES // 2
RING = 8
TILE = 128


def mod8(value):
    return lax.rem(value + 16, RING)


def split(value):
    hi = value.astype(jnp.bfloat16)
    lo = (value - hi.astype(jnp.float32)).astype(jnp.bfloat16)
    return hi, lo


def kernel(x_ref, out_ref, stage, traw, rows, cols, lhs, rhs,
           in_s, t_s, t_r, rx_s, rx_r, cx_s, cx_r, rr_s, rr_r, c_s, c_r, sib_s, sib_r):
    row = lax.axis_index("row")
    col = lax.axis_index("col")
    half = lax.axis_index("half")
    y, xl = row // 2, lax.rem(row, 2)
    xh, z = col // RING, lax.rem(col, RING)
    other = 1 - half

    fetch = pltpu.make_async_copy(x_ref, stage, in_s)
    fetch.start()

    sibling = (row, col, other)
    rx_peer = (row, (1 - xh) * RING + z, half)
    z_peer = {n: (row, xh * RING + mod8(z + n), half) for n in (1, -1, 2, -2)}
    cx_peer = (y * 2 + 1 - xl, col, half)
    y_peer = {n: (mod8(y + n) * 2 + xl, col, half) for n in (1, -1, 2, -2)}
    diagonal = {n: (mod8(y + n) * 2 + 1 - xl, col, half) for n in (1, -1, 2, -2)}

    yy = mod8(z + lax.rem(row, RING) + 4 * xh)
    t_dest = [(yy * 2 + s, row, xh) for s in range(2)]
    t_self = [(yy * 2 + s == row) & (row == col) & (xh == half) for s in range(2)]

    def part(place):
        return mod8(place - z + 4 * half)

    t_col = RING * half + part(y)
    from_self = (row == col) & (col == t_col)

    barrier = pltpu.get_barrier_semaphore()
    for peer in (sibling, rx_peer, cx_peer, *z_peer.values(), *y_peer.values(), *diagonal.values(), (col, t_col, other)):
        pl.semaphore_signal(barrier, inc=1, device_id=peer, device_id_type=MESH)

    @pl.when(jnp.logical_not(from_self))
    def _():
        pl.semaphore_signal(barrier, inc=1, device_id=(col, t_col, half), device_id_type=MESH)

    fetch.wait()
    rows[half, xh, z] = stage[...]
    pl.semaphore_wait(barrier, jnp.where(from_self, 16, 17))

    def remote(src, dst, send, recv, peer):
        return pltpu.make_async_remote_copy(
            src_ref=src, dst_ref=dst, send_sem=send, recv_sem=recv, device_id=peer, device_id_type=MESH)

    def arrived(ref, sem):
        pltpu.make_async_copy(ref, ref, sem).wait()

    pending = []

    def start(copy):
        copy.start()
        pending.append(copy)

    t_copies = []

    def transpose_out():
        for s in range(2):
            src = stage.at[pl.ds(s * 32, 32)]
            far = remote(src, traw.at[half], t_s.at[s], t_r.at[half], t_dest[s])
            near = pltpu.make_async_copy(src, traw.at[half], t_r.at[half])

            @pl.when(t_self[s])
            def _():
                near.start()

            @pl.when(jnp.logical_not(t_self[s]))
            def _():
                far.start()

            t_copies.append((t_self[s], far))

    signs = (1, -1)
    distances = (0, -1, 1, -2, 2, -3, 3, 4)

    def row_ref(u, d):
        return rows.at[half, xh if u == 0 else 1 - xh, mod8(z + d)]

    def row_pair(d, core):
        return rows.at[core, :, mod8(z + d)]

    def col_ref(u, d):
        return cols.at[part(mod8(y + d)), xl if u == 0 else 1 - xl]

    def col_pair(d):
        return cols.at[part(mod8(y + d))]

    def hop(which, direction, step, u):
        behind, ahead = ((0, 1), (0, 2), (2, 1), (2, 2))[step - 1]
        at = (0 if direction == 1 else 1, step - 1, u)
        d = -direction * behind
        if which == "row":
            ref = row_pair(d, half) if step == 3 else row_ref(u, d)
            return remote(ref, ref, rr_s.at[at], rr_r.at[at], z_peer[direction * ahead])
        peer = y_peer[direction * ahead]
        if step == 3:
            ref = col_pair(d)
        elif u == 1 and step < 3:
            ref, peer = col_ref(0, 0), diagonal[direction * ahead]
        else:
            ref = col_ref(u, d)
        return remote(ref, ref, c_s.at[at], c_r.at[at], peer)

    def to_sibling(d):
        slot = distances.index(d)
        start(remote(row_pair(d, half), row_pair(d, half), sib_s.at[slot], sib_r.at[slot], sibling))

    def begin_row(u):
        if u == 1:
            arrived(row_ref(1, 0), rx_r)
        for step in (2, 1):
            for direction in signs:
                start(hop("row", direction, step, u))
        if u == 1:
            to_sibling(0)

    def come(which, direction, step):
        recv = rr_r if which == "row" else c_r
        i = 0 if direction == 1 else 1
        d = -direction * step
        if step == 3:
            arrived(row_pair(d, half) if which == "row" else col_pair(d), recv.at[i, 2, 0])
        elif step == 4:
            u = i
            arrived(row_ref(u, 4) if which == "row" else col_ref(u, 4), recv.at[i, 3, u])
        else:
            for u in range(2):
                arrived(row_ref(u, d) if which == "row" else col_ref(u, d), recv.at[i, step - 1, u])

    def forward(which, step):
        for direction in signs:
            come(which, direction, step)
            if step == 2:
                start(hop(which, direction, 4, 0 if direction == 1 else 1))
                start(hop(which, direction, 3, 0))
            if which == "row" and step < 4:
                to_sibling(-direction * step)
        if which == "row" and step == 4:
            to_sibling(4)

    def to_lhs(*ds):
        for d in ds:
            arrived(row_pair(d, other), sib_r.at[distances.index(d)])
            for x in range(2):
                first, second = rows[0, x, mod8(z + d)], rows[1, x, mod8(z + d)]
                total = jnp.sum(first, axis=1, keepdims=True) + jnp.sum(second, axis=1, keepdims=True)
                mean = total / FRAMES
                here = pl.ds(pl.multiple_of(x * 512 + mod8(z + d) * 64, 64), 64)
                for j, value in enumerate((first, second)):
                    hi, lo = split(value - mean)
                    lhs[here, j * HALF:(j + 1) * HALF] = hi
                    lhs[here, FRAMES + j * HALF:FRAMES + (j + 1) * HALF] = lo
                    lhs[here, 2 * FRAMES + j * HALF:2 * FRAMES + (j + 1) * HALF] = hi

    def begin_col():
        for g in range(2):
            arrived(traw.at[g], t_r.at[g])
        first, second = traw[0], traw[1]
        total = jnp.sum(first, axis=1, keepdims=True) + jnp.sum(second, axis=1, keepdims=True)
        mean = total / FRAMES
        mine = col_ref(0, 0)
        mine[:, :HALF] = first - mean
        mine[:, HALF:] = second - mean
        for step in (2, 1):
            for u in range(2):
                for direction in (1, -1):
                    start(hop("col", direction, step, u))
        start(remote(mine, mine, cx_s, cx_r, cx_peer))

    base = part(y)
    sign = 1 - 2 * lax.rem(base, 2)

    def tile_of(step):
        return mod8(base + sign * (1, -2, 3, 4)[step - 1]) // 2

    def to_rhs(steps):
        for i, step in enumerate(steps):
            value = cols[pl.ds(2 * tile_of(step), 2)].reshape(TILE, FRAMES) * (1.0 / (FRAMES - 1))
            hi, lo = split(value)
            here = pl.ds(i * TILE, TILE)
            rhs[here, :FRAMES] = hi
            rhs[here, FRAMES:2 * FRAMES] = hi
            rhs[here, 2 * FRAMES:] = lo

    def multiply(steps, u):
        here = pl.ds(u * 512, 512)
        product = lax.dot_general(
            lhs[here, :], rhs[...], (((1,), (1,)), ((), ())), preferred_element_type=jnp.float32)
        for i, step in enumerate(steps):
            there = pl.ds(pl.multiple_of(tile_of(step) * TILE, TILE), TILE)
            out_ref[here, there] = product[:, i * TILE:(i + 1) * TILE]

    transpose_out()
    start(remote(row_ref(0, 0), row_ref(0, 0), rx_s, rx_r, rx_peer))
    begin_row(0)
    begin_row(1)
    begin_col()
    forward("row", 2)
    forward("col", 2)
    to_lhs(0)
    forward("row", 1)
    to_lhs(-2, 2)
    forward("row", 3)
    forward("row", 4)
    to_lhs(-1, 1)
    forward("col", 1)
    arrived(col_ref(1, 0), cx_r)
    to_rhs((1, 2))
    to_lhs(-3, 3, 4)
    multiply((1, 2), 0)
    multiply((1, 2), 1)
    forward("col", 3)
    forward("col", 4)
    to_rhs((3, 4))
    multiply((3, 4), 0)
    multiply((3, 4), 1)

    for copy in pending:
        copy.wait_send()
    for local, copy in t_copies:
        @pl.when(jnp.logical_not(local))
        def _():
            copy.wait_send()


def body(frames):
    dma = pltpu.SemaphoreType.DMA
    return pl.pallas_call(
        kernel,
        out_shape=jax.ShapeDtypeStruct((1024, 512), jnp.float32),
        in_specs=[pl.BlockSpec(memory_space=pltpu.HBM)],
        out_specs=pl.BlockSpec(memory_space=pltpu.VMEM),
        scratch_shapes=[
            pltpu.VMEM((64, HALF), jnp.float32),
            pltpu.VMEM((2, 32, HALF), jnp.float32),
            pltpu.VMEM((2, 2, 8, 64, HALF), jnp.float32),
            pltpu.VMEM((8, 2, 32, FRAMES), jnp.float32),
            pltpu.VMEM((1024, 3 * FRAMES), jnp.bfloat16),
            pltpu.VMEM((2 * TILE, 3 * FRAMES), jnp.bfloat16),
            dma, dma((2,)), dma((2,)), dma, dma, dma, dma, dma((2, 4, 2)), dma((2, 4, 2)), dma((2, 4, 2)), dma((2, 4, 2)),
            dma((8,)), dma((8,)),
        ],
        compiler_params=pltpu.CompilerParams(
            collective_id=0, has_side_effects=True, vmem_limit_bytes=40 * 1024 * 1024),
        cost_estimate=pl.CostEstimate(flops=3 * 2 * 1024 * 512 * 512, bytes_accessed=2 << 20, transcendentals=0),
    )(pltpu.with_memory_space_constraint(frames.T, pltpu.HBM))


def solution(mesh):
    in_specs = (P("half", ("row", "col")),)
    out_specs = P("row", ("col", "half"))
    return jax.shard_map(body, mesh=mesh, in_specs=in_specs, out_specs=out_specs, check_vma=False)
```

```python
import jax
import jax.numpy as jnp
from jax import lax
from jax.experimental import pallas as pl
from jax.experimental.pallas import tpu as pltpu
from jax.sharding import PartitionSpec as P

MESH = pl.DeviceIdType.MESH
FRAMES = 512
HALF = FRAMES // 2
RING = 8
TILE = 128


def mod8(value):
    return lax.rem(value + 16, RING)


def split(value):
    hi = value.astype(jnp.bfloat16)
    lo = (value - hi.astype(jnp.float32)).astype(jnp.bfloat16)
    return hi, lo


def kernel(x_ref, out_ref, stage, traw, rows, cols, lhs, rhs,
           in_s, t_s, t_r, rx_s, rx_r, cx_s, cx_r, rr_s, rr_r, c_s, c_r, sib_s, sib_r):
    row = lax.axis_index("row")
    col = lax.axis_index("col")
    half = lax.axis_index("half")
    y, xl = row // 2, lax.rem(row, 2)
    xh, z = col // RING, lax.rem(col, RING)
    other = 1 - half

    fetch = pltpu.make_async_copy(x_ref, stage, in_s)
    fetch.start()

    sibling = (row, col, other)
    rx_peer = (row, (1 - xh) * RING + z, half)
    z_peer = {n: (row, xh * RING + mod8(z + n), half) for n in (1, -1, 2, -2)}
    cx_peer = (y * 2 + 1 - xl, col, half)
    y_peer = {n: (mod8(y + n) * 2 + xl, col, half) for n in (1, -1, 2, -2)}
    diagonal = {n: (mod8(y + n) * 2 + 1 - xl, col, half) for n in (1, -1, 2, -2)}

    yy = mod8(z + lax.rem(row, RING) + 4 * xh)
    t_dest = [(yy * 2 + s, row, xh) for s in range(2)]
    t_self = [(yy * 2 + s == row) & (row == col) & (xh == half) for s in range(2)]

    def part(place):
        return mod8(place - z + 4 * half)

    t_col = RING * half + part(y)
    from_self = (row == col) & (col == t_col)

    barrier = pltpu.get_barrier_semaphore()
    for peer in (sibling, rx_peer, cx_peer, *z_peer.values(), *y_peer.values(), *diagonal.values(), (col, t_col, other)):
        pl.semaphore_signal(barrier, inc=1, device_id=peer, device_id_type=MESH)

    @pl.when(jnp.logical_not(from_self))
    def _():
        pl.semaphore_signal(barrier, inc=1, device_id=(col, t_col, half), device_id_type=MESH)

    fetch.wait()
    rows[half, xh, z] = stage[...]
    pl.semaphore_wait(barrier, jnp.where(from_self, 16, 17))

    def remote(src, dst, send, recv, peer):
        return pltpu.make_async_remote_copy(
            src_ref=src, dst_ref=dst, send_sem=send, recv_sem=recv, device_id=peer, device_id_type=MESH)

    def arrived(ref, sem):
        pltpu.make_async_copy(ref, ref, sem).wait()

    pending = []

    def start(copy):
        copy.start()
        pending.append(copy)

    t_copies = []

    def transpose_out():
        for s in range(2):
            src = stage.at[pl.ds(s * 32, 32)]
            far = remote(src, traw.at[half], t_s.at[s], t_r.at[half], t_dest[s])
            near = pltpu.make_async_copy(src, traw.at[half], t_r.at[half])

            @pl.when(t_self[s])
            def _():
                near.start()

            @pl.when(jnp.logical_not(t_self[s]))
            def _():
                far.start()

            t_copies.append((t_self[s], far))

    signs = (1, -1)
    distances = (0, -1, 1, -2, 2, -3, 3, 4)

    def row_ref(u, d):
        return rows.at[half, xh if u == 0 else 1 - xh, mod8(z + d)]

    def row_pair(d, core):
        return rows.at[core, :, mod8(z + d)]

    def col_ref(u, d):
        return cols.at[part(mod8(y + d)), xl if u == 0 else 1 - xl]

    def col_pair(d):
        return cols.at[part(mod8(y + d))]

    def hop(which, direction, step, u):
        behind, ahead = ((0, 1), (0, 2), (2, 1), (2, 2))[step - 1]
        at = (0 if direction == 1 else 1, step - 1, u)
        d = -direction * behind
        if which == "row":
            ref = row_pair(d, half) if step == 3 else row_ref(u, d)
            return remote(ref, ref, rr_s.at[at], rr_r.at[at], z_peer[direction * ahead])
        peer = y_peer[direction * ahead]
        if step == 3:
            ref = col_pair(d)
        elif u == 1 and step < 3:
            ref, peer = col_ref(0, 0), diagonal[direction * ahead]
        else:
            ref = col_ref(u, d)
        return remote(ref, ref, c_s.at[at], c_r.at[at], peer)

    def to_sibling(d):
        slot = distances.index(d)
        start(remote(row_pair(d, half), row_pair(d, half), sib_s.at[slot], sib_r.at[slot], sibling))

    def begin_row(u):
        if u == 1:
            arrived(row_ref(1, 0), rx_r)
        for step in (2, 1):
            for direction in signs:
                start(hop("row", direction, step, u))
        if u == 1:
            to_sibling(0)

    def come(which, direction, step):
        recv = rr_r if which == "row" else c_r
        i = 0 if direction == 1 else 1
        d = -direction * step
        if step == 3:
            arrived(row_pair(d, half) if which == "row" else col_pair(d), recv.at[i, 2, 0])
        elif step == 4:
            u = i
            arrived(row_ref(u, 4) if which == "row" else col_ref(u, 4), recv.at[i, 3, u])
        else:
            for u in range(2):
                arrived(row_ref(u, d) if which == "row" else col_ref(u, d), recv.at[i, step - 1, u])

    def forward(which, step):
        for direction in signs:
            come(which, direction, step)
            if step == 2:
                start(hop(which, direction, 4, 0 if direction == 1 else 1))
                start(hop(which, direction, 3, 0))
            if which == "row" and step < 4:
                to_sibling(-direction * step)
        if which == "row" and step == 4:
            to_sibling(4)

    def to_lhs(*ds):
        for d in ds:
            arrived(row_pair(d, other), sib_r.at[distances.index(d)])
            for x in range(2):
                first, second = rows[0, x, mod8(z + d)], rows[1, x, mod8(z + d)]
                total = jnp.sum(first, axis=1, keepdims=True) + jnp.sum(second, axis=1, keepdims=True)
                mean = total / FRAMES
                here = pl.ds(pl.multiple_of(x * 512 + mod8(z + d) * 64, 64), 64)
                for j, value in enumerate((first, second)):
                    hi, lo = split(value - mean)
                    lhs[here, j * HALF:(j + 1) * HALF] = hi
                    lhs[here, FRAMES + j * HALF:FRAMES + (j + 1) * HALF] = lo
                    lhs[here, 2 * FRAMES + j * HALF:2 * FRAMES + (j + 1) * HALF] = hi

    def begin_col():
        for g in range(2):
            arrived(traw.at[g], t_r.at[g])
        first, second = traw[0], traw[1]
        total = jnp.sum(first, axis=1, keepdims=True) + jnp.sum(second, axis=1, keepdims=True)
        mean = total / FRAMES
        mine = col_ref(0, 0)
        mine[:, :HALF] = first - mean
        mine[:, HALF:] = second - mean
        for step in (2, 1):
            for u in range(2):
                for direction in (1, -1):
                    start(hop("col", direction, step, u))
        start(remote(mine, mine, cx_s, cx_r, cx_peer))

    base = part(y)
    sign = 1 - 2 * lax.rem(base, 2)

    def tile_of(step):
        return mod8(base + sign * (1, -2, 3, 4)[step - 1]) // 2

    def to_rhs(steps):
        for i, step in enumerate(steps):
            value = cols[pl.ds(2 * tile_of(step), 2)].reshape(TILE, FRAMES) * (1.0 / (FRAMES - 1))
            hi, lo = split(value)
            here = pl.ds(i * TILE, TILE)
            rhs[here, :FRAMES] = hi
            rhs[here, FRAMES:2 * FRAMES] = hi
            rhs[here, 2 * FRAMES:] = lo

    def multiply(steps):
        product = lax.dot_general(
            lhs[...], rhs[...], (((1,), (1,)), ((), ())), preferred_element_type=jnp.float32)
        for i, step in enumerate(steps):
            there = pl.ds(pl.multiple_of(tile_of(step) * TILE, TILE), TILE)
            out_ref[:, there] = product[:, i * TILE:(i + 1) * TILE]

    transpose_out()
    start(remote(row_ref(0, 0), row_ref(0, 0), rx_s, rx_r, rx_peer))
    begin_row(0)
    begin_row(1)
    begin_col()
    forward("row", 2)
    to_lhs(0)
    forward("col", 2)
    forward("row", 1)
    to_lhs(-2, 2)
    forward("row", 3)
    forward("row", 4)
    to_lhs(-1, 1)
    forward("col", 1)
    arrived(col_ref(1, 0), cx_r)
    to_rhs((1, 2))
    to_lhs(-3, 3, 4)
    multiply((1, 2))
    forward("col", 3)
    forward("col", 4)
    to_rhs((3, 4))
    multiply((3, 4))

    for copy in pending:
        copy.wait_send()
    for local, copy in t_copies:
        @pl.when(jnp.logical_not(local))
        def _():
            copy.wait_send()


def body(frames):
    dma = pltpu.SemaphoreType.DMA
    return pl.pallas_call(
        kernel,
        out_shape=jax.ShapeDtypeStruct((1024, 512), jnp.float32),
        in_specs=[pl.BlockSpec(memory_space=pltpu.HBM)],
        out_specs=pl.BlockSpec(memory_space=pltpu.VMEM),
        scratch_shapes=[
            pltpu.VMEM((64, HALF), jnp.float32),
            pltpu.VMEM((2, 32, HALF), jnp.float32),
            pltpu.VMEM((2, 2, 8, 64, HALF), jnp.float32),
            pltpu.VMEM((8, 2, 32, FRAMES), jnp.float32),
            pltpu.VMEM((1024, 3 * FRAMES), jnp.bfloat16),
            pltpu.VMEM((2 * TILE, 3 * FRAMES), jnp.bfloat16),
            dma, dma((2,)), dma((2,)), dma, dma, dma, dma, dma((2, 4, 2)), dma((2, 4, 2)), dma((2, 4, 2)), dma((2, 4, 2)),
            dma((8,)), dma((8,)),
        ],
        compiler_params=pltpu.CompilerParams(
            collective_id=0, has_side_effects=True, vmem_limit_bytes=40 * 1024 * 1024),
        cost_estimate=pl.CostEstimate(flops=3 * 2 * 1024 * 512 * 512, bytes_accessed=2 << 20, transcendentals=0),
    )(pltpu.with_memory_space_constraint(frames.T, pltpu.HBM))


def solution(mesh):
    in_specs = (P("half", ("row", "col")),)
    out_specs = P("row", ("col", "half"))
    return jax.shard_map(body, mesh=mesh, in_specs=in_specs, out_specs=out_specs, check_vma=False)
```

```python
import jax
import jax.numpy as jnp
from jax import lax
from jax.experimental import pallas as pl
from jax.experimental.pallas import tpu as pltpu
from jax.sharding import PartitionSpec as P

MESH = pl.DeviceIdType.MESH
FRAMES = 512
HALF = FRAMES // 2
RING = 8
TILE = 128


def mod8(value):
    return lax.rem(value + 16, RING)


def split(value):
    hi = value.astype(jnp.bfloat16)
    lo = (value - hi.astype(jnp.float32)).astype(jnp.bfloat16)
    return hi, lo


def kernel(x_ref, out_ref, stage, traw, rows, cols, lhs, rhs,
           in_s, t_s, t_r, rx_s, rx_r, cx_s, cx_r, rr_s, rr_r, c_s, c_r, sib_s, sib_r):
    row = lax.axis_index("row")
    col = lax.axis_index("col")
    half = lax.axis_index("half")
    y, xl = row // 2, lax.rem(row, 2)
    xh, z = col // RING, lax.rem(col, RING)
    other = 1 - half

    fetch = pltpu.make_async_copy(x_ref, stage, in_s)
    fetch.start()

    sibling = (row, col, other)
    rx_peer = (row, (1 - xh) * RING + z, half)
    z_peer = {n: (row, xh * RING + mod8(z + n), half) for n in (1, -1, 2, -2)}
    cx_peer = (y * 2 + 1 - xl, col, half)
    y_peer = {n: (mod8(y + n) * 2 + xl, col, half) for n in (1, -1, 2, -2)}
    diagonal = {n: (mod8(y + n) * 2 + 1 - xl, col, half) for n in (1, -1, 2, -2)}

    yy = mod8(z + lax.rem(row, RING) + 4 * xh)
    t_dest = [(yy * 2 + s, row, xh) for s in range(2)]
    t_self = [(yy * 2 + s == row) & (row == col) & (xh == half) for s in range(2)]

    def part(place):
        return mod8(place - z + 4 * half)

    t_col = RING * half + part(y)
    from_self = (row == col) & (col == t_col)

    barrier = pltpu.get_barrier_semaphore()
    for peer in (sibling, rx_peer, cx_peer, *z_peer.values(), *y_peer.values(), *diagonal.values(), (col, t_col, other)):
        pl.semaphore_signal(barrier, inc=1, device_id=peer, device_id_type=MESH)

    @pl.when(jnp.logical_not(from_self))
    def _():
        pl.semaphore_signal(barrier, inc=1, device_id=(col, t_col, half), device_id_type=MESH)

    fetch.wait()
    rows[half, xh, z] = stage[...]
    pl.semaphore_wait(barrier, jnp.where(from_self, 16, 17))

    def remote(src, dst, send, recv, peer):
        return pltpu.make_async_remote_copy(
            src_ref=src, dst_ref=dst, send_sem=send, recv_sem=recv, device_id=peer, device_id_type=MESH)

    def arrived(ref, sem):
        pltpu.make_async_copy(ref, ref, sem).wait()

    pending = []

    def start(copy):
        copy.start()
        pending.append(copy)

    t_copies = []

    def transpose_out():
        for s in range(2):
            src = stage.at[pl.ds(s * 32, 32)]
            far = remote(src, traw.at[half], t_s.at[s], t_r.at[half], t_dest[s])
            near = pltpu.make_async_copy(src, traw.at[half], t_r.at[half])

            @pl.when(t_self[s])
            def _():
                near.start()

            @pl.when(jnp.logical_not(t_self[s]))
            def _():
                far.start()

            t_copies.append((t_self[s], far))

    signs = (1, -1)
    distances = (0, -1, 1, -2, 2, -3, 3, 4)

    def row_ref(u, d):
        return rows.at[half, xh if u == 0 else 1 - xh, mod8(z + d)]

    def row_pair(d, core):
        return rows.at[core, :, mod8(z + d)]

    def col_ref(u, d):
        return cols.at[part(mod8(y + d)), xl if u == 0 else 1 - xl]

    def col_pair(d):
        return cols.at[part(mod8(y + d))]

    def hop(which, direction, step, u):
        behind, ahead = ((0, 1), (0, 2), (2, 1), (2, 2))[step - 1]
        at = (0 if direction == 1 else 1, step - 1, u)
        d = -direction * behind
        if which == "row":
            ref = row_pair(d, half) if step == 3 else row_ref(u, d)
            return remote(ref, ref, rr_s.at[at], rr_r.at[at], z_peer[direction * ahead])
        peer = y_peer[direction * ahead]
        if step == 3:
            ref = col_pair(d)
        elif u == 1 and step < 3:
            ref, peer = col_ref(0, 0), diagonal[direction * ahead]
        else:
            ref = col_ref(u, d)
        return remote(ref, ref, c_s.at[at], c_r.at[at], peer)

    def to_sibling(d):
        slot = distances.index(d)
        start(remote(row_pair(d, half), row_pair(d, half), sib_s.at[slot], sib_r.at[slot], sibling))

    def begin_row(u):
        if u == 1:
            arrived(row_ref(1, 0), rx_r)
        for step in (2, 1):
            for direction in signs:
                start(hop("row", direction, step, u))
        if u == 1:
            to_sibling(0)

    def come(which, direction, step):
        recv = rr_r if which == "row" else c_r
        i = 0 if direction == 1 else 1
        d = -direction * step
        if step == 3:
            arrived(row_pair(d, half) if which == "row" else col_pair(d), recv.at[i, 2, 0])
        elif step == 4:
            u = i
            arrived(row_ref(u, 4) if which == "row" else col_ref(u, 4), recv.at[i, 3, u])
        else:
            for u in range(2):
                arrived(row_ref(u, d) if which == "row" else col_ref(u, d), recv.at[i, step - 1, u])

    def forward(which, step):
        for direction in signs:
            come(which, direction, step)
            if step == 2:
                start(hop(which, direction, 4, 0 if direction == 1 else 1))
                start(hop(which, direction, 3, 0))
            if which == "row" and step < 4:
                to_sibling(-direction * step)
        if which == "row" and step == 4:
            to_sibling(4)

    def to_lhs(*ds):
        for d in ds:
            arrived(row_pair(d, other), sib_r.at[distances.index(d)])
            for x in range(2):
                first, second = rows[0, x, mod8(z + d)], rows[1, x, mod8(z + d)]
                total = jnp.sum(first, axis=1, keepdims=True) + jnp.sum(second, axis=1, keepdims=True)
                mean = total / FRAMES
                here = pl.ds(pl.multiple_of(x * 512 + mod8(z + d) * 64, 64), 64)
                for j, value in enumerate((first, second)):
                    hi, lo = split(value - mean)
                    lhs[here, j * HALF:(j + 1) * HALF] = hi
                    lhs[here, FRAMES + j * HALF:FRAMES + (j + 1) * HALF] = lo
                    lhs[here, 2 * FRAMES + j * HALF:2 * FRAMES + (j + 1) * HALF] = hi

    def begin_col():
        for g in range(2):
            arrived(traw.at[g], t_r.at[g])
        first, second = traw[0], traw[1]
        total = jnp.sum(first, axis=1, keepdims=True) + jnp.sum(second, axis=1, keepdims=True)
        mean = total / FRAMES
        mine = col_ref(0, 0)
        mine[:, :HALF] = first - mean
        mine[:, HALF:] = second - mean
        for step in (2, 1):
            for u in range(2):
                for direction in (1, -1):
                    start(hop("col", direction, step, u))
        start(remote(mine, mine, cx_s, cx_r, cx_peer))

    base = part(y)
    sign = 1 - 2 * lax.rem(base, 2)

    def tile_of(step):
        return mod8(base + sign * (1, -2, 3, 4)[step - 1]) // 2

    def to_rhs(steps):
        for i, step in enumerate(steps):
            value = cols[pl.ds(2 * tile_of(step), 2)].reshape(TILE, FRAMES) * (1.0 / (FRAMES - 1))
            hi, lo = split(value)
            here = pl.ds(i * TILE, TILE)
            rhs[here, :FRAMES] = hi
            rhs[here, FRAMES:2 * FRAMES] = hi
            rhs[here, 2 * FRAMES:] = lo

    def multiply(steps, m):
        here = pl.ds(m * 256, 256)
        product = lax.dot_general(
            lhs[here, :], rhs[...], (((1,), (1,)), ((), ())), preferred_element_type=jnp.float32)
        for i, step in enumerate(steps):
            there = pl.ds(pl.multiple_of(tile_of(step) * TILE, TILE), TILE)
            out_ref[here, there] = product[:, i * TILE:(i + 1) * TILE]

    transpose_out()
    start(remote(row_ref(0, 0), row_ref(0, 0), rx_s, rx_r, rx_peer))
    begin_row(0)
    begin_row(1)
    begin_col()
    forward("row", 2)
    to_lhs(0)
    forward("col", 2)
    forward("row", 1)
    to_lhs(-2, 2)
    forward("row", 3)
    forward("row", 4)
    to_lhs(-1, 1)
    forward("col", 1)
    arrived(col_ref(1, 0), cx_r)
    to_rhs((1, 2))
    to_lhs(-3, 3, 4)
    for m in range(4):
        multiply((1, 2), m)
    forward("col", 3)
    forward("col", 4)
    to_rhs((3, 4))
    for m in range(4):
        multiply((3, 4), m)

    for copy in pending:
        copy.wait_send()
    for local, copy in t_copies:
        @pl.when(jnp.logical_not(local))
        def _():
            copy.wait_send()


def body(frames):
    dma = pltpu.SemaphoreType.DMA
    return pl.pallas_call(
        kernel,
        out_shape=jax.ShapeDtypeStruct((1024, 512), jnp.float32),
        in_specs=[pl.BlockSpec(memory_space=pltpu.HBM)],
        out_specs=pl.BlockSpec(memory_space=pltpu.VMEM),
        scratch_shapes=[
            pltpu.VMEM((64, HALF), jnp.float32),
            pltpu.VMEM((2, 32, HALF), jnp.float32),
            pltpu.VMEM((2, 2, 8, 64, HALF), jnp.float32),
            pltpu.VMEM((8, 2, 32, FRAMES), jnp.float32),
            pltpu.VMEM((1024, 3 * FRAMES), jnp.bfloat16),
            pltpu.VMEM((2 * TILE, 3 * FRAMES), jnp.bfloat16),
            dma, dma((2,)), dma((2,)), dma, dma, dma, dma, dma((2, 4, 2)), dma((2, 4, 2)), dma((2, 4, 2)), dma((2, 4, 2)),
            dma((8,)), dma((8,)),
        ],
        compiler_params=pltpu.CompilerParams(
            collective_id=0, has_side_effects=True, vmem_limit_bytes=40 * 1024 * 1024),
        cost_estimate=pl.CostEstimate(flops=3 * 2 * 1024 * 512 * 512, bytes_accessed=2 << 20, transcendentals=0),
    )(pltpu.with_memory_space_constraint(frames.T, pltpu.HBM))


def solution(mesh):
    in_specs = (P("half", ("row", "col")),)
    out_specs = P("row", ("col", "half"))
    return jax.shard_map(body, mesh=mesh, in_specs=in_specs, out_specs=out_specs, check_vma=False)
```

```python
import jax
import jax.numpy as jnp
from jax import lax
from jax.experimental import pallas as pl
from jax.experimental.pallas import tpu as pltpu
from jax.sharding import PartitionSpec as P

MESH = pl.DeviceIdType.MESH
FRAMES = 512
HALF = FRAMES // 2
RING = 8
TILE = 128


def mod8(value):
    return lax.rem(value + 16, RING)


def split(value):
    hi = value.astype(jnp.bfloat16)
    lo = (value - hi.astype(jnp.float32)).astype(jnp.bfloat16)
    return hi, lo


def kernel(x_ref, out_ref, stage, traw, rows, cols, lhs, rhs,
           in_s, t_s, t_r, rx_s, rx_r, cx_s, cx_r, rr_s, rr_r, c_s, c_r, sib_s, sib_r):
    row = lax.axis_index("row")
    col = lax.axis_index("col")
    half = lax.axis_index("half")
    y, xl = row // 2, lax.rem(row, 2)
    xh, z = col // RING, lax.rem(col, RING)
    other = 1 - half

    fetch = pltpu.make_async_copy(x_ref, stage, in_s)
    fetch.start()

    sibling = (row, col, other)
    rx_peer = (row, (1 - xh) * RING + z, half)
    z_peer = {n: (row, xh * RING + mod8(z + n), half) for n in (1, -1, 2, -2)}
    cx_peer = (y * 2 + 1 - xl, col, half)
    y_peer = {n: (mod8(y + n) * 2 + xl, col, half) for n in (1, -1, 2, -2)}
    diagonal = {n: (mod8(y + n) * 2 + 1 - xl, col, half) for n in (1, -1, 2, -2)}

    yy = mod8(z + lax.rem(row, RING) + 4 * xh)
    t_dest = [(yy * 2 + s, row, xh) for s in range(2)]
    t_self = [(yy * 2 + s == row) & (row == col) & (xh == half) for s in range(2)]

    def part(place):
        return mod8(place - z + 4 * half)

    t_col = RING * half + part(y)
    from_self = (row == col) & (col == t_col)

    barrier = pltpu.get_barrier_semaphore()
    for peer in (sibling, rx_peer, cx_peer, *z_peer.values(), *y_peer.values(), *diagonal.values(), (col, t_col, other)):
        pl.semaphore_signal(barrier, inc=1, device_id=peer, device_id_type=MESH)

    @pl.when(jnp.logical_not(from_self))
    def _():
        pl.semaphore_signal(barrier, inc=1, device_id=(col, t_col, half), device_id_type=MESH)

    fetch.wait()
    rows[half, xh, z] = stage[...]
    pl.semaphore_wait(barrier, jnp.where(from_self, 16, 17))

    def remote(src, dst, send, recv, peer):
        return pltpu.make_async_remote_copy(
            src_ref=src, dst_ref=dst, send_sem=send, recv_sem=recv, device_id=peer, device_id_type=MESH)

    def arrived(ref, sem):
        pltpu.make_async_copy(ref, ref, sem).wait()

    pending = []

    def start(copy):
        copy.start()
        pending.append(copy)

    t_copies = []

    def transpose_out():
        for s in range(2):
            src = stage.at[pl.ds(s * 32, 32)]
            far = remote(src, traw.at[half], t_s.at[s], t_r.at[half], t_dest[s])
            near = pltpu.make_async_copy(src, traw.at[half], t_r.at[half])

            @pl.when(t_self[s])
            def _():
                near.start()

            @pl.when(jnp.logical_not(t_self[s]))
            def _():
                far.start()

            t_copies.append((t_self[s], far))

    signs = (1, -1)
    distances = (0, -1, 1, -2, 2, -3, 3, 4)

    def row_ref(u, d):
        return rows.at[half, xh if u == 0 else 1 - xh, mod8(z + d)]

    def row_pair(d, core):
        return rows.at[core, :, mod8(z + d)]

    def col_ref(u, d):
        return cols.at[part(mod8(y + d)), xl if u == 0 else 1 - xl]

    def col_pair(d):
        return cols.at[part(mod8(y + d))]

    def hop(which, direction, step, u):
        behind, ahead = ((0, 1), (0, 2), (2, 1), (2, 2))[step - 1]
        at = (0 if direction == 1 else 1, step - 1, u)
        d = -direction * behind
        if which == "row":
            ref = row_pair(d, half) if step == 3 else row_ref(u, d)
            return remote(ref, ref, rr_s.at[at], rr_r.at[at], z_peer[direction * ahead])
        peer = y_peer[direction * ahead]
        if step == 3:
            ref = col_pair(d)
        elif u == 1 and step < 3:
            ref, peer = col_ref(0, 0), diagonal[direction * ahead]
        else:
            ref = col_ref(u, d)
        return remote(ref, ref, c_s.at[at], c_r.at[at], peer)

    def to_sibling(d):
        slot = distances.index(d)
        start(remote(row_pair(d, half), row_pair(d, half), sib_s.at[slot], sib_r.at[slot], sibling))

    def begin_row(u):
        if u == 1:
            arrived(row_ref(1, 0), rx_r)
        for step in (2, 1):
            for direction in signs:
                start(hop("row", direction, step, u))
        if u == 1:
            to_sibling(0)

    def come(which, direction, step):
        recv = rr_r if which == "row" else c_r
        i = 0 if direction == 1 else 1
        d = -direction * step
        if step == 3:
            arrived(row_pair(d, half) if which == "row" else col_pair(d), recv.at[i, 2, 0])
        elif step == 4:
            u = i
            arrived(row_ref(u, 4) if which == "row" else col_ref(u, 4), recv.at[i, 3, u])
        else:
            for u in range(2):
                arrived(row_ref(u, d) if which == "row" else col_ref(u, d), recv.at[i, step - 1, u])

    def forward(which, step):
        for direction in signs:
            come(which, direction, step)
            if step == 2:
                start(hop(which, direction, 4, 0 if direction == 1 else 1))
                start(hop(which, direction, 3, 0))
            if which == "row" and step < 4:
                to_sibling(-direction * step)
        if which == "row" and step == 4:
            to_sibling(4)

    def to_lhs(*ds):
        for d in ds:
            arrived(row_pair(d, other), sib_r.at[distances.index(d)])
            for x in range(2):
                first, second = rows[0, x, mod8(z + d)], rows[1, x, mod8(z + d)]
                total = jnp.sum(first, axis=1, keepdims=True) + jnp.sum(second, axis=1, keepdims=True)
                mean = total / FRAMES
                here = pl.ds(pl.multiple_of(x * 512 + mod8(z + d) * 64, 64), 64)
                for j, value in enumerate((first, second)):
                    hi, lo = split(value - mean)
                    lhs[here, j * HALF:(j + 1) * HALF] = hi
                    lhs[here, FRAMES + j * HALF:FRAMES + (j + 1) * HALF] = lo
                    lhs[here, 2 * FRAMES + j * HALF:2 * FRAMES + (j + 1) * HALF] = hi

    def begin_col():
        for g in range(2):
            arrived(traw.at[g], t_r.at[g])
        first, second = traw[0], traw[1]
        total = jnp.sum(first, axis=1, keepdims=True) + jnp.sum(second, axis=1, keepdims=True)
        mean = total / FRAMES
        mine = col_ref(0, 0)
        mine[:, :HALF] = first - mean
        mine[:, HALF:] = second - mean
        for step in (2, 1):
            for u in range(2):
                for direction in (1, -1):
                    start(hop("col", direction, step, u))
        start(remote(mine, mine, cx_s, cx_r, cx_peer))

    base = part(y)
    sign = 1 - 2 * lax.rem(base, 2)

    def tile_of(step):
        return mod8(base + sign * (1, -2, 3, 4)[step - 1]) // 2

    def to_rhs(steps):
        for i, step in enumerate(steps):
            value = cols[pl.ds(2 * tile_of(step), 2)].reshape(TILE, FRAMES) * (1.0 / (FRAMES - 1))
            hi, lo = split(value)
            here = pl.ds(i * TILE, TILE)
            rhs[here, :FRAMES] = hi
            rhs[here, FRAMES:2 * FRAMES] = hi
            rhs[here, 2 * FRAMES:] = lo

    def multiply(steps, m):
        here = pl.ds(m * 128, 128)
        product = lax.dot_general(
            lhs[here, :], rhs[...], (((1,), (1,)), ((), ())), preferred_element_type=jnp.float32)
        for i, step in enumerate(steps):
            there = pl.ds(pl.multiple_of(tile_of(step) * TILE, TILE), TILE)
            out_ref[here, there] = product[:, i * TILE:(i + 1) * TILE]

    transpose_out()
    start(remote(row_ref(0, 0), row_ref(0, 0), rx_s, rx_r, rx_peer))
    begin_row(0)
    begin_row(1)
    begin_col()
    forward("row", 2)
    to_lhs(0)
    forward("col", 2)
    forward("row", 1)
    to_lhs(-2, 2)
    forward("row", 3)
    forward("row", 4)
    to_lhs(-1, 1)
    forward("col", 1)
    arrived(col_ref(1, 0), cx_r)
    to_rhs((1, 2))
    to_lhs(-3, 3, 4)
    for m in range(8):
        multiply((1, 2), m)
    forward("col", 3)
    forward("col", 4)
    to_rhs((3, 4))
    for m in range(8):
        multiply((3, 4), m)

    for copy in pending:
        copy.wait_send()
    for local, copy in t_copies:
        @pl.when(jnp.logical_not(local))
        def _():
            copy.wait_send()


def body(frames):
    dma = pltpu.SemaphoreType.DMA
    return pl.pallas_call(
        kernel,
        out_shape=jax.ShapeDtypeStruct((1024, 512), jnp.float32),
        in_specs=[pl.BlockSpec(memory_space=pltpu.HBM)],
        out_specs=pl.BlockSpec(memory_space=pltpu.VMEM),
        scratch_shapes=[
            pltpu.VMEM((64, HALF), jnp.float32),
            pltpu.VMEM((2, 32, HALF), jnp.float32),
            pltpu.VMEM((2, 2, 8, 64, HALF), jnp.float32),
            pltpu.VMEM((8, 2, 32, FRAMES), jnp.float32),
            pltpu.VMEM((1024, 3 * FRAMES), jnp.bfloat16),
            pltpu.VMEM((2 * TILE, 3 * FRAMES), jnp.bfloat16),
            dma, dma((2,)), dma((2,)), dma, dma, dma, dma, dma((2, 4, 2)), dma((2, 4, 2)), dma((2, 4, 2)), dma((2, 4, 2)),
            dma((8,)), dma((8,)),
        ],
        compiler_params=pltpu.CompilerParams(
            collective_id=0, has_side_effects=True, vmem_limit_bytes=40 * 1024 * 1024),
        cost_estimate=pl.CostEstimate(flops=3 * 2 * 1024 * 512 * 512, bytes_accessed=2 << 20, transcendentals=0),
    )(pltpu.with_memory_space_constraint(frames.T, pltpu.HBM))


def solution(mesh):
    in_specs = (P("half", ("row", "col")),)
    out_specs = P("row", ("col", "half"))
    return jax.shard_map(body, mesh=mesh, in_specs=in_specs, out_specs=out_specs, check_vma=False)
```
